32 devices in a mesh: groups: 2 (over y), section: 4 (over z), sector: 4 (over x, core).
Axes of the slice: x: 2, y: 2, z: 4, core: 2. Of those that a mesh axis runs over, the one named last changes fastest.
Arguments:
- env_left: bfloat16 [8, 8, 30, 128, 128], P(('groups', 'section'), 'sector'), parts along dimension 0, may hold values from -0.5 to 0.5
- env_right: bfloat16 [8, 8, 30, 128, 128], P(('groups', 'section'), 'sector'), parts along dimension 0, may hold values from -0.5 to 0.5
- edge_left: bfloat16 [8, 8, 128, 128], P(('groups', 'section'), 'sector'), parts along dimension 0, may hold values from -0.5 to 0.5
- edge_right: bfloat16 [8, 8, 128, 128], P(('groups', 'section'), 'sector'), parts along dimension 0, may hold values from -0.5 to 0.5
- wave_blocks: bfloat16 [8, 8, 128, 128], P(('groups', 'section'), 'sector'), parts along dimension 0, may hold values from -12 to 12
- mpo_coef: float32 [8, 8, 30], P(('groups', 'section'), 'sector'), parts along dimension 0, may hold values from -4 to 4
- onsite: float32 [8, 8], P(('groups', 'section'), 'sector'), parts along dimension 0, may hold values from 1 to 4
- routes: int32 [8, 8, 30], P(('groups', 'section'), 'sector'), parts along dimension 0, may hold values from 0 to 7
- sector_sizes: int32 [16], P(('groups', 'sector')), parts along dimension 0, may hold values from 64 to 128
Outputs:
- first_image: bfloat16 [8, 8, 128, 128], P(('groups', 'section'), 'sector'), parts along dimension 0
- second_image: bfloat16 [8, 8, 128, 128], P(('groups', 'section'), 'sector'), parts along dimension 0
The draws below stay inside these ranges and needn't reach their ends.
There are 2 independent parts, one for each index of `groups`. The reference program is written for one: setup_inputs(seed, part) draws one part's arguments, and reference() takes and returns one part's arrays. A program takes and returns all parts, laid end to end along the dimension named above; each array names one. Nothing has to cross between parts.
All inputs are finite; a program needn't handle non-finite values.
Results may differ from the reference program's by a relative error of at most 0.0069.
Values may be sent and summed in bfloat16 or wider, within the bound.
No kernel may reach another device: no remote copies, remote signals or barrier semaphores. Data moves between devices by JAX's collectives and lax.ppermute only.
A program may use at most 64 MiB of HBM per device.

```python
import jax
import jax.numpy as jnp
from jax import lax

P_SIZE = 128
W = 30
NS = 8
NC = 4


def draw_wave_blocks(key, part):
    key = jax.random.fold_in(key, 11)
    key_base, key_rows, key_cols = jax.random.split(key, 3)
    shape = (NC, NS, P_SIZE, P_SIZE)
    rising = 0.5 + jnp.arange(NS, dtype=jnp.float32) / max(NS - 1, 1)
    row_scale = jnp.exp(jax.random.uniform(key_rows, (NC, NS, P_SIZE, 1), minval=0.0, maxval=1.1513))
    col_scale = jnp.exp(jax.random.uniform(key_cols, (NC, NS, 1, P_SIZE), minval=0.0, maxval=1.1513))
    base = jnp.clip(jax.random.normal(key_base, shape), -4.0, 4.0)
    values = base * rising[None, :, None, None] * row_scale * col_scale / 5.0
    return values.astype(jnp.bfloat16)


def place_ends(entries, own_key, smallest, high):
    extent = entries.shape
    spot = [jax.random.randint(jax.random.fold_in(own_key, axis), (), 0, extent[axis]) for axis in range(len(extent))]
    entries = entries.at[tuple(spot)].set(smallest)
    longest = extent.index(max(extent))
    spot[longest] = (spot[longest] + 1) % extent[longest]
    return entries.at[tuple(spot)].set(high)


def level_of(key, shape, pieces, low, largest):
    gain, own = 1.0, jax.random.fold_in(key, 6)
    for dim, blocks in pieces:
        heights = jnp.exp(jax.random.uniform(jax.random.fold_in(own, dim), (blocks,), jnp.float32, low / len(pieces), largest / len(pieces)))
        gain = gain * jnp.repeat(heights, shape[dim] // blocks).reshape([-1 if axis == dim else 1 for axis in range(len(shape))])
    return gain


def scatter_about(stream_key, shape, deviation, reach, pieces=(), held_as=jnp.bfloat16):
    array = jax.random.normal(stream_key, shape, jnp.float32) * deviation
    if len(pieces) > 0:
        array = level_of(stream_key, shape, pieces, -0.22, 0.18) * array
    return jnp.clip(array, min=-reach, max=reach).astype(held_as)


def setup_inputs(seed: int = 0, part: int = 0) -> dict:
    key_of = jax.random.split(jax.random.key(seed), 10)
    part_keys = jax.random.split(jax.random.fold_in(key_of[9], part), 10)
    return {
        "env_left": scatter_about(part_keys[0], (NC, NS, W, P_SIZE, P_SIZE), P_SIZE ** -0.5, 0.5, ((0, 4), (1, 4))),
        "env_right": scatter_about(part_keys[1], (NC, NS, W, P_SIZE, P_SIZE), P_SIZE ** -0.5, 0.5, ((0, 4), (1, 4))),
        "edge_left": scatter_about(part_keys[2], (NC, NS, P_SIZE, P_SIZE), P_SIZE ** -0.5, 0.5, ((0, 4), (1, 4))),
        "edge_right": scatter_about(part_keys[3], (NC, NS, P_SIZE, P_SIZE), P_SIZE ** -0.5, 0.5, ((0, 4), (1, 4))),
        "wave_blocks": draw_wave_blocks(jax.random.fold_in(jax.random.fold_in(key_of[9], part), 71), part),
        "mpo_coef": scatter_about(part_keys[5], (NC, NS, W), 1.0, 4.0, ((0, 4), (1, 4)), jnp.float32),
        "onsite": jnp.clip(1.0 + 3.0 * jax.random.uniform(part_keys[6], (NC, NS), jnp.float32) ** level_of(part_keys[6], (NC, NS), ((0, 4), (1, 4)), -0.2, 0.2), 1.0, 4.0),
        "routes": place_ends(jax.random.randint(part_keys[7], (NC, NS, W), 0, NS), jax.random.fold_in(part_keys[7], 1), 0, NS - 1).astype(jnp.int32),
        "sector_sizes": place_ends(jax.random.randint(part_keys[8], (NS,), P_SIZE // 2, P_SIZE + 1), jax.random.fold_in(part_keys[8], 1), P_SIZE // 2, P_SIZE).astype(jnp.int32),
    }


def live_of(sector_sizes):
    position = jnp.arange(P_SIZE, dtype=jnp.int32)
    alive = position[None, :] < sector_sizes[:, None]
    return alive[:, :, None] & alive[:, None, :]

def grow_left(packed):
    edge, env = packed
    inner_left = jnp.einsum('kba,kwbc->kwac', edge.astype(jnp.float32), env.astype(jnp.float32)).astype(jnp.bfloat16)
    return jnp.einsum('kwac,kcd->kwad', inner_left.astype(jnp.float32), edge.astype(jnp.float32)).astype(jnp.bfloat16)

def grow_right(packed):
    edge, env = packed
    inner_right = jnp.einsum('kab,kwbc->kwac', edge.astype(jnp.float32), env.astype(jnp.float32)).astype(jnp.bfloat16)
    return jnp.einsum('kwac,kdc->kwad', inner_right.astype(jnp.float32), edge.astype(jnp.float32)).astype(jnp.bfloat16)

def apply_hamiltonian(vectors, new_left, new_right, mpo_coef, onsite, routes, live_mask):

    def one_section(packed):
        vector, left_env, right_env, coef, energy, route = packed
        masked = jnp.where(live_mask, vector, jnp.zeros_like(vector))
        right_half = jnp.einsum('kab,kwcb->kwac', masked.astype(jnp.float32), right_env.astype(jnp.float32)).astype(jnp.bfloat16)
        contrib = jnp.einsum('kwab,kwbc->kwac', left_env.astype(jnp.float32), right_half.astype(jnp.float32))
        weighted = contrib * (coef * W ** (-0.5))[:, :, None, None]
        summed = jax.ops.segment_sum(weighted.reshape(NS * W, P_SIZE, P_SIZE), route.reshape(NS * W), num_segments=NS)
        total = summed + energy[:, None, None] * masked.astype(jnp.float32)
        return jnp.where(live_mask, total, jnp.zeros_like(total))
    return lax.map(one_section, (vectors, new_left, new_right, mpo_coef, onsite, routes))

def reference(env_left, env_right, edge_left, edge_right, wave_blocks, mpo_coef, onsite, routes, sector_sizes):
    live_mask = live_of(sector_sizes)
    passed_left = lax.map(grow_left, (edge_left, env_left))
    passed_right = lax.map(grow_right, (edge_right, env_right))
    new_left = jnp.concatenate([env_left[:1], passed_left[:-1]], axis=0)
    new_right = jnp.concatenate([passed_right[1:], env_right[-1:]], axis=0)
    image1 = apply_hamiltonian(wave_blocks, new_left, new_right, mpo_coef, onsite, routes, live_mask)
    masked_wave = jnp.where(live_mask[None], wave_blocks, jnp.zeros_like(wave_blocks)).astype(jnp.float32)
    correlation = lax.optimization_barrier(jnp.sum(masked_wave * image1, axis=(1, 2, 3)))
    squares = lax.optimization_barrier(jnp.sum(masked_wave * masked_wave, axis=(1, 2, 3)))
    ritz_value = correlation / (squares + 1e-06)
    resid = image1 - ritz_value[:, None, None, None] * masked_wave
    resid_sq = lax.optimization_barrier(jnp.sum(resid * resid, axis=(1, 2, 3)))
    correction = (resid * jnp.sqrt(squares / (resid_sq + 1e-06))[:, None, None, None]).astype(jnp.bfloat16)
    image2 = apply_hamiltonian(correction, new_left, new_right, mpo_coef, onsite, routes, live_mask)
    return (image1.astype(jnp.bfloat16), image2.astype(jnp.bfloat16))
```

```python
import functools

import jax
import jax.numpy as jnp
from jax import lax
from jax.experimental import pallas as pl
from jax.experimental.pallas import tpu as pltpu
from jax.sharding import PartitionSpec as P

epsilon = 1e-06
VMEM_BYTES = 24 * 1024 * 1024
EXTRA = 16

f32 = jnp.float32
bf16 = jnp.bfloat16

VM = pl.BlockSpec(memory_space=pltpu.VMEM)
SM = pl.BlockSpec(memory_space=pltpu.SMEM)
HB = pl.BlockSpec(memory_space=pl.ANY)


def call(kernel, outs, in_specs, scratch=(), aliases=None, flops=0, moved=0, out_specs=None):
    return pl.pallas_call(
        kernel,
        out_shape=outs,
        in_specs=in_specs,
        out_specs=[VM] * len(outs) if out_specs is None else out_specs,
        scratch_shapes=list(scratch),
        input_output_aliases=aliases or {},
        compiler_params=pltpu.CompilerParams(vmem_limit_bytes=VMEM_BYTES),
        cost_estimate=pl.CostEstimate(flops=flops, bytes_accessed=moved, transcendentals=0),
    )


def dot(a, b):
    return jnp.dot(a, b, preferred_element_type=f32)


def dot_t(a, b):
    return lax.dot_general(a, b, (((1,), (1,)), ((), ())), preferred_element_type=f32)


def chunk_sizes(channels):
    first = max(1, channels // 10)
    last = max(1, channels // 6)
    middle = channels - first - last
    return [c for c in (first, middle, last) if c > 0]


def grow_kernel(start, count, left_hbm, right_hbm, edge_l, edge_r, out_l, out_r, buf_l, buf_r, sems):
    copies = [
        pltpu.make_async_copy(src.at[0, :, pl.ds(start, count)], dst, sems.at[i])
        for i, (src, dst) in enumerate(((left_hbm, buf_l), (right_hbm, buf_r)))
    ]
    for c in copies:
        c.start()
    for c in copies:
        c.wait()
    for k in range(buf_l.shape[0]):
        e = edge_l[0, k]
        e_t = e.T
        f = edge_r[0, k]

        def step(w, carry):
            inner = dot(e_t, buf_l[k, w]).astype(bf16)
            out_l[k, w] = dot(inner, e).astype(bf16)
            inner = dot(f, buf_r[k, w]).astype(bf16)
            out_r[k, w] = dot_t(inner, f).astype(bf16)
            return carry

        lax.fori_loop(0, count, step, 0, unroll=3 if count % 3 == 0 else 1)


def grow(env_left, env_right, edge_left, edge_right, start, count):
    _, pd, _, b, _ = env_left.shape
    block = jax.ShapeDtypeStruct((pd, count, b, b), bf16)
    buf = pltpu.VMEM((pd, count, b, b), bf16)
    return call(
        functools.partial(grow_kernel, start, count),
        [block, block],
        [HB, HB, VM, VM],
        [buf, buf, pltpu.SemaphoreType.DMA((2,))],
        flops=8 * pd * count * b**3,
        moved=8 * pd * count * b * b,
    )(env_left, env_right, edge_left, edge_right)


def live_of(size, shape):
    rows = lax.broadcasted_iota(jnp.int32, shape, 0) < size
    cols = lax.broadcasted_iota(jnp.int32, shape, 1) < size
    return rows & cols


def mask_kernel(wave, sizes, out):
    for k in range(wave.shape[1]):
        v = wave[0, k].astype(f32)
        out[k] = jnp.where(live_of(sizes[k], v.shape), v, 0.0).astype(bf16)


def mask_wave(wave, sizes):
    _, pd, b, _ = wave.shape
    return call(mask_kernel, [jax.ShapeDtypeStruct((pd, b, b), bf16)], [VM, SM], moved=4 * pd * b * b)(wave, sizes)[0]


def apply_block(left, right, lead, start, count, m, k, acc, coef, routes, scale):
    for w in range(count):
        t = dot(left[k, lead + w], m).astype(bf16)
        contrib = dot_t(t, right[k, lead + w])
        j = routes[0, k, start + w]
        acc[j] += contrib * (coef[0, k, start + w] * scale)


def select_copy(flag, own, got, dst, sem, start, count, lead):
    @pl.when(flag)
    def _():
        pltpu.make_async_copy(own.at[0, :, pl.ds(start, count)], dst, sem).start()

    @pl.when(jnp.logical_not(flag))
    def _():
        pltpu.make_async_copy(got.at[:, pl.ds(lead, count)], dst, sem).start()


def wait_copy(got, dst, sem, lead, count):
    pltpu.make_async_copy(got.at[:, pl.ds(lead, count)], dst, sem).wait()


def three_terms(x, rows):
    hi = x.astype(bf16).astype(f32)
    mid = (x - hi).astype(bf16).astype(f32)
    low = x - hi - mid
    place = lax.broadcasted_iota(jnp.int32, (EXTRA, 128), 0)
    return jnp.where(place == 0, hi, jnp.where(place == 1, mid, jnp.where(place == 2, low, 0.0))).astype(bf16)


def from_terms(rows):
    return jnp.sum(rows.astype(f32), axis=0, keepdims=True)


def total_of(x):
    return jnp.sum(jnp.sum(x, axis=0, keepdims=True), axis=1, keepdims=True)


def split_halves(acc, groups, pd, b, bit, send, keep, extra):
    for i in range(groups // 2):
        for q in range(pd):
            kept = acc[(2 * i + bit) * pd + q]
            sent = acc[(2 * i + 1 - bit) * pd + q]
            keep[i * pd + q] = kept
            send[pl.ds((i * pd + q) * b, b)] = sent.astype(bf16)
    send[pl.ds(groups // 2 * pd * b, EXTRA)] = three_terms(extra, EXTRA)


def first_kernel(
    chunk, is_first, is_last, groups, scale,
    left_own, right_own, left_got, right_got, m, coef, routes, *rest
):
    start, count = chunk
    rest = list(rest)
    acc_in = None if is_first else rest.pop(0)
    if is_last:
        gathered, onsite = rest.pop(0), rest.pop(0)
        send, keep, squares_out, corr_out = [rest.pop(0) for _ in range(4)]
    else:
        acc_out = rest.pop(0)
    buf_l, buf_r, acc, sems = rest
    pd, b = m.shape[0], m.shape[1]
    section = lax.axis_index("section")
    at_start = section == 0
    at_end = section == lax.axis_size("section") - 1
    select_copy(at_start, left_own, left_got, buf_l, sems.at[0], start, count, 0)
    select_copy(at_end, right_own, right_got, buf_r, sems.at[1], start, count, 0)
    if is_first:
        acc[...] = jnp.zeros_like(acc)
    else:
        acc[...] = acc_in[...]
    wait_copy(left_got, buf_l, sems.at[0], 0, count)
    wait_copy(right_got, buf_r, sems.at[1], 0, count)
    unit = 3 if count % 3 == 0 else (5 if count % 5 == 0 else (2 if count % 2 == 0 else 1))
    for k in range(pd):
        mk = m[k]

        def step(s, carry):
            apply_block(buf_l, buf_r, s * unit, start + s * unit, unit, mk, k, acc, coef, routes, scale)
            return carry

        lax.fori_loop(0, count // unit, step, 0)
    if not is_last:
        acc_out[...] = acc[...]
        return
    me = lax.axis_index("sector")
    corr = jnp.zeros((b, b), f32)
    squares = jnp.zeros((b, b), f32)
    for j in range(groups * pd):
        g = gathered[j].astype(f32)
        corr += g * acc[j]
        squares += g * g
    for k in range(pd):
        g = m[k].astype(f32)
        corr += onsite[0, k] * (g * g)
    corr = total_of(corr)
    squares_out[...] = jnp.broadcast_to(total_of(squares), squares_out.shape)
    corr_out[...] = jnp.broadcast_to(corr, corr_out.shape)
    split_halves(acc, groups, pd, b, lax.rem(me, 2), send, keep, corr)


def first_apply(chunk, is_first, is_last, groups, channels, arrays, acc_in, extra):
    start, count = chunk
    left_own, right_own, left_got, right_got, m, coef, routes = arrays
    pd, b, _ = m.shape
    total = jax.ShapeDtypeStruct((groups * pd, b, b), f32)
    args = [left_own, right_own, left_got, right_got, m, coef, routes]
    specs = [HB, HB, HB, HB, VM, SM, SM]
    if not is_first:
        args.append(acc_in)
        specs.append(VM)
    if is_last:
        args += list(extra)
        specs += [VM, SM]
        outs = exchange_shapes(groups, pd, b) + [jax.ShapeDtypeStruct((8, 128), f32)] * 2
    else:
        outs = [total]
    buf = pltpu.VMEM((pd, count, b, b), bf16)
    return call(
        functools.partial(first_kernel, chunk, is_first, is_last, groups, channels ** (-0.5)),
        outs,
        specs,
        [buf, buf, pltpu.VMEM((groups * pd, b, b), f32), pltpu.SemaphoreType.DMA((2,))],
        flops=4 * pd * count * b**3,
        moved=4 * pd * count * b * b,
    )(*args)


def exchange_shapes(groups, pd, b):
    half = groups // 2 * pd
    return [
        jax.ShapeDtypeStruct((half * b + EXTRA, b), bf16),
        jax.ShapeDtypeStruct((half, b, b), f32),
    ]


def combine_kernel(groups, stage, pd, keep_in, got, extra_in, send, keep, extra_out, acc):
    b = keep_in.shape[1]
    me = lax.axis_index("sector")
    for i in range(groups * pd):
        acc[i] = keep_in[i] + got[pl.ds(i * b, b)].astype(f32)
    extra = extra_in[0:1, 0:1] + from_terms(got[pl.ds(groups * pd * b, EXTRA)])[:, 0:1]
    extra_out[...] = jnp.broadcast_to(extra, extra_out.shape)
    bit = lax.rem(lax.div(me, 2**stage), 2)
    split_halves(acc, groups, pd, b, bit, send, keep, extra)


def combine(groups, stage, pd, keep, got, extra):
    b = keep.shape[1]
    return call(
        functools.partial(combine_kernel, groups, stage, pd),
        exchange_shapes(groups, pd, b) + [jax.ShapeDtypeStruct((8, 128), f32)],
        [VM, VM, VM],
        [pltpu.VMEM((groups * pd, b, b), f32)],
        flops=groups * pd * b * b,
        moved=8 * groups * pd * b * b,
    )(keep, got, extra)


def exchange(sectors, pd, send, keep, extra):
    stage = 0
    groups = sectors
    while True:
        got = lax.ppermute(send, "sector", [(i, i ^ (1 << stage)) for i in range(sectors)])
        groups //= 2
        stage += 1
        if groups == 1:
            return keep, got, extra
        send, keep, extra = combine(groups, stage, pd, keep, got, extra)


def second_kernel(
    bounds, groups, scale,
    left_own, right_own, *rest
):
    n = len(bounds)
    left_got, right_got = rest[:n], rest[n : 2 * n]
    (m, coef, routes, onsite, sizes, keep_in, got, corr_in, squares_in,
     image_out, resid_out, send, keep, sq_out, buf_l, buf_r, acc, sems) = rest[2 * n :]
    pd, b = m.shape[0], m.shape[1]
    section = lax.axis_index("section")
    at_start = section == 0
    at_end = section == lax.axis_size("section") - 1
    for i, (start, count) in enumerate(bounds):
        dst = pl.ds(start, count)
        select_copy(at_start, left_own, left_got[i], buf_l.at[:, dst], sems.at[0, i], start, count, 0)
        select_copy(at_end, right_own, right_got[i], buf_r.at[:, dst], sems.at[1, i], start, count, 0)
    acc[...] = jnp.zeros_like(acc)
    squares = squares_in[0:1, 0:1]
    corr = corr_in[0:1, 0:1] + from_terms(got[pl.ds(pd * b, EXTRA)])[:, 0:1]
    ritz = corr / (squares + epsilon)
    sums = jnp.zeros((b, b), f32)
    for k in range(pd):
        g = m[k].astype(f32)
        summed = keep_in[k] + got[pl.ds(k * b, b)].astype(f32) + onsite[0, k] * g
        image = jnp.where(live_of(sizes[k], (b, b)), summed, 0.0)
        image_out[0, k] = image.astype(bf16)
        resid = image - ritz * g
        resid_out[k] = resid.astype(bf16)
        sums += resid * resid
    total = total_of(sums)
    sq_out[...] = jnp.broadcast_to(total, sq_out.shape)
    for i, (start, count) in enumerate(bounds):
        dst = pl.ds(start, count)
        wait_copy(left_got[i], buf_l.at[:, dst], sems.at[0, i], 0, count)
        wait_copy(right_got[i], buf_r.at[:, dst], sems.at[1, i], 0, count)
        unit = 3 if count % 3 == 0 else (5 if count % 5 == 0 else (2 if count % 2 == 0 else 1))
        for k in range(pd):
            mk = resid_out[k]

            def step(s, carry):
                at = start + s * unit
                apply_block(buf_l, buf_r, at, at, unit, mk, k, acc, coef, routes, scale)
                return carry

            lax.fori_loop(0, count // unit, step, 0)
    me = lax.axis_index("sector")
    split_halves(acc, groups, pd, b, lax.rem(me, 2), send, keep, total)


def second_apply(bounds, groups, channels, left_own, right_own, lefts, rights, m, coef, routes, onsite, sizes, keep, got, corr, squares):
    pd, b, _ = m.shape
    n = len(bounds)
    block = jax.ShapeDtypeStruct((1, pd, b, b), bf16)
    buf = pltpu.VMEM((pd, channels, b, b), bf16)
    return call(
        functools.partial(second_kernel, bounds, groups, channels ** (-0.5)),
        [block, jax.ShapeDtypeStruct((pd, b, b), bf16)]
        + exchange_shapes(groups, pd, b)
        + [jax.ShapeDtypeStruct((8, 128), f32)],
        [HB] * (2 + 2 * n) + [VM, SM, SM, SM, SM, VM, VM, VM, VM],
        [buf, buf, pltpu.VMEM((groups * pd, b, b), f32), pltpu.SemaphoreType.DMA((2, n))],
        flops=4 * pd * channels * b**3,
        moved=4 * pd * channels * b * b,
    )(left_own, right_own, *lefts, *rights, m, coef, routes, onsite, sizes, keep, got, corr, squares)


def final_kernel(resid, onsite, sizes, keep, got, sq_in, squares_in, out):
    pd, b = resid.shape[0], resid.shape[1]
    sq = sq_in[0:1, 0:1] + from_terms(got[pl.ds(pd * b, EXTRA)])[:, 0:1]
    alpha = jnp.sqrt(squares_in[0:1, 0:1] / (sq + epsilon))
    for k in range(pd):
        summed = keep[k] + got[pl.ds(k * b, b)].astype(f32) + onsite[0, k] * resid[k].astype(f32)
        out[0, k] = jnp.where(live_of(sizes[k], (b, b)), alpha * summed, 0.0).astype(bf16)


def final(resid, onsite, sizes, keep, got, sq, squares):
    pd, b, _ = resid.shape
    return call(
        final_kernel,
        [jax.ShapeDtypeStruct((1, pd, b, b), bf16)],
        [VM, SM, SM, VM, VM, VM, VM],
        moved=8 * pd * b * b,
    )(resid, onsite, sizes, keep, got, sq, squares)[0]


def gather_waves(sectors, m):
    me = lax.axis_index("sector")
    held = m[None]
    for stage in range(sectors.bit_length() - 1):
        step = 1 << stage
        other = lax.ppermute(held, "sector", [(i, i ^ step) for i in range(sectors)])
        mine_low = (me & step) == 0
        low = jnp.where(mine_low, held, other)
        high = jnp.where(mine_low, other, held)
        held = jnp.concatenate([low, high], axis=0)
    return held.reshape((-1,) + m.shape[1:])


def body(
    env_left, env_right, edge_left, edge_right, wave_blocks, mpo_coef, onsite, routes, sector_sizes
):
    channels = env_left.shape[2]
    sections = lax.axis_size("section")
    sectors = lax.axis_size("sector")
    pd = wave_blocks.shape[1]
    sizes = chunk_sizes(channels)
    bounds = []
    at = 0
    for c in sizes:
        bounds.append((at, c))
        at += c
    up = [(i, i + 1) for i in range(sections - 1)]
    down = [(i + 1, i) for i in range(sections - 1)]
    lefts, rights = [], []
    for start, count in bounds:
        gl, gr = grow(env_left, env_right, edge_left, edge_right, start, count)
        lefts.append(lax.ppermute(gl, "section", up))
        rights.append(lax.ppermute(gr, "section", down))
    m = mask_wave(wave_blocks, sector_sizes)
    gathered = gather_waves(sectors, m)
    acc = None
    for i, chunk in enumerate(bounds):
        is_last = i == len(bounds) - 1
        res = first_apply(
            chunk, i == 0, is_last, sectors, channels,
            (env_left, env_right, lefts[i], rights[i], m, mpo_coef, routes), acc, (gathered, onsite),
        )
        acc = res[0]
    send, keep, squares, corr = res
    keep, got, corr = exchange(sectors, pd, send, keep, corr)
    image1, resid, send, keep, sq = second_apply(
        bounds, sectors, channels, env_left, env_right, lefts, rights, m, mpo_coef, routes, onsite,
        sector_sizes, keep, got, corr, squares,
    )
    keep, got, sq = exchange(sectors, pd, send, keep, sq)
    image2 = final(resid, onsite, sector_sizes, keep, got, sq, squares)
    return (image1, image2)


def solution(mesh):
    in_specs = (
        P(("groups", "section"), "sector", None, None, None),
        P(("groups", "section"), "sector", None, None, None),
        P(("groups", "section"), "sector", None, None),
        P(("groups", "section"), "sector", None, None),
        P(("groups", "section"), "sector", None, None),
        P(("groups", "section"), "sector", None),
        P(("groups", "section"), "sector"),
        P(("groups", "section"), "sector", None),
        P(("groups", "sector")),
    )
    out_specs = (
        P(("groups", "section"), "sector", None, None),
        P(("groups", "section"), "sector", None, None),
    )
    return jax.shard_map(body, mesh=mesh, in_specs=in_specs, out_specs=out_specs, check_vma=False)
```

```python
import functools

import jax
import jax.numpy as jnp
from jax import lax
from jax.experimental import pallas as pl
from jax.experimental.pallas import tpu as pltpu
from jax.sharding import PartitionSpec as P

epsilon = 1e-06
VMEM_BYTES = 16 * 1024 * 1024
VMEM_LARGE = 56 * 1024 * 1024
EXTRA = 16

f32 = jnp.float32
bf16 = jnp.bfloat16

VM = pl.BlockSpec(memory_space=pltpu.VMEM)
SM = pl.BlockSpec(memory_space=pltpu.SMEM)
HB = pl.BlockSpec(memory_space=pltpu.HBM)


def call(kernel, outs, in_specs, scratch=(), aliases=None, flops=0, moved=0, out_specs=None, vmem=VMEM_BYTES):
    return pl.pallas_call(
        kernel,
        out_shape=outs,
        in_specs=in_specs,
        out_specs=[VM] * len(outs) if out_specs is None else out_specs,
        scratch_shapes=list(scratch),
        input_output_aliases=aliases or {},
        compiler_params=pltpu.CompilerParams(vmem_limit_bytes=vmem),
        cost_estimate=pl.CostEstimate(flops=flops, bytes_accessed=moved, transcendentals=0),
    )


def dot(a, b):
    return jnp.dot(a, b, preferred_element_type=f32)


def dot_t(a, b):
    return lax.dot_general(a, b, (((1,), (1,)), ((), ())), preferred_element_type=f32)


def chunk_sizes(channels):
    first, last = max(1, channels // 5), max(1, channels * 2 // 15)
    return [c for c in (first, channels - first - last, last) if c > 0]


def unit_of(count, most=11):
    return max(u for u in range(1, most + 1) if count % u == 0)


def grow_kernel(bounds, left_hbm, right_hbm, edge_l_hbm, edge_r_hbm, *rest):
    n = len(bounds)
    rest = rest[-6 * n - 6 :]
    token, rest = rest[0], rest[1:]
    outs, bufs, results = rest[: 2 * n], rest[2 * n : 4 * n], rest[4 * n : 6 * n]
    edge_l, edge_r, edge_sems, in_sems, out_sems = rest[6 * n :]
    pd, b = edge_l.shape[0], edge_l.shape[1]
    edges = [
        pltpu.make_async_copy(edge_l_hbm.at[0], edge_l, edge_sems.at[0]),
        pltpu.make_async_copy(edge_r_hbm.at[0], edge_r, edge_sems.at[1]),
    ]
    for c in edges:
        c.start()
    loads = {}
    for i, (start, count) in enumerate(bounds):
        for k in range(pd):
            for side, src in enumerate((left_hbm, right_hbm)):
                c = pltpu.make_async_copy(
                    src.at[0, k, pl.ds(start, count)], bufs[2 * i + side].at[k], in_sems.at[i, k, side]
                )
                c.start()
                loads[i, k, side] = c
    for c in edges:
        c.wait()
    sends = []
    for i, (start, count) in enumerate(bounds):
        unit = unit_of(count)
        buf_l, buf_r = bufs[2 * i], bufs[2 * i + 1]
        res_l, res_r = results[2 * i], results[2 * i + 1]
        for k in range(pd):
            e = edge_l[k]
            e_t = e.T
            f = edge_r[k]
            loads[i, k, 0].wait()
            loads[i, k, 1].wait()

            def step(s, carry):
                at = s * unit
                left = [dot(e_t, buf_l[k, at + u]).astype(bf16) for u in range(unit)]
                right = [dot(f, buf_r[k, at + u]).astype(bf16) for u in range(unit)]
                grown = dot(jnp.concatenate(left, axis=0), e).astype(bf16)
                res_l[k, pl.ds(at, unit)] = grown.reshape(unit, b, b)
                for u in range(unit):
                    res_r[k, at + u] = dot_t(f, right[u]).astype(bf16)
                return carry

            if count == unit:
                step(0, 0)
            else:
                lax.fori_loop(0, count // unit, step, 0)
            for side, res in enumerate((res_l, res_r)):
                c = pltpu.make_async_copy(res.at[k], outs[2 * i + side].at[k], out_sems.at[i, k, side])
                c.start()
                sends.append(c)
    token[...] = jnp.zeros_like(token)
    for c in sends:
        c.wait()


def grow(env_left, env_right, edge_left, edge_right, bounds, after, vmem):
    _, pd, _, b, _ = env_left.shape
    n = len(bounds)
    counts = [c for _, c in bounds for _ in range(2)]
    total = sum(c for _, c in bounds)
    blocks = [pltpu.VMEM((pd, c, b, b), bf16) for c in counts]
    edge = pltpu.VMEM((pd, b, b), bf16)
    res = call(
        functools.partial(grow_kernel, bounds),
        [jax.ShapeDtypeStruct((8, 128), f32)] + [jax.ShapeDtypeStruct((pd, c, b, b), bf16) for c in counts],
        [HB] * (4 + len(after)),
        blocks + blocks + [
            edge, edge, pltpu.SemaphoreType.DMA((2,)),
            pltpu.SemaphoreType.DMA((n, pd, 2)), pltpu.SemaphoreType.DMA((n, pd, 2)),
        ],
        flops=8 * pd * total * b**3,
        moved=8 * pd * total * b * b,
        out_specs=[VM] + [HB] * (2 * n),
        vmem=vmem,
    )(env_left, env_right, edge_left, edge_right, *after)
    return res[0], [(res[2 * i + 1], res[2 * i + 2]) for i in range(n)]


def gate_kernel(*refs):
    refs[-1][...] = jnp.zeros_like(refs[-1])


def gate(arrays, after):
    *held, token = call(
        gate_kernel,
        [jax.ShapeDtypeStruct(a.shape, a.dtype) for a in arrays] + [jax.ShapeDtypeStruct((8, 128), f32)],
        [HB] * (len(arrays) + len(after)),
        aliases={i: i for i in range(len(arrays))},
        out_specs=[HB] * len(arrays) + [VM],
        vmem=VMEM_LARGE,
    )(*arrays, *after)
    return held, token


def own_kernel(left_hbm, right_hbm, after, out_l, out_r, sem):
    section = lax.axis_index("section")
    at_start = section == 0
    at_end = section == lax.axis_size("section") - 1
    pd, channels = out_l.shape[0], out_l.shape[1]

    @pl.when(at_start)
    def _():
        c = pltpu.make_async_copy(left_hbm.at[0], out_l, sem)
        c.start()
        c.wait()

    @pl.when(jnp.logical_not(at_start))
    def _():
        out_l[...] = jnp.zeros_like(out_l)

    @pl.when(at_end)
    def _():
        c = pltpu.make_async_copy(right_hbm.at[0], out_r, sem)
        c.start()
        c.wait()
        for k in range(pd):

            def step(w, carry):
                out_r[k, w] = out_r[k, w].T
                return carry

            lax.fori_loop(0, channels, step, 0)

    @pl.when(jnp.logical_not(at_end))
    def _():
        out_r[...] = jnp.zeros_like(out_r)


def own_ends(env_left, env_right, after):
    _, pd, channels, b, _ = env_left.shape
    shape = jax.ShapeDtypeStruct((pd, channels, b, b), bf16)
    return call(
        own_kernel, [shape, shape], [HB, HB, HB], [pltpu.SemaphoreType.DMA],
        flops=pd * channels * b * b, moved=4 * pd * channels * b * b,
    )(env_left, env_right, after)


def live_of(size, shape):
    rows = lax.broadcasted_iota(jnp.int32, shape, 0) < size
    cols = lax.broadcasted_iota(jnp.int32, shape, 1) < size
    return rows & cols


def mask_kernel(wave, sizes, after, out):
    for k in range(wave.shape[1]):
        v = wave[0, k].astype(f32)
        out[k] = jnp.where(live_of(sizes[k], v.shape), v, 0.0).astype(bf16)


def mask_wave(wave, sizes, after):
    _, pd, b, _ = wave.shape
    return call(mask_kernel, [jax.ShapeDtypeStruct((pd, b, b), bf16)], [VM, SM, HB], moved=4 * pd * b * b)(wave, sizes, after)[0]


def apply_blocks(load, count, vectors, first, acc, coef, routes, scale, unit):
    pd, b = len(vectors), vectors[0].shape[0]

    def step(s, carry):
        at = s * unit
        loaded = [load(k, at, unit) for k in range(pd)]
        halves = [dot(loaded[k][0].reshape(unit * b, b), vectors[k]).astype(bf16) for k in range(pd)]
        for k in range(pd):
            for u in range(unit):
                contrib = dot(halves[k][u * b : (u + 1) * b], loaded[k][1][u])
                j = routes[0, k, first + at + u]
                acc[j] += contrib * (coef[0, k, first + at + u] * scale)
        return carry

    if count == unit:
        step(0, 0)
    else:
        lax.fori_loop(0, count // unit, step, 0)


def three_terms(x, rows):
    hi = x.astype(bf16).astype(f32)
    mid = (x - hi).astype(bf16).astype(f32)
    low = x - hi - mid
    place = lax.broadcasted_iota(jnp.int32, (EXTRA, 128), 0)
    return jnp.where(place == 0, hi, jnp.where(place == 1, mid, jnp.where(place == 2, low, 0.0))).astype(bf16)


def from_terms(rows):
    return jnp.sum(rows.astype(f32), axis=0, keepdims=True)


def total_of(x):
    return jnp.sum(jnp.sum(x, axis=0, keepdims=True), axis=1, keepdims=True)


def split_halves(acc, groups, pd, b, bit, send, keep, extra):
    for i in range(groups // 2):
        for q in range(pd):
            kept = acc[(2 * i + bit) * pd + q]
            sent = acc[(2 * i + 1 - bit) * pd + q]
            keep[i * pd + q] = kept
            send[pl.ds((i * pd + q) * b, b)] = sent.astype(bf16)
    send[pl.ds(groups // 2 * pd * b, EXTRA)] = three_terms(extra, EXTRA)


def first_kernel(
    chunk, is_first, is_last, groups, scale,
    own_l, own_r, got_l, got_r, m, coef, routes, *rest
):
    start, count = chunk
    rest = list(rest)
    acc_in = None if is_first else rest.pop(0)
    if is_last:
        onsite = rest.pop(0)
        pieces = []
        at = 1
        while at < groups:
            pieces.append(rest.pop(0))
            at += pieces[-1].shape[0]
        new_l, new_r, send, keep, squares_out, corr_out, acc = rest
    else:
        new_l, new_r, acc = rest
    pd, b = m.shape[0], m.shape[1]
    if is_first:
        acc[...] = jnp.zeros_like(acc)
    else:
        acc[...] = acc_in[...]

    def load(k, at, unit):
        here, there = pl.ds(at, unit), pl.ds(start + at, unit)
        left = got_l[k, here] + own_l[k, there]
        right = got_r[k, here] + own_r[k, there]
        new_l[k, here] = left
        new_r[k, here] = right
        return left, right

    apply_blocks(load, count, [m[k] for k in range(pd)], start, acc, coef, routes, scale, unit_of(count))
    if not is_last:
        return
    me = lax.axis_index("sector")
    corr = jnp.zeros((b, b), f32)
    squares = jnp.zeros((b, b), f32)
    for k in range(pd):
        g = m[k].astype(f32)
        corr += g * (acc[me * pd + k] + onsite[0, k] * g)
        squares += g * g
    distance = 1
    for piece in pieces:
        for i in range(piece.shape[0]):
            owner = lax.bitwise_xor(me, distance)
            for k in range(pd):
                g = piece[i, k].astype(f32)
                corr += g * acc[owner * pd + k]
                squares += g * g
            distance += 1
    corr = total_of(corr)
    squares_out[...] = jnp.broadcast_to(total_of(squares), squares_out.shape)
    corr_out[...] = jnp.broadcast_to(corr, corr_out.shape)
    split_halves(acc, groups, pd, b, lax.rem(me, 2), send, keep, corr)


def first_apply(chunk, is_first, is_last, groups, channels, arrays, acc_in, extra):
    start, count = chunk
    m = arrays[4]
    pd, b, _ = m.shape
    total = jax.ShapeDtypeStruct((groups * pd, b, b), f32)
    block = jax.ShapeDtypeStruct((pd, count, b, b), bf16)
    args = list(arrays)
    specs = [VM, VM, VM, VM, VM, SM, SM]
    if not is_first:
        args.append(acc_in)
        specs.append(VM)
    scratch = []
    if is_last:
        args += list(extra)
        specs += [SM] + [VM] * (len(extra) - 1)
        outs = [block, block] + exchange_shapes(groups, pd, b) + [jax.ShapeDtypeStruct((8, 128), f32)] * 2
        scratch = [pltpu.VMEM((groups * pd, b, b), f32)]
    else:
        outs = [block, block, total]
    return call(
        functools.partial(first_kernel, chunk, is_first, is_last, groups, channels ** (-0.5)),
        outs,
        specs,
        scratch,
        flops=4 * pd * count * b**3,
        moved=4 * pd * count * b * b,
    )(*args)


def exchange_shapes(groups, pd, b):
    half = groups // 2 * pd
    return [
        jax.ShapeDtypeStruct((half * b + EXTRA, b), bf16),
        jax.ShapeDtypeStruct((half, b, b), f32),
    ]


def combine_kernel(groups, stage, pd, keep_in, got, extra_in, send, keep, extra_out, acc):
    b = keep_in.shape[1]
    me = lax.axis_index("sector")
    for i in range(groups * pd):
        acc[i] = keep_in[i] + got[pl.ds(i * b, b)].astype(f32)
    extra = extra_in[0:1, 0:1] + from_terms(got[pl.ds(groups * pd * b, EXTRA)])[:, 0:1]
    extra_out[...] = jnp.broadcast_to(extra, extra_out.shape)
    bit = lax.rem(lax.div(me, 2**stage), 2)
    split_halves(acc, groups, pd, b, bit, send, keep, extra)


def combine(groups, stage, pd, keep, got, extra):
    b = keep.shape[1]
    return call(
        functools.partial(combine_kernel, groups, stage, pd),
        exchange_shapes(groups, pd, b) + [jax.ShapeDtypeStruct((8, 128), f32)],
        [VM, VM, VM],
        [pltpu.VMEM((groups * pd, b, b), f32)],
        flops=groups * pd * b * b,
        moved=8 * groups * pd * b * b,
    )(keep, got, extra)


def exchange(sectors, pd, send, keep, extra):
    stage = 0
    groups = sectors
    while True:
        got = lax.ppermute(send, "sector", [(i, i ^ (1 << stage)) for i in range(sectors)])
        groups //= 2
        stage += 1
        if groups == 1:
            return keep, got, extra
        send, keep, extra = combine(groups, stage, pd, keep, got, extra)


def second_kernel(bounds, groups, scale, *rest):
    n = len(bounds)
    lefts, rights = rest[:n], rest[n : 2 * n]
    (m, coef, routes, onsite, sizes, keep_in, got, corr_in, squares_in,
     image_out, resid_out, send, keep, sq_out, acc) = rest[2 * n :]
    pd, b = m.shape[0], m.shape[1]
    acc[...] = jnp.zeros_like(acc)
    squares = squares_in[0:1, 0:1]
    corr = corr_in[0:1, 0:1] + from_terms(got[pl.ds(pd * b, EXTRA)])[:, 0:1]
    ritz = corr / (squares + epsilon)
    sums = jnp.zeros((b, b), f32)
    for k in range(pd):
        g = m[k].astype(f32)
        summed = keep_in[k] + got[pl.ds(k * b, b)].astype(f32) + onsite[0, k] * g
        image = jnp.where(live_of(sizes[k], (b, b)), summed, 0.0)
        image_out[0, k] = image.astype(bf16)
        resid = image - ritz * g
        resid_out[k] = resid.astype(bf16)
        sums += resid * resid
    total = total_of(sums)
    sq_out[...] = jnp.broadcast_to(total, sq_out.shape)
    vectors = [resid_out[k] for k in range(pd)]
    for i, (start, count) in enumerate(bounds):

        def load(k, at, unit):
            return lefts[i][k, pl.ds(at, unit)], rights[i][k, pl.ds(at, unit)]

        apply_blocks(load, count, vectors, start, acc, coef, routes, scale, unit_of(count))
    me = lax.axis_index("sector")
    split_halves(acc, groups, pd, b, lax.rem(me, 2), send, keep, total)


def second_apply(bounds, groups, channels, lefts, rights, m, coef, routes, onsite, sizes, keep, got, corr, squares):
    pd, b, _ = m.shape
    n = len(bounds)
    block = jax.ShapeDtypeStruct((1, pd, b, b), bf16)
    return call(
        functools.partial(second_kernel, bounds, groups, channels ** (-0.5)),
        [block, jax.ShapeDtypeStruct((pd, b, b), bf16)]
        + exchange_shapes(groups, pd, b)
        + [jax.ShapeDtypeStruct((8, 128), f32)],
        [VM] * (2 * n) + [VM, SM, SM, SM, SM, VM, VM, VM, VM],
        [pltpu.VMEM((groups * pd, b, b), f32)],
        flops=4 * pd * channels * b**3,
        moved=4 * pd * channels * b * b,
    )(*lefts, *rights, m, coef, routes, onsite, sizes, keep, got, corr, squares)


def final_kernel(resid, onsite, sizes, keep, got, sq_in, squares_in, out):
    pd, b = resid.shape[0], resid.shape[1]
    sq = sq_in[0:1, 0:1] + from_terms(got[pl.ds(pd * b, EXTRA)])[:, 0:1]
    alpha = jnp.sqrt(squares_in[0:1, 0:1] / (sq + epsilon))
    for k in range(pd):
        summed = keep[k] + got[pl.ds(k * b, b)].astype(f32) + onsite[0, k] * resid[k].astype(f32)
        out[0, k] = jnp.where(live_of(sizes[k], (b, b)), alpha * summed, 0.0).astype(bf16)


def final(resid, onsite, sizes, keep, got, sq, squares):
    pd, b, _ = resid.shape
    return call(
        final_kernel,
        [jax.ShapeDtypeStruct((1, pd, b, b), bf16)],
        [VM, SM, SM, VM, VM, VM, VM],
        moved=8 * pd * b * b,
    )(resid, onsite, sizes, keep, got, sq, squares)[0]


def gather_waves(sectors, m):
    held, pieces = m[None], []
    step = 1
    while step < sectors:
        other = lax.ppermute(held, "sector", [(i, i ^ step) for i in range(sectors)])
        pieces.append(other)
        step *= 2
        if step < sectors:
            held = jnp.concatenate([held, other], axis=0)
    return pieces


def body(
    env_left, env_right, edge_left, edge_right, wave_blocks, mpo_coef, onsite, routes, sector_sizes
):
    channels = env_left.shape[2]
    sections = lax.axis_size("section")
    sectors = lax.axis_size("sector")
    pd = wave_blocks.shape[1]
    bounds, at = [], 0
    for c in chunk_sizes(channels):
        bounds.append((at, c))
        at += c
    up = [(i, i + 1) for i in range(sections - 1)]
    down = [(i + 1, i) for i in range(sections - 1)]
    def pass_on(grown):
        return lax.ppermute(grown[0], "section", up), lax.ppermute(grown[1], "section", down)

    token, (head,) = grow(env_left, env_right, edge_left, edge_right, bounds[:1], (), VMEM_LARGE)
    got = [pass_on(head)]
    _, (middle, last) = grow(env_left, env_right, edge_left, edge_right, bounds[1:], (token,), VMEM_LARGE)
    grown, token = gate((*middle, *last), got[0])
    got.append(pass_on(grown[:2]))
    m = mask_wave(wave_blocks, sector_sizes, token)
    got.append(pass_on(gate(grown[2:], (m,))[0]))
    pieces = gather_waves(sectors, m)
    own_l, own_r = own_ends(env_left, env_right, m)
    acc, lefts, rights = None, [], []
    for i, chunk in enumerate(bounds):
        is_last = i == len(bounds) - 1
        res = first_apply(
            chunk, i == 0, is_last, sectors, channels,
            (own_l, own_r, got[i][0], got[i][1], m, mpo_coef, routes), acc, (onsite, *pieces),
        )
        lefts.append(res[0])
        rights.append(res[1])
        acc = res[2]
    send, keep, squares, corr = res[2:]
    keep, summed, corr = exchange(sectors, pd, send, keep, corr)
    image1, resid, send, keep, sq = second_apply(
        bounds, sectors, channels, lefts, rights, m, mpo_coef, routes, onsite,
        sector_sizes, keep, summed, corr, squares,
    )
    keep, summed, sq = exchange(sectors, pd, send, keep, sq)
    image2 = final(resid, onsite, sector_sizes, keep, summed, sq, squares)
    return (image1, image2)


def solution(mesh):
    in_specs = (
        P(("groups", "section"), "sector", None, None, None),
        P(("groups", "section"), "sector", None, None, None),
        P(("groups", "section"), "sector", None, None),
        P(("groups", "section"), "sector", None, None),
        P(("groups", "section"), "sector", None, None),
        P(("groups", "section"), "sector", None),
        P(("groups", "section"), "sector"),
        P(("groups", "section"), "sector", None),
        P(("groups", "sector")),
    )
    out_specs = (
        P(("groups", "section"), "sector", None, None),
        P(("groups", "section"), "sector", None, None),
    )
    return jax.shard_map(body, mesh=mesh, in_specs=in_specs, out_specs=out_specs, check_vma=False)
```

```python
import functools

import jax
import jax.numpy as jnp
from jax import lax
from jax.experimental import pallas as pl
from jax.experimental.pallas import tpu as pltpu
from jax.sharding import PartitionSpec as P

epsilon = 1e-06
VMEM_BYTES = 16 * 1024 * 1024
VMEM_LARGE = 56 * 1024 * 1024
EXTRA = 16

f32 = jnp.float32
bf16 = jnp.bfloat16

VM = pl.BlockSpec(memory_space=pltpu.VMEM)
SM = pl.BlockSpec(memory_space=pltpu.SMEM)
HB = pl.BlockSpec(memory_space=pltpu.HBM)


def call(kernel, outs, in_specs, scratch=(), aliases=None, flops=0, moved=0, out_specs=None, vmem=VMEM_BYTES):
    return pl.pallas_call(
        kernel,
        out_shape=outs,
        in_specs=in_specs,
        out_specs=[VM] * len(outs) if out_specs is None else out_specs,
        scratch_shapes=list(scratch),
        input_output_aliases=aliases or {},
        compiler_params=pltpu.CompilerParams(vmem_limit_bytes=vmem),
        cost_estimate=pl.CostEstimate(flops=flops, bytes_accessed=moved, transcendentals=0),
    )


def dot(a, b):
    return jnp.dot(a, b, preferred_element_type=f32)


def dot_t(a, b):
    return lax.dot_general(a, b, (((1,), (1,)), ((), ())), preferred_element_type=f32)


def chunk_sizes(channels):
    first, last = max(1, channels // 5), max(1, channels * 2 // 15)
    return [c for c in (first, channels - first - last, last) if c > 0]


def unit_of(count, most=11):
    return max(u for u in range(1, most + 1) if count % u == 0)


def grow_kernel(bounds, left_hbm, right_hbm, edge_l_hbm, edge_r_hbm, *rest):
    n = len(bounds)
    rest = rest[-6 * n - 6 :]
    token, rest = rest[0], rest[1:]
    outs, bufs, results = rest[: 2 * n], rest[2 * n : 4 * n], rest[4 * n : 6 * n]
    edge_l, edge_r, edge_sems, in_sems, out_sems = rest[6 * n :]
    pd, b = edge_l.shape[0], edge_l.shape[1]
    edges = [
        pltpu.make_async_copy(edge_l_hbm.at[0], edge_l, edge_sems.at[0]),
        pltpu.make_async_copy(edge_r_hbm.at[0], edge_r, edge_sems.at[1]),
    ]
    for c in edges:
        c.start()
    loads = {}
    for i, (start, count) in enumerate(bounds):
        for k in range(pd):
            for side, src in enumerate((left_hbm, right_hbm)):
                c = pltpu.make_async_copy(
                    src.at[0, k, pl.ds(start, count)], bufs[2 * i + side].at[k], in_sems.at[i, k, side]
                )
                c.start()
                loads[i, k, side] = c
    for c in edges:
        c.wait()
    sends = []
    for i, (start, count) in enumerate(bounds):
        unit = unit_of(count)
        buf_l, buf_r = bufs[2 * i], bufs[2 * i + 1]
        res_l, res_r = results[2 * i], results[2 * i + 1]
        for k in range(pd):
            e = edge_l[k]
            e_t = e.T
            f = edge_r[k]
            loads[i, k, 0].wait()
            loads[i, k, 1].wait()

            def step(s, carry):
                at = s * unit
                left = [dot(e_t, buf_l[k, at + u]).astype(bf16) for u in range(unit)]
                right = [dot(f, buf_r[k, at + u]).astype(bf16) for u in range(unit)]
                grown = dot(jnp.concatenate(left, axis=0), e).astype(bf16)
                res_l[k, pl.ds(at, unit)] = grown.reshape(unit, b, b)
                for u in range(unit):
                    res_r[k, at + u] = dot_t(f, right[u]).astype(bf16)
                return carry

            if count == unit:
                step(0, 0)
            else:
                lax.fori_loop(0, count // unit, step, 0)
            for side, res in enumerate((res_l, res_r)):
                c = pltpu.make_async_copy(res.at[k], outs[2 * i + side].at[k], out_sems.at[i, k, side])
                c.start()
                sends.append(c)
    token[...] = jnp.zeros_like(token)
    for c in sends:
        c.wait()


def grow(env_left, env_right, edge_left, edge_right, bounds, after, vmem):
    _, pd, _, b, _ = env_left.shape
    n = len(bounds)
    counts = [c for _, c in bounds for _ in range(2)]
    total = sum(c for _, c in bounds)
    blocks = [pltpu.VMEM((pd, c, b, b), bf16) for c in counts]
    edge = pltpu.VMEM((pd, b, b), bf16)
    res = call(
        functools.partial(grow_kernel, bounds),
        [jax.ShapeDtypeStruct((8, 128), f32)] + [jax.ShapeDtypeStruct((pd, c, b, b), bf16) for c in counts],
        [HB] * (4 + len(after)),
        blocks + blocks + [
            edge, edge, pltpu.SemaphoreType.DMA((2,)),
            pltpu.SemaphoreType.DMA((n, pd, 2)), pltpu.SemaphoreType.DMA((n, pd, 2)),
        ],
        flops=8 * pd * total * b**3,
        moved=8 * pd * total * b * b,
        out_specs=[VM] + [HB] * (2 * n),
        vmem=vmem,
    )(env_left, env_right, edge_left, edge_right, *after)
    return res[0], [(res[2 * i + 1], res[2 * i + 2]) for i in range(n)]


def gate_kernel(*refs):
    refs[-1][...] = jnp.zeros_like(refs[-1])


def gate(arrays, after):
    *held, token = call(
        gate_kernel,
        [jax.ShapeDtypeStruct(a.shape, a.dtype) for a in arrays] + [jax.ShapeDtypeStruct((8, 128), f32)],
        [HB] * (len(arrays) + len(after)),
        aliases={i: i for i in range(len(arrays))},
        out_specs=[HB] * len(arrays) + [VM],
    )(*arrays, *after)
    return held, token


def own_kernel(left_hbm, right_hbm, after, out_l, out_r, sem):
    section = lax.axis_index("section")
    at_start = section == 0
    at_end = section == lax.axis_size("section") - 1
    pd, channels = out_l.shape[0], out_l.shape[1]

    @pl.when(at_start)
    def _():
        c = pltpu.make_async_copy(left_hbm.at[0], out_l, sem)
        c.start()
        c.wait()

    @pl.when(jnp.logical_not(at_start))
    def _():
        out_l[...] = jnp.zeros_like(out_l)

    @pl.when(at_end)
    def _():
        c = pltpu.make_async_copy(right_hbm.at[0], out_r, sem)
        c.start()
        c.wait()
        for k in range(pd):

            def step(w, carry):
                out_r[k, w] = out_r[k, w].T
                return carry

            lax.fori_loop(0, channels, step, 0)

    @pl.when(jnp.logical_not(at_end))
    def _():
        out_r[...] = jnp.zeros_like(out_r)


def own_ends(env_left, env_right, after):
    _, pd, channels, b, _ = env_left.shape
    shape = jax.ShapeDtypeStruct((pd, channels, b, b), bf16)
    return call(
        own_kernel, [shape, shape], [HB, HB, HB], [pltpu.SemaphoreType.DMA],
        flops=10**10, moved=10**6,
    )(env_left, env_right, after)


def live_of(size, shape):
    rows = lax.broadcasted_iota(jnp.int32, shape, 0) < size
    cols = lax.broadcasted_iota(jnp.int32, shape, 1) < size
    return rows & cols


def mask_kernel(wave, sizes, after, out):
    for k in range(wave.shape[1]):
        v = wave[0, k].astype(f32)
        out[k] = jnp.where(live_of(sizes[k], v.shape), v, 0.0).astype(bf16)


def mask_wave(wave, sizes, after):
    _, pd, b, _ = wave.shape
    return call(mask_kernel, [jax.ShapeDtypeStruct((pd, b, b), bf16)], [VM, SM, HB], moved=4 * pd * b * b)(wave, sizes, after)[0]


def apply_blocks(load, count, vectors, first, acc, coef, routes, scale, unit):
    pd, b = len(vectors), vectors[0].shape[0]

    def step(s, carry):
        at = s * unit
        loaded = [load(k, at, unit) for k in range(pd)]
        halves = [dot(loaded[k][0].reshape(unit * b, b), vectors[k]).astype(bf16) for k in range(pd)]
        for k in range(pd):
            for u in range(unit):
                contrib = dot(halves[k][u * b : (u + 1) * b], loaded[k][1][u])
                j = routes[0, k, first + at + u]
                acc[j] += contrib * (coef[0, k, first + at + u] * scale)
        return carry

    if count == unit:
        step(0, 0)
    else:
        lax.fori_loop(0, count // unit, step, 0)


def three_terms(x, rows):
    hi = x.astype(bf16).astype(f32)
    mid = (x - hi).astype(bf16).astype(f32)
    low = x - hi - mid
    place = lax.broadcasted_iota(jnp.int32, (EXTRA, 128), 0)
    return jnp.where(place == 0, hi, jnp.where(place == 1, mid, jnp.where(place == 2, low, 0.0))).astype(bf16)


def from_terms(rows):
    return jnp.sum(rows.astype(f32), axis=0, keepdims=True)


def total_of(x):
    return jnp.sum(jnp.sum(x, axis=0, keepdims=True), axis=1, keepdims=True)


def split_halves(acc, groups, pd, b, bit, send, keep, extra):
    for i in range(groups // 2):
        for q in range(pd):
            kept = acc[(2 * i + bit) * pd + q]
            sent = acc[(2 * i + 1 - bit) * pd + q]
            keep[i * pd + q] = kept
            send[pl.ds((i * pd + q) * b, b)] = sent.astype(bf16)
    send[pl.ds(groups // 2 * pd * b, EXTRA)] = three_terms(extra, EXTRA)


def first_kernel(
    chunk, is_first, is_last, groups, scale,
    own_l, own_r, got_l, got_r, m, coef, routes, *rest
):
    start, count = chunk
    rest = list(rest)
    acc_in = None if is_first else rest.pop(0)
    if is_last:
        onsite = rest.pop(0)
        pieces = []
        at = 1
        while at < groups:
            pieces.append(rest.pop(0))
            at += pieces[-1].shape[0]
        new_l, new_r, send, keep, squares_out, corr_out, acc = rest
    else:
        new_l, new_r, acc = rest
    pd, b = m.shape[0], m.shape[1]
    if is_first:
        acc[...] = jnp.zeros_like(acc)
    else:
        acc[...] = acc_in[...]

    def load(k, at, unit):
        here, there = pl.ds(at, unit), pl.ds(start + at, unit)
        left = got_l[k, here] + own_l[k, there]
        right = got_r[k, here] + own_r[k, there]
        new_l[k, here] = left
        new_r[k, here] = right
        return left, right

    apply_blocks(load, count, [m[k] for k in range(pd)], start, acc, coef, routes, scale, unit_of(count))
    if not is_last:
        return
    me = lax.axis_index("sector")
    corr = jnp.zeros((b, b), f32)
    squares = jnp.zeros((b, b), f32)
    for k in range(pd):
        g = m[k].astype(f32)
        corr += g * (acc[me * pd + k] + onsite[0, k] * g)
        squares += g * g
    distance = 1
    for piece in pieces:
        for i in range(piece.shape[0]):
            owner = lax.bitwise_xor(me, distance)
            for k in range(pd):
                g = piece[i, k].astype(f32)
                corr += g * acc[owner * pd + k]
                squares += g * g
            distance += 1
    corr = total_of(corr)
    squares_out[...] = jnp.broadcast_to(total_of(squares), squares_out.shape)
    corr_out[...] = jnp.broadcast_to(corr, corr_out.shape)
    split_halves(acc, groups, pd, b, lax.rem(me, 2), send, keep, corr)


def first_apply(chunk, is_first, is_last, groups, channels, arrays, acc_in, extra):
    start, count = chunk
    m = arrays[4]
    pd, b, _ = m.shape
    total = jax.ShapeDtypeStruct((groups * pd, b, b), f32)
    block = jax.ShapeDtypeStruct((pd, count, b, b), bf16)
    args = list(arrays)
    specs = [VM, VM, VM, VM, VM, SM, SM]
    if not is_first:
        args.append(acc_in)
        specs.append(VM)
    scratch = []
    if is_last:
        args += list(extra)
        specs += [SM] + [VM] * (len(extra) - 1)
        outs = [block, block] + exchange_shapes(groups, pd, b) + [jax.ShapeDtypeStruct((8, 128), f32)] * 2
        scratch = [pltpu.VMEM((groups * pd, b, b), f32)]
    else:
        outs = [block, block, total]
    return call(
        functools.partial(first_kernel, chunk, is_first, is_last, groups, channels ** (-0.5)),
        outs,
        specs,
        scratch,
        flops=4 * pd * count * b**3,
        moved=4 * pd * count * b * b,
    )(*args)


def exchange_shapes(groups, pd, b):
    half = groups // 2 * pd
    return [
        jax.ShapeDtypeStruct((half * b + EXTRA, b), bf16),
        jax.ShapeDtypeStruct((half, b, b), f32),
    ]


def combine_kernel(groups, stage, pd, keep_in, got, extra_in, send, keep, extra_out, acc):
    b = keep_in.shape[1]
    me = lax.axis_index("sector")
    for i in range(groups * pd):
        acc[i] = keep_in[i] + got[pl.ds(i * b, b)].astype(f32)
    extra = extra_in[0:1, 0:1] + from_terms(got[pl.ds(groups * pd * b, EXTRA)])[:, 0:1]
    extra_out[...] = jnp.broadcast_to(extra, extra_out.shape)
    bit = lax.rem(lax.div(me, 2**stage), 2)
    split_halves(acc, groups, pd, b, bit, send, keep, extra)


def combine(groups, stage, pd, keep, got, extra):
    b = keep.shape[1]
    return call(
        functools.partial(combine_kernel, groups, stage, pd),
        exchange_shapes(groups, pd, b) + [jax.ShapeDtypeStruct((8, 128), f32)],
        [VM, VM, VM],
        [pltpu.VMEM((groups * pd, b, b), f32)],
        flops=groups * pd * b * b,
        moved=8 * groups * pd * b * b,
    )(keep, got, extra)


def exchange(sectors, pd, send, keep, extra):
    stage = 0
    groups = sectors
    while True:
        got = lax.ppermute(send, "sector", [(i, i ^ (1 << stage)) for i in range(sectors)])
        groups //= 2
        stage += 1
        if groups == 1:
            return keep, got, extra
        send, keep, extra = combine(groups, stage, pd, keep, got, extra)


def second_kernel(bounds, groups, scale, *rest):
    n = len(bounds)
    lefts, rights = rest[:n], rest[n : 2 * n]
    (m, coef, routes, onsite, sizes, keep_in, got, corr_in, squares_in,
     image_out, resid_out, send, keep, sq_out, acc) = rest[2 * n :]
    pd, b = m.shape[0], m.shape[1]
    acc[...] = jnp.zeros_like(acc)
    squares = squares_in[0:1, 0:1]
    corr = corr_in[0:1, 0:1] + from_terms(got[pl.ds(pd * b, EXTRA)])[:, 0:1]
    ritz = corr / (squares + epsilon)
    sums = jnp.zeros((b, b), f32)
    for k in range(pd):
        g = m[k].astype(f32)
        summed = keep_in[k] + got[pl.ds(k * b, b)].astype(f32) + onsite[0, k] * g
        image = jnp.where(live_of(sizes[k], (b, b)), summed, 0.0)
        image_out[0, k] = image.astype(bf16)
        resid = image - ritz * g
        resid_out[k] = resid.astype(bf16)
        sums += resid * resid
    total = total_of(sums)
    sq_out[...] = jnp.broadcast_to(total, sq_out.shape)
    vectors = [resid_out[k] for k in range(pd)]
    for i, (start, count) in enumerate(bounds):

        def load(k, at, unit):
            return lefts[i][k, pl.ds(at, unit)], rights[i][k, pl.ds(at, unit)]

        apply_blocks(load, count, vectors, start, acc, coef, routes, scale, unit_of(count))
    me = lax.axis_index("sector")
    split_halves(acc, groups, pd, b, lax.rem(me, 2), send, keep, total)


def second_apply(bounds, groups, channels, lefts, rights, m, coef, routes, onsite, sizes, keep, got, corr, squares):
    pd, b, _ = m.shape
    n = len(bounds)
    block = jax.ShapeDtypeStruct((1, pd, b, b), bf16)
    return call(
        functools.partial(second_kernel, bounds, groups, channels ** (-0.5)),
        [block, jax.ShapeDtypeStruct((pd, b, b), bf16)]
        + exchange_shapes(groups, pd, b)
        + [jax.ShapeDtypeStruct((8, 128), f32)],
        [VM] * (2 * n) + [VM, SM, SM, SM, SM, VM, VM, VM, VM],
        [pltpu.VMEM((groups * pd, b, b), f32)],
        flops=4 * pd * channels * b**3,
        moved=4 * pd * channels * b * b,
    )(*lefts, *rights, m, coef, routes, onsite, sizes, keep, got, corr, squares)


def final_kernel(resid, onsite, sizes, keep, got, sq_in, squares_in, out):
    pd, b = resid.shape[0], resid.shape[1]
    sq = sq_in[0:1, 0:1] + from_terms(got[pl.ds(pd * b, EXTRA)])[:, 0:1]
    alpha = jnp.sqrt(squares_in[0:1, 0:1] / (sq + epsilon))
    for k in range(pd):
        summed = keep[k] + got[pl.ds(k * b, b)].astype(f32) + onsite[0, k] * resid[k].astype(f32)
        out[0, k] = jnp.where(live_of(sizes[k], (b, b)), alpha * summed, 0.0).astype(bf16)


def final(resid, onsite, sizes, keep, got, sq, squares):
    pd, b, _ = resid.shape
    return call(
        final_kernel,
        [jax.ShapeDtypeStruct((1, pd, b, b), bf16)],
        [VM, SM, SM, VM, VM, VM, VM],
        moved=8 * pd * b * b,
    )(resid, onsite, sizes, keep, got, sq, squares)[0]


def gather_waves(sectors, m):
    held, pieces = m[None], []
    step = 1
    while step < sectors:
        other = lax.ppermute(held, "sector", [(i, i ^ step) for i in range(sectors)])
        pieces.append(other)
        step *= 2
        if step < sectors:
            held = jnp.concatenate([held, other], axis=0)
    return pieces


def body(
    env_left, env_right, edge_left, edge_right, wave_blocks, mpo_coef, onsite, routes, sector_sizes
):
    channels = env_left.shape[2]
    sections = lax.axis_size("section")
    sectors = lax.axis_size("sector")
    pd = wave_blocks.shape[1]
    bounds, at = [], 0
    for c in chunk_sizes(channels):
        bounds.append((at, c))
        at += c
    up = [(i, i + 1) for i in range(sections - 1)]
    down = [(i + 1, i) for i in range(sections - 1)]
    def pass_on(grown):
        return lax.ppermute(grown[0], "section", up), lax.ppermute(grown[1], "section", down)

    token, (head,) = grow(env_left, env_right, edge_left, edge_right, bounds[:1], (), VMEM_LARGE)
    got = [pass_on(head)]
    _, (middle, last) = grow(env_left, env_right, edge_left, edge_right, bounds[1:], (token,), VMEM_LARGE)
    got.append(pass_on(middle))
    grown, token = gate(last, got[0])
    m = mask_wave(wave_blocks, sector_sizes, token)
    got.append(pass_on(grown))
    pieces = gather_waves(sectors, m)
    own_l, own_r = own_ends(env_left, env_right, m)
    acc, lefts, rights = None, [], []
    for i, chunk in enumerate(bounds):
        is_last = i == len(bounds) - 1
        res = first_apply(
            chunk, i == 0, is_last, sectors, channels,
            (own_l, own_r, got[i][0], got[i][1], m, mpo_coef, routes), acc, (onsite, *pieces),
        )
        lefts.append(res[0])
        rights.append(res[1])
        acc = res[2]
    send, keep, squares, corr = res[2:]
    keep, summed, corr = exchange(sectors, pd, send, keep, corr)
    image1, resid, send, keep, sq = second_apply(
        bounds, sectors, channels, lefts, rights, m, mpo_coef, routes, onsite,
        sector_sizes, keep, summed, corr, squares,
    )
    keep, summed, sq = exchange(sectors, pd, send, keep, sq)
    image2 = final(resid, onsite, sector_sizes, keep, summed, sq, squares)
    return (image1, image2)


def solution(mesh):
    in_specs = (
        P(("groups", "section"), "sector", None, None, None),
        P(("groups", "section"), "sector", None, None, None),
        P(("groups", "section"), "sector", None, None),
        P(("groups", "section"), "sector", None, None),
        P(("groups", "section"), "sector", None, None),
        P(("groups", "section"), "sector", None),
        P(("groups", "section"), "sector"),
        P(("groups", "section"), "sector", None),
        P(("groups", "sector")),
    )
    out_specs = (
        P(("groups", "section"), "sector", None, None),
        P(("groups", "section"), "sector", None, None),
    )
    return jax.shard_map(body, mesh=mesh, in_specs=in_specs, out_specs=out_specs, check_vma=False)
```

```python
import functools

import jax
import jax.numpy as jnp
from jax import lax
from jax.experimental import pallas as pl
from jax.experimental.pallas import tpu as pltpu
from jax.sharding import PartitionSpec as P

epsilon = 1e-06
VMEM_BYTES = 16 * 1024 * 1024
VMEM_LARGE = 56 * 1024 * 1024
EXTRA = 16

f32 = jnp.float32
bf16 = jnp.bfloat16

VM = pl.BlockSpec(memory_space=pltpu.VMEM)
SM = pl.BlockSpec(memory_space=pltpu.SMEM)
HB = pl.BlockSpec(memory_space=pltpu.HBM)


def call(kernel, outs, in_specs, scratch=(), aliases=None, flops=0, moved=0, out_specs=None, vmem=VMEM_BYTES):
    return pl.pallas_call(
        kernel,
        out_shape=outs,
        in_specs=in_specs,
        out_specs=[VM] * len(outs) if out_specs is None else out_specs,
        scratch_shapes=list(scratch),
        input_output_aliases=aliases or {},
        compiler_params=pltpu.CompilerParams(vmem_limit_bytes=vmem),
        cost_estimate=pl.CostEstimate(flops=flops, bytes_accessed=moved, transcendentals=0),
    )


def dot(a, b):
    return jnp.dot(a, b, preferred_element_type=f32)


def dot_t(a, b):
    return lax.dot_general(a, b, (((1,), (1,)), ((), ())), preferred_element_type=f32)


def chunk_sizes(channels):
    first, last = max(1, channels * 3 // 10), max(1, channels // 10)
    return [c for c in (first, channels - first - last, last) if c > 0]


def unit_of(count, most=11):
    return max(u for u in range(1, most + 1) if count % u == 0)


def grow_kernel(bounds, left_hbm, right_hbm, edge_l_hbm, edge_r_hbm, *rest):
    n = len(bounds)
    rest = rest[-6 * n - 6 :]
    token, rest = rest[0], rest[1:]
    outs, bufs, results = rest[: 2 * n], rest[2 * n : 4 * n], rest[4 * n : 6 * n]
    edge_l, edge_r, edge_sems, in_sems, out_sems = rest[6 * n :]
    pd, b = edge_l.shape[0], edge_l.shape[1]
    edges = [
        pltpu.make_async_copy(edge_l_hbm.at[0], edge_l, edge_sems.at[0]),
        pltpu.make_async_copy(edge_r_hbm.at[0], edge_r, edge_sems.at[1]),
    ]
    for c in edges:
        c.start()
    loads = {}
    for i, (start, count) in enumerate(bounds):
        for k in range(pd):
            for side, src in enumerate((left_hbm, right_hbm)):
                c = pltpu.make_async_copy(
                    src.at[0, k, pl.ds(start, count)], bufs[2 * i + side].at[k], in_sems.at[i, k, side]
                )
                c.start()
                loads[i, k, side] = c
    for c in edges:
        c.wait()
    sends = []
    for i, (start, count) in enumerate(bounds):
        unit = unit_of(count)
        buf_l, buf_r = bufs[2 * i], bufs[2 * i + 1]
        res_l, res_r = results[2 * i], results[2 * i + 1]
        for k in range(pd):
            e = edge_l[k]
            e_t = e.T
            f = edge_r[k]
            loads[i, k, 0].wait()
            loads[i, k, 1].wait()

            def step(s, carry):
                at = s * unit
                left = [dot(e_t, buf_l[k, at + u]).astype(bf16) for u in range(unit)]
                right = [dot(f, buf_r[k, at + u]).astype(bf16) for u in range(unit)]
                grown = dot(jnp.concatenate(left, axis=0), e).astype(bf16)
                res_l[k, pl.ds(at, unit)] = grown.reshape(unit, b, b)
                for u in range(unit):
                    res_r[k, at + u] = dot_t(f, right[u]).astype(bf16)
                return carry

            if count == unit:
                step(0, 0)
            else:
                lax.fori_loop(0, count // unit, step, 0)
            for side, res in enumerate((res_l, res_r)):
                c = pltpu.make_async_copy(res.at[k], outs[2 * i + side].at[k], out_sems.at[i, k, side])
                c.start()
                sends.append(c)
    token[...] = jnp.zeros_like(token)
    for c in sends:
        c.wait()


def grow(env_left, env_right, edge_left, edge_right, bounds, after, vmem):
    _, pd, _, b, _ = env_left.shape
    n = len(bounds)
    counts = [c for _, c in bounds for _ in range(2)]
    total = sum(c for _, c in bounds)
    blocks = [pltpu.VMEM((pd, c, b, b), bf16) for c in counts]
    edge = pltpu.VMEM((pd, b, b), bf16)
    res = call(
        functools.partial(grow_kernel, bounds),
        [jax.ShapeDtypeStruct((8, 128), f32)] + [jax.ShapeDtypeStruct((pd, c, b, b), bf16) for c in counts],
        [HB] * (4 + len(after)),
        blocks + blocks + [
            edge, edge, pltpu.SemaphoreType.DMA((2,)),
            pltpu.SemaphoreType.DMA((n, pd, 2)), pltpu.SemaphoreType.DMA((n, pd, 2)),
        ],
        flops=8 * pd * total * b**3,
        moved=8 * pd * total * b * b,
        out_specs=[VM] + [HB] * (2 * n),
        vmem=vmem,
    )(env_left, env_right, edge_left, edge_right, *after)
    return res[0], [(res[2 * i + 1], res[2 * i + 2]) for i in range(n)]


def gate_kernel(*refs):
    refs[-1][...] = jnp.zeros_like(refs[-1])


def gate(arrays, after):
    *held, token = call(
        gate_kernel,
        [jax.ShapeDtypeStruct(a.shape, a.dtype) for a in arrays] + [jax.ShapeDtypeStruct((8, 128), f32)],
        [HB] * (len(arrays) + len(after)),
        aliases={i: i for i in range(len(arrays))},
        out_specs=[HB] * len(arrays) + [VM],
    )(*arrays, *after)
    return held, token


def own_kernel(left_hbm, right_hbm, after, out_l, out_r, sem):
    section = lax.axis_index("section")
    at_start = section == 0
    at_end = section == lax.axis_size("section") - 1
    pd, channels = out_l.shape[0], out_l.shape[1]

    @pl.when(at_start)
    def _():
        c = pltpu.make_async_copy(left_hbm.at[0], out_l, sem)
        c.start()
        c.wait()

    @pl.when(jnp.logical_not(at_start))
    def _():
        out_l[...] = jnp.zeros_like(out_l)

    @pl.when(at_end)
    def _():
        c = pltpu.make_async_copy(right_hbm.at[0], out_r, sem)
        c.start()
        c.wait()
        for k in range(pd):

            def step(w, carry):
                out_r[k, w] = out_r[k, w].T
                return carry

            lax.fori_loop(0, channels, step, 0)

    @pl.when(jnp.logical_not(at_end))
    def _():
        out_r[...] = jnp.zeros_like(out_r)


def own_ends(env_left, env_right, after):
    _, pd, channels, b, _ = env_left.shape
    shape = jax.ShapeDtypeStruct((pd, channels, b, b), bf16)
    return call(
        own_kernel, [shape, shape], [HB, HB, HB], [pltpu.SemaphoreType.DMA],
        flops=10**10, moved=10**6,
    )(env_left, env_right, after)


def live_of(size, shape):
    rows = lax.broadcasted_iota(jnp.int32, shape, 0) < size
    cols = lax.broadcasted_iota(jnp.int32, shape, 1) < size
    return rows & cols


def mask_kernel(wave, sizes, after, out):
    for k in range(wave.shape[1]):
        v = wave[0, k].astype(f32)
        out[k] = jnp.where(live_of(sizes[k], v.shape), v, 0.0).astype(bf16)


def mask_wave(wave, sizes, after):
    _, pd, b, _ = wave.shape
    return call(mask_kernel, [jax.ShapeDtypeStruct((pd, b, b), bf16)], [VM, SM, HB], moved=4 * pd * b * b)(wave, sizes, after)[0]


def apply_blocks(load, count, vectors, first, acc, coef, routes, scale, unit):
    pd, b = len(vectors), vectors[0].shape[0]

    def step(s, carry):
        at = s * unit
        loaded = [load(k, at, unit) for k in range(pd)]
        halves = [dot(loaded[k][0].reshape(unit * b, b), vectors[k]).astype(bf16) for k in range(pd)]
        for k in range(pd):
            for u in range(unit):
                contrib = dot(halves[k][u * b : (u + 1) * b], loaded[k][1][u])
                j = routes[0, k, first + at + u]
                acc[j] += contrib * (coef[0, k, first + at + u] * scale)
        return carry

    if count == unit:
        step(0, 0)
    else:
        lax.fori_loop(0, count // unit, step, 0)


def three_terms(x, rows):
    hi = x.astype(bf16).astype(f32)
    mid = (x - hi).astype(bf16).astype(f32)
    low = x - hi - mid
    place = lax.broadcasted_iota(jnp.int32, (EXTRA, 128), 0)
    return jnp.where(place == 0, hi, jnp.where(place == 1, mid, jnp.where(place == 2, low, 0.0))).astype(bf16)


def from_terms(rows):
    return jnp.sum(rows.astype(f32), axis=0, keepdims=True)


def total_of(x):
    return jnp.sum(jnp.sum(x, axis=0, keepdims=True), axis=1, keepdims=True)


def split_halves(acc, groups, pd, b, bit, send, keep, extra):
    for i in range(groups // 2):
        for q in range(pd):
            kept = acc[(2 * i + bit) * pd + q]
            sent = acc[(2 * i + 1 - bit) * pd + q]
            keep[i * pd + q] = kept
            send[pl.ds((i * pd + q) * b, b)] = sent.astype(bf16)
    send[pl.ds(groups // 2 * pd * b, EXTRA)] = three_terms(extra, EXTRA)


def first_kernel(
    chunk, is_first, is_last, groups, scale,
    own_l, own_r, got_l, got_r, m, coef, routes, *rest
):
    start, count = chunk
    rest = list(rest)
    acc_in = None if is_first else rest.pop(0)
    if is_last:
        onsite = rest.pop(0)
        pieces = []
        at = 1
        while at < groups:
            pieces.append(rest.pop(0))
            at += pieces[-1].shape[0]
        new_l, new_r, send, keep, squares_out, corr_out, acc = rest
    else:
        new_l, new_r, acc = rest
    pd, b = m.shape[0], m.shape[1]
    if is_first:
        acc[...] = jnp.zeros_like(acc)
    else:
        acc[...] = acc_in[...]

    def load(k, at, unit):
        here, there = pl.ds(at, unit), pl.ds(start + at, unit)
        left = got_l[k, here] + own_l[k, there]
        right = got_r[k, here] + own_r[k, there]
        new_l[k, here] = left
        new_r[k, here] = right
        return left, right

    apply_blocks(load, count, [m[k] for k in range(pd)], start, acc, coef, routes, scale, unit_of(count))
    if not is_last:
        return
    me = lax.axis_index("sector")
    corr = jnp.zeros((b, b), f32)
    squares = jnp.zeros((b, b), f32)
    for k in range(pd):
        g = m[k].astype(f32)
        corr += g * (acc[me * pd + k] + onsite[0, k] * g)
        squares += g * g
    distance = 1
    for piece in pieces:
        for i in range(piece.shape[0]):
            owner = lax.bitwise_xor(me, distance)
            for k in range(pd):
                g = piece[i, k].astype(f32)
                corr += g * acc[owner * pd + k]
                squares += g * g
            distance += 1
    corr = total_of(corr)
    squares_out[...] = jnp.broadcast_to(total_of(squares), squares_out.shape)
    corr_out[...] = jnp.broadcast_to(corr, corr_out.shape)
    split_halves(acc, groups, pd, b, lax.rem(me, 2), send, keep, corr)


def first_apply(chunk, is_first, is_last, groups, channels, arrays, acc_in, extra):
    start, count = chunk
    m = arrays[4]
    pd, b, _ = m.shape
    total = jax.ShapeDtypeStruct((groups * pd, b, b), f32)
    block = jax.ShapeDtypeStruct((pd, count, b, b), bf16)
    args = list(arrays)
    specs = [VM, VM, VM, VM, VM, SM, SM]
    if not is_first:
        args.append(acc_in)
        specs.append(VM)
    scratch = []
    if is_last:
        args += list(extra)
        specs += [SM] + [VM] * (len(extra) - 1)
        outs = [block, block] + exchange_shapes(groups, pd, b) + [jax.ShapeDtypeStruct((8, 128), f32)] * 2
        scratch = [pltpu.VMEM((groups * pd, b, b), f32)]
    else:
        outs = [block, block, total]
    return call(
        functools.partial(first_kernel, chunk, is_first, is_last, groups, channels ** (-0.5)),
        outs,
        specs,
        scratch,
        flops=4 * pd * count * b**3,
        moved=4 * pd * count * b * b,
    )(*args)


def exchange_shapes(groups, pd, b):
    half = groups // 2 * pd
    return [
        jax.ShapeDtypeStruct((half * b + EXTRA, b), bf16),
        jax.ShapeDtypeStruct((half, b, b), f32),
    ]


def combine_kernel(groups, stage, pd, keep_in, got, extra_in, send, keep, extra_out, acc):
    b = keep_in.shape[1]
    me = lax.axis_index("sector")
    for i in range(groups * pd):
        acc[i] = keep_in[i] + got[pl.ds(i * b, b)].astype(f32)
    extra = extra_in[0:1, 0:1] + from_terms(got[pl.ds(groups * pd * b, EXTRA)])[:, 0:1]
    extra_out[...] = jnp.broadcast_to(extra, extra_out.shape)
    bit = lax.rem(lax.div(me, 2**stage), 2)
    split_halves(acc, groups, pd, b, bit, send, keep, extra)


def combine(groups, stage, pd, keep, got, extra):
    b = keep.shape[1]
    return call(
        functools.partial(combine_kernel, groups, stage, pd),
        exchange_shapes(groups, pd, b) + [jax.ShapeDtypeStruct((8, 128), f32)],
        [VM, VM, VM],
        [pltpu.VMEM((groups * pd, b, b), f32)],
        flops=groups * pd * b * b,
        moved=8 * groups * pd * b * b,
    )(keep, got, extra)


def exchange(sectors, pd, send, keep, extra):
    stage = 0
    groups = sectors
    while True:
        got = lax.ppermute(send, "sector", [(i, i ^ (1 << stage)) for i in range(sectors)])
        groups //= 2
        stage += 1
        if groups == 1:
            return keep, got, extra
        send, keep, extra = combine(groups, stage, pd, keep, got, extra)


def second_kernel(bounds, groups, scale, *rest):
    n = len(bounds)
    lefts, rights = rest[:n], rest[n : 2 * n]
    (m, coef, routes, onsite, sizes, keep_in, got, corr_in, squares_in,
     image_out, resid_out, send, keep, sq_out, acc) = rest[2 * n :]
    pd, b = m.shape[0], m.shape[1]
    acc[...] = jnp.zeros_like(acc)
    squares = squares_in[0:1, 0:1]
    corr = corr_in[0:1, 0:1] + from_terms(got[pl.ds(pd * b, EXTRA)])[:, 0:1]
    ritz = corr / (squares + epsilon)
    sums = jnp.zeros((b, b), f32)
    for k in range(pd):
        g = m[k].astype(f32)
        summed = keep_in[k] + got[pl.ds(k * b, b)].astype(f32) + onsite[0, k] * g
        image = jnp.where(live_of(sizes[k], (b, b)), summed, 0.0)
        image_out[0, k] = image.astype(bf16)
        resid = image - ritz * g
        resid_out[k] = resid.astype(bf16)
        sums += resid * resid
    total = total_of(sums)
    sq_out[...] = jnp.broadcast_to(total, sq_out.shape)
    vectors = [resid_out[k] for k in range(pd)]
    for i, (start, count) in enumerate(bounds):

        def load(k, at, unit):
            return lefts[i][k, pl.ds(at, unit)], rights[i][k, pl.ds(at, unit)]

        apply_blocks(load, count, vectors, start, acc, coef, routes, scale, unit_of(count))
    me = lax.axis_index("sector")
    split_halves(acc, groups, pd, b, lax.rem(me, 2), send, keep, total)


def second_apply(bounds, groups, channels, lefts, rights, m, coef, routes, onsite, sizes, keep, got, corr, squares):
    pd, b, _ = m.shape
    n = len(bounds)
    block = jax.ShapeDtypeStruct((1, pd, b, b), bf16)
    return call(
        functools.partial(second_kernel, bounds, groups, channels ** (-0.5)),
        [block, jax.ShapeDtypeStruct((pd, b, b), bf16)]
        + exchange_shapes(groups, pd, b)
        + [jax.ShapeDtypeStruct((8, 128), f32)],
        [VM] * (2 * n) + [VM, SM, SM, SM, SM, VM, VM, VM, VM],
        [pltpu.VMEM((groups * pd, b, b), f32)],
        flops=4 * pd * channels * b**3,
        moved=4 * pd * channels * b * b,
    )(*lefts, *rights, m, coef, routes, onsite, sizes, keep, got, corr, squares)


def final_kernel(resid, onsite, sizes, keep, got, sq_in, squares_in, out):
    pd, b = resid.shape[0], resid.shape[1]
    sq = sq_in[0:1, 0:1] + from_terms(got[pl.ds(pd * b, EXTRA)])[:, 0:1]
    alpha = jnp.sqrt(squares_in[0:1, 0:1] / (sq + epsilon))
    for k in range(pd):
        summed = keep[k] + got[pl.ds(k * b, b)].astype(f32) + onsite[0, k] * resid[k].astype(f32)
        out[0, k] = jnp.where(live_of(sizes[k], (b, b)), alpha * summed, 0.0).astype(bf16)


def final(resid, onsite, sizes, keep, got, sq, squares):
    pd, b, _ = resid.shape
    return call(
        final_kernel,
        [jax.ShapeDtypeStruct((1, pd, b, b), bf16)],
        [VM, SM, SM, VM, VM, VM, VM],
        moved=8 * pd * b * b,
    )(resid, onsite, sizes, keep, got, sq, squares)[0]


def gather_waves(sectors, m):
    held, pieces = m[None], []
    step = 1
    while step < sectors:
        other = lax.ppermute(held, "sector", [(i, i ^ step) for i in range(sectors)])
        pieces.append(other)
        step *= 2
        if step < sectors:
            held = jnp.concatenate([held, other], axis=0)
    return pieces


def body(
    env_left, env_right, edge_left, edge_right, wave_blocks, mpo_coef, onsite, routes, sector_sizes
):
    channels = env_left.shape[2]
    sections = lax.axis_size("section")
    sectors = lax.axis_size("sector")
    pd = wave_blocks.shape[1]
    bounds, at = [], 0
    for c in chunk_sizes(channels):
        bounds.append((at, c))
        at += c
    up = [(i, i + 1) for i in range(sections - 1)]
    down = [(i + 1, i) for i in range(sections - 1)]
    def pass_on(grown):
        return lax.ppermute(grown[0], "section", up), lax.ppermute(grown[1], "section", down)

    token, (head,) = grow(env_left, env_right, edge_left, edge_right, bounds[:1], (), VMEM_LARGE)
    got = [pass_on(head)]
    _, (middle, last) = grow(env_left, env_right, edge_left, edge_right, bounds[1:], (token,), VMEM_LARGE)
    got.append(pass_on(middle))
    grown, token = gate(last, got[0])
    m = mask_wave(wave_blocks, sector_sizes, token)
    got.append(pass_on(grown))
    pieces = gather_waves(sectors, m)
    own_l, own_r = own_ends(env_left, env_right, m)
    acc, lefts, rights = None, [], []
    for i, chunk in enumerate(bounds):
        is_last = i == len(bounds) - 1
        res = first_apply(
            chunk, i == 0, is_last, sectors, channels,
            (own_l, own_r, got[i][0], got[i][1], m, mpo_coef, routes), acc, (onsite, *pieces),
        )
        lefts.append(res[0])
        rights.append(res[1])
        acc = res[2]
    send, keep, squares, corr = res[2:]
    keep, summed, corr = exchange(sectors, pd, send, keep, corr)
    image1, resid, send, keep, sq = second_apply(
        bounds, sectors, channels, lefts, rights, m, mpo_coef, routes, onsite,
        sector_sizes, keep, summed, corr, squares,
    )
    keep, summed, sq = exchange(sectors, pd, send, keep, sq)
    image2 = final(resid, onsite, sector_sizes, keep, summed, sq, squares)
    return (image1, image2)


def solution(mesh):
    in_specs = (
        P(("groups", "section"), "sector", None, None, None),
        P(("groups", "section"), "sector", None, None, None),
        P(("groups", "section"), "sector", None, None),
        P(("groups", "section"), "sector", None, None),
        P(("groups", "section"), "sector", None, None),
        P(("groups", "section"), "sector", None),
        P(("groups", "section"), "sector"),
        P(("groups", "section"), "sector", None),
        P(("groups", "sector")),
    )
    out_specs = (
        P(("groups", "section"), "sector", None, None),
        P(("groups", "section"), "sector", None, None),
    )
    return jax.shard_map(body, mesh=mesh, in_specs=in_specs, out_specs=out_specs, check_vma=False)
```

```python
import functools

import jax
import jax.numpy as jnp
from jax import lax
from jax.experimental import pallas as pl
from jax.experimental.pallas import tpu as pltpu
from jax.sharding import PartitionSpec as P

epsilon = 1e-06
VMEM_BYTES = 16 * 1024 * 1024
VMEM_LARGE = 56 * 1024 * 1024
EXTRA = 16

f32 = jnp.float32
bf16 = jnp.bfloat16

VM = pl.BlockSpec(memory_space=pltpu.VMEM)
SM = pl.BlockSpec(memory_space=pltpu.SMEM)
HB = pl.BlockSpec(memory_space=pltpu.HBM)


def call(kernel, outs, in_specs, scratch=(), aliases=None, flops=0, moved=0, out_specs=None, vmem=VMEM_BYTES):
    return pl.pallas_call(
        kernel,
        out_shape=outs,
        in_specs=in_specs,
        out_specs=[VM] * len(outs) if out_specs is None else out_specs,
        scratch_shapes=list(scratch),
        input_output_aliases=aliases or {},
        compiler_params=pltpu.CompilerParams(vmem_limit_bytes=vmem),
        cost_estimate=pl.CostEstimate(flops=flops, bytes_accessed=moved, transcendentals=0),
    )


def dot(a, b):
    return jnp.dot(a, b, preferred_element_type=f32)


def dot_t(a, b):
    return lax.dot_general(a, b, (((1,), (1,)), ((), ())), preferred_element_type=f32)


def chunk_sizes(channels):
    first, last = max(1, channels * 3 // 10), max(1, channels // 10)
    return [c for c in (first, channels - first - last, last) if c > 0]


def unit_of(count, most=11):
    return max(u for u in range(1, most + 1) if count % u == 0)


def up_first():
    return lax.rem(lax.axis_index("sector"), 2) == 0


def grow_kernel(bounds, left_hbm, right_hbm, edge_l_hbm, edge_r_hbm, *rest):
    n = len(bounds)
    rest = rest[-6 * n - 6 :]
    token, rest = rest[0], rest[1:]
    outs, bufs, results = rest[: 2 * n], rest[2 * n : 4 * n], rest[4 * n : 6 * n]
    edge_l, edge_r, edge_sems, in_sems, out_sems = rest[6 * n :]
    pd, b = edge_l.shape[0], edge_l.shape[1]
    edges = [
        pltpu.make_async_copy(edge_l_hbm.at[0], edge_l, edge_sems.at[0]),
        pltpu.make_async_copy(edge_r_hbm.at[0], edge_r, edge_sems.at[1]),
    ]
    for c in edges:
        c.start()
    loads = {}
    for i, (start, count) in enumerate(bounds):
        for k in range(pd):
            for side, src in enumerate((left_hbm, right_hbm)):
                c = pltpu.make_async_copy(
                    src.at[0, k, pl.ds(start, count)], bufs[2 * i + side].at[k], in_sems.at[i, k, side]
                )
                c.start()
                loads[i, k, side] = c
    for c in edges:
        c.wait()
    sends = []
    for i, (start, count) in enumerate(bounds):
        unit = unit_of(count)
        buf_l, buf_r = bufs[2 * i], bufs[2 * i + 1]
        res_l, res_r = results[2 * i], results[2 * i + 1]
        for k in range(pd):
            e = edge_l[k]
            e_t = e.T
            f = edge_r[k]
            loads[i, k, 0].wait()
            loads[i, k, 1].wait()

            def step(s, carry):
                at = s * unit
                left = [dot(e_t, buf_l[k, at + u]).astype(bf16) for u in range(unit)]
                right = [dot(f, buf_r[k, at + u]).astype(bf16) for u in range(unit)]
                grown = dot(jnp.concatenate(left, axis=0), e).astype(bf16)
                res_l[k, pl.ds(at, unit)] = grown.reshape(unit, b, b)
                for u in range(unit):
                    res_r[k, at + u] = dot_t(f, right[u]).astype(bf16)
                return carry

            if count == unit:
                step(0, 0)
            else:
                lax.fori_loop(0, count // unit, step, 0)
            out_x, out_y = outs[2 * i].at[k], outs[2 * i + 1].at[k]
            sem_x, sem_y = out_sems.at[i, k, 0], out_sems.at[i, k, 1]

            @pl.when(up_first())
            def _():
                pltpu.make_async_copy(res_l.at[k], out_x, sem_x).start()
                pltpu.make_async_copy(res_r.at[k], out_y, sem_y).start()

            @pl.when(jnp.logical_not(up_first()))
            def _():
                pltpu.make_async_copy(res_r.at[k], out_x, sem_x).start()
                pltpu.make_async_copy(res_l.at[k], out_y, sem_y).start()

            sends.append(pltpu.make_async_copy(res_l.at[k], out_x, sem_x))
            sends.append(pltpu.make_async_copy(res_r.at[k], out_y, sem_y))
    token[...] = jnp.zeros_like(token)
    for c in sends:
        c.wait()


def grow(env_left, env_right, edge_left, edge_right, bounds, after, vmem):
    _, pd, _, b, _ = env_left.shape
    n = len(bounds)
    counts = [c for _, c in bounds for _ in range(2)]
    total = sum(c for _, c in bounds)
    blocks = [pltpu.VMEM((pd, c, b, b), bf16) for c in counts]
    edge = pltpu.VMEM((pd, b, b), bf16)
    res = call(
        functools.partial(grow_kernel, bounds),
        [jax.ShapeDtypeStruct((8, 128), f32)] + [jax.ShapeDtypeStruct((pd, c, b, b), bf16) for c in counts],
        [HB] * (4 + len(after)),
        blocks + blocks + [
            edge, edge, pltpu.SemaphoreType.DMA((2,)),
            pltpu.SemaphoreType.DMA((n, pd, 2)), pltpu.SemaphoreType.DMA((n, pd, 2)),
        ],
        flops=8 * pd * total * b**3,
        moved=8 * pd * total * b * b,
        out_specs=[VM] + [HB] * (2 * n),
        vmem=vmem,
    )(env_left, env_right, edge_left, edge_right, *after)
    return res[0], [(res[2 * i + 1], res[2 * i + 2]) for i in range(n)]


def gate_kernel(*refs):
    refs[-1][...] = jnp.zeros_like(refs[-1])


def gate(arrays, after):
    *held, token = call(
        gate_kernel,
        [jax.ShapeDtypeStruct(a.shape, a.dtype) for a in arrays] + [jax.ShapeDtypeStruct((8, 128), f32)],
        [HB] * (len(arrays) + len(after)),
        aliases={i: i for i in range(len(arrays))},
        out_specs=[HB] * len(arrays) + [VM],
    )(*arrays, *after)
    return held, token


def own_kernel(left_hbm, right_hbm, after, out_l, out_r, sem):
    section = lax.axis_index("section")
    at_start = section == 0
    at_end = section == lax.axis_size("section") - 1
    pd, channels = out_l.shape[0], out_l.shape[1]

    @pl.when(at_start)
    def _():
        c = pltpu.make_async_copy(left_hbm.at[0], out_l, sem)
        c.start()
        c.wait()

    @pl.when(jnp.logical_not(at_start))
    def _():
        out_l[...] = jnp.zeros_like(out_l)

    @pl.when(at_end)
    def _():
        c = pltpu.make_async_copy(right_hbm.at[0], out_r, sem)
        c.start()
        c.wait()
        for k in range(pd):

            def step(w, carry):
                out_r[k, w] = out_r[k, w].T
                return carry

            lax.fori_loop(0, channels, step, 0)

    @pl.when(jnp.logical_not(at_end))
    def _():
        out_r[...] = jnp.zeros_like(out_r)


def own_ends(env_left, env_right, after):
    _, pd, channels, b, _ = env_left.shape
    shape = jax.ShapeDtypeStruct((pd, channels, b, b), bf16)
    return call(
        own_kernel, [shape, shape], [HB, HB, HB], [pltpu.SemaphoreType.DMA],
        flops=10**10, moved=10**6,
    )(env_left, env_right, after)


def live_of(size, shape):
    rows = lax.broadcasted_iota(jnp.int32, shape, 0) < size
    cols = lax.broadcasted_iota(jnp.int32, shape, 1) < size
    return rows & cols


def mask_kernel(wave, sizes, after, out):
    for k in range(wave.shape[1]):
        v = wave[0, k].astype(f32)
        out[k] = jnp.where(live_of(sizes[k], v.shape), v, 0.0).astype(bf16)


def mask_wave(wave, sizes, after):
    _, pd, b, _ = wave.shape
    return call(mask_kernel, [jax.ShapeDtypeStruct((pd, b, b), bf16)], [VM, SM, HB], moved=4 * pd * b * b)(wave, sizes, after)[0]


def apply_blocks(load, count, vectors, first, acc, coef, routes, scale, unit):
    pd, b = len(vectors), vectors[0].shape[0]

    def step(s, carry):
        at = s * unit
        loaded = [load(k, at, unit) for k in range(pd)]
        halves = [dot(loaded[k][0].reshape(unit * b, b), vectors[k]).astype(bf16) for k in range(pd)]
        for k in range(pd):
            for u in range(unit):
                contrib = dot(halves[k][u * b : (u + 1) * b], loaded[k][1][u])
                j = routes[0, k, first + at + u]
                acc[j] += contrib * (coef[0, k, first + at + u] * scale)
        return carry

    if count == unit:
        step(0, 0)
    else:
        lax.fori_loop(0, count // unit, step, 0)


def three_terms(x, rows):
    hi = x.astype(bf16).astype(f32)
    mid = (x - hi).astype(bf16).astype(f32)
    low = x - hi - mid
    place = lax.broadcasted_iota(jnp.int32, (EXTRA, 128), 0)
    return jnp.where(place == 0, hi, jnp.where(place == 1, mid, jnp.where(place == 2, low, 0.0))).astype(bf16)


def from_terms(rows):
    return jnp.sum(rows.astype(f32), axis=0, keepdims=True)


def total_of(x):
    return jnp.sum(jnp.sum(x, axis=0, keepdims=True), axis=1, keepdims=True)


def split_halves(acc, groups, pd, b, bit, send, keep, extra):
    for i in range(groups // 2):
        for q in range(pd):
            kept = acc[(2 * i + bit) * pd + q]
            sent = acc[(2 * i + 1 - bit) * pd + q]
            keep[i * pd + q] = kept
            send[pl.ds((i * pd + q) * b, b)] = sent.astype(bf16)
    send[pl.ds(groups // 2 * pd * b, EXTRA)] = three_terms(extra, EXTRA)


def first_kernel(
    chunk, is_first, is_last, groups, scale,
    own_l, own_r, got_x, got_y, m, coef, routes, *rest
):
    start, count = chunk
    up = up_first()
    rest = list(rest)
    acc_in = None if is_first else rest.pop(0)
    if is_last:
        onsite = rest.pop(0)
        pieces = []
        at = 1
        while at < groups:
            pieces.append(rest.pop(0))
            at += pieces[-1].shape[0]
        new_l, new_r, send, keep, squares_out, corr_out, acc = rest
    else:
        new_l, new_r, acc = rest
    pd, b = m.shape[0], m.shape[1]
    if is_first:
        acc[...] = jnp.zeros_like(acc)
    else:
        acc[...] = acc_in[...]

    def load(k, at, unit):
        here, there = pl.ds(at, unit), pl.ds(start + at, unit)
        got_first, got_second = got_x[k, here], got_y[k, here]
        left = jnp.where(up, got_first, got_second) + own_l[k, there]
        right = jnp.where(up, got_second, got_first) + own_r[k, there]
        new_l[k, here] = left
        new_r[k, here] = right
        return left, right

    apply_blocks(load, count, [m[k] for k in range(pd)], start, acc, coef, routes, scale, unit_of(count))
    if not is_last:
        return
    me = lax.axis_index("sector")
    corr = jnp.zeros((b, b), f32)
    squares = jnp.zeros((b, b), f32)
    for k in range(pd):
        g = m[k].astype(f32)
        corr += g * (acc[me * pd + k] + onsite[0, k] * g)
        squares += g * g
    distance = 1
    for piece in pieces:
        for i in range(piece.shape[0]):
            owner = lax.bitwise_xor(me, distance)
            for k in range(pd):
                g = piece[i, k].astype(f32)
                corr += g * acc[owner * pd + k]
                squares += g * g
            distance += 1
    corr = total_of(corr)
    squares_out[...] = jnp.broadcast_to(total_of(squares), squares_out.shape)
    corr_out[...] = jnp.broadcast_to(corr, corr_out.shape)
    split_halves(acc, groups, pd, b, lax.rem(me, 2), send, keep, corr)


def first_apply(chunk, is_first, is_last, groups, channels, arrays, acc_in, extra):
    start, count = chunk
    m = arrays[4]
    pd, b, _ = m.shape
    total = jax.ShapeDtypeStruct((groups * pd, b, b), f32)
    block = jax.ShapeDtypeStruct((pd, count, b, b), bf16)
    args = list(arrays)
    specs = [VM, VM, VM, VM, VM, SM, SM]
    if not is_first:
        args.append(acc_in)
        specs.append(VM)
    scratch = []
    if is_last:
        args += list(extra)
        specs += [SM] + [VM] * (len(extra) - 1)
        outs = [block, block] + exchange_shapes(groups, pd, b) + [jax.ShapeDtypeStruct((8, 128), f32)] * 2
        scratch = [pltpu.VMEM((groups * pd, b, b), f32)]
    else:
        outs = [block, block, total]
    return call(
        functools.partial(first_kernel, chunk, is_first, is_last, groups, channels ** (-0.5)),
        outs,
        specs,
        scratch,
        flops=4 * pd * count * b**3,
        moved=4 * pd * count * b * b,
    )(*args)


def exchange_shapes(groups, pd, b):
    half = groups // 2 * pd
    return [
        jax.ShapeDtypeStruct((half * b + EXTRA, b), bf16),
        jax.ShapeDtypeStruct((half, b, b), f32),
    ]


def combine_kernel(groups, stage, pd, keep_in, got, extra_in, send, keep, extra_out, acc):
    b = keep_in.shape[1]
    me = lax.axis_index("sector")
    for i in range(groups * pd):
        acc[i] = keep_in[i] + got[pl.ds(i * b, b)].astype(f32)
    extra = extra_in[0:1, 0:1] + from_terms(got[pl.ds(groups * pd * b, EXTRA)])[:, 0:1]
    extra_out[...] = jnp.broadcast_to(extra, extra_out.shape)
    bit = lax.rem(lax.div(me, 2**stage), 2)
    split_halves(acc, groups, pd, b, bit, send, keep, extra)


def combine(groups, stage, pd, keep, got, extra):
    b = keep.shape[1]
    return call(
        functools.partial(combine_kernel, groups, stage, pd),
        exchange_shapes(groups, pd, b) + [jax.ShapeDtypeStruct((8, 128), f32)],
        [VM, VM, VM],
        [pltpu.VMEM((groups * pd, b, b), f32)],
        flops=groups * pd * b * b,
        moved=8 * groups * pd * b * b,
    )(keep, got, extra)


def exchange(sectors, pd, send, keep, extra):
    stage = 0
    groups = sectors
    while True:
        got = lax.ppermute(send, "sector", [(i, i ^ (1 << stage)) for i in range(sectors)])
        groups //= 2
        stage += 1
        if groups == 1:
            return keep, got, extra
        send, keep, extra = combine(groups, stage, pd, keep, got, extra)


def second_kernel(bounds, groups, scale, *rest):
    n = len(bounds)
    lefts, rights = rest[:n], rest[n : 2 * n]
    (m, coef, routes, onsite, sizes, keep_in, got, corr_in, squares_in,
     image_out, resid_out, send, keep, sq_out, acc) = rest[2 * n :]
    pd, b = m.shape[0], m.shape[1]
    acc[...] = jnp.zeros_like(acc)
    squares = squares_in[0:1, 0:1]
    corr = corr_in[0:1, 0:1] + from_terms(got[pl.ds(pd * b, EXTRA)])[:, 0:1]
    ritz = corr / (squares + epsilon)
    sums = jnp.zeros((b, b), f32)
    for k in range(pd):
        g = m[k].astype(f32)
        summed = keep_in[k] + got[pl.ds(k * b, b)].astype(f32) + onsite[0, k] * g
        image = jnp.where(live_of(sizes[k], (b, b)), summed, 0.0)
        image_out[0, k] = image.astype(bf16)
        resid = image - ritz * g
        resid_out[k] = resid.astype(bf16)
        sums += resid * resid
    total = total_of(sums)
    sq_out[...] = jnp.broadcast_to(total, sq_out.shape)
    vectors = [resid_out[k] for k in range(pd)]
    for i, (start, count) in enumerate(bounds):

        def load(k, at, unit):
            return lefts[i][k, pl.ds(at, unit)], rights[i][k, pl.ds(at, unit)]

        apply_blocks(load, count, vectors, start, acc, coef, routes, scale, unit_of(count))
    me = lax.axis_index("sector")
    split_halves(acc, groups, pd, b, lax.rem(me, 2), send, keep, total)


def second_apply(bounds, groups, channels, lefts, rights, m, coef, routes, onsite, sizes, keep, got, corr, squares):
    pd, b, _ = m.shape
    n = len(bounds)
    block = jax.ShapeDtypeStruct((1, pd, b, b), bf16)
    return call(
        functools.partial(second_kernel, bounds, groups, channels ** (-0.5)),
        [block, jax.ShapeDtypeStruct((pd, b, b), bf16)]
        + exchange_shapes(groups, pd, b)
        + [jax.ShapeDtypeStruct((8, 128), f32)],
        [VM] * (2 * n) + [VM, SM, SM, SM, SM, VM, VM, VM, VM],
        [pltpu.VMEM((groups * pd, b, b), f32)],
        flops=4 * pd * channels * b**3,
        moved=4 * pd * channels * b * b,
    )(*lefts, *rights, m, coef, routes, onsite, sizes, keep, got, corr, squares)


def final_kernel(resid, onsite, sizes, keep, got, sq_in, squares_in, out):
    pd, b = resid.shape[0], resid.shape[1]
    sq = sq_in[0:1, 0:1] + from_terms(got[pl.ds(pd * b, EXTRA)])[:, 0:1]
    alpha = jnp.sqrt(squares_in[0:1, 0:1] / (sq + epsilon))
    for k in range(pd):
        summed = keep[k] + got[pl.ds(k * b, b)].astype(f32) + onsite[0, k] * resid[k].astype(f32)
        out[0, k] = jnp.where(live_of(sizes[k], (b, b)), alpha * summed, 0.0).astype(bf16)


def final(resid, onsite, sizes, keep, got, sq, squares):
    pd, b, _ = resid.shape
    return call(
        final_kernel,
        [jax.ShapeDtypeStruct((1, pd, b, b), bf16)],
        [VM, SM, SM, VM, VM, VM, VM],
        moved=8 * pd * b * b,
    )(resid, onsite, sizes, keep, got, sq, squares)[0]


def gather_waves(sectors, m):
    held, pieces = m[None], []
    step = 1
    while step < sectors:
        other = lax.ppermute(held, "sector", [(i, i ^ step) for i in range(sectors)])
        pieces.append(other)
        step *= 2
        if step < sectors:
            held = jnp.concatenate([held, other], axis=0)
    return pieces


def body(
    env_left, env_right, edge_left, edge_right, wave_blocks, mpo_coef, onsite, routes, sector_sizes
):
    channels = env_left.shape[2]
    sections = lax.axis_size("section")
    sectors = lax.axis_size("sector")
    pd = wave_blocks.shape[1]
    bounds, at = [], 0
    for c in chunk_sizes(channels):
        bounds.append((at, c))
        at += c
    up = [(i * sectors + j, (i + 1) * sectors + j) for i in range(sections - 1) for j in range(sectors)]
    first = [(a, b) if a % sectors % 2 == 0 else (b, a) for a, b in up]
    second = [(b, a) for a, b in first]

    def pass_on(grown):
        axes = ("section", "sector")
        return lax.ppermute(grown[0], axes, first), lax.ppermute(grown[1], axes, second)

    token, (head,) = grow(env_left, env_right, edge_left, edge_right, bounds[:1], (), VMEM_LARGE)
    got = [pass_on(head)]
    _, (middle, last) = grow(env_left, env_right, edge_left, edge_right, bounds[1:], (token,), VMEM_LARGE)
    got.append(pass_on(middle))
    grown, token = gate(last, got[0])
    m = mask_wave(wave_blocks, sector_sizes, token)
    got.append(pass_on(grown))
    pieces = gather_waves(sectors, m)
    own_l, own_r = own_ends(env_left, env_right, m)
    acc, lefts, rights = None, [], []
    for i, chunk in enumerate(bounds):
        is_last = i == len(bounds) - 1
        res = first_apply(
            chunk, i == 0, is_last, sectors, channels,
            (own_l, own_r, got[i][0], got[i][1], m, mpo_coef, routes), acc, (onsite, *pieces),
        )
        lefts.append(res[0])
        rights.append(res[1])
        acc = res[2]
    send, keep, squares, corr = res[2:]
    keep, summed, corr = exchange(sectors, pd, send, keep, corr)
    image1, resid, send, keep, sq = second_apply(
        bounds, sectors, channels, lefts, rights, m, mpo_coef, routes, onsite,
        sector_sizes, keep, summed, corr, squares,
    )
    keep, summed, sq = exchange(sectors, pd, send, keep, sq)
    image2 = final(resid, onsite, sector_sizes, keep, summed, sq, squares)
    return (image1, image2)


def solution(mesh):
    in_specs = (
        P(("groups", "section"), "sector", None, None, None),
        P(("groups", "section"), "sector", None, None, None),
        P(("groups", "section"), "sector", None, None),
        P(("groups", "section"), "sector", None, None),
        P(("groups", "section"), "sector", None, None),
        P(("groups", "section"), "sector", None),
        P(("groups", "section"), "sector"),
        P(("groups", "section"), "sector", None),
        P(("groups", "sector")),
    )
    out_specs = (
        P(("groups", "section"), "sector", None, None),
        P(("groups", "section"), "sector", None, None),
    )
    return jax.shard_map(body, mesh=mesh, in_specs=in_specs, out_specs=out_specs, check_vma=False)
```

```python
import functools

import jax
import jax.numpy as jnp
from jax import lax
from jax.experimental import pallas as pl
from jax.experimental.pallas import tpu as pltpu
from jax.sharding import PartitionSpec as P

epsilon = 1e-06
VMEM_BYTES = 16 * 1024 * 1024
VMEM_LARGE = 56 * 1024 * 1024
EXTRA = 32

f32 = jnp.float32
bf16 = jnp.bfloat16

VM = pl.BlockSpec(memory_space=pltpu.VMEM)
SM = pl.BlockSpec(memory_space=pltpu.SMEM)
HB = pl.BlockSpec(memory_space=pltpu.HBM)


def call(kernel, outs, in_specs, scratch=(), aliases=None, flops=0, moved=0, out_specs=None, vmem=VMEM_BYTES):
    return pl.pallas_call(
        kernel,
        out_shape=outs,
        in_specs=in_specs,
        out_specs=[VM] * len(outs) if out_specs is None else out_specs,
        scratch_shapes=list(scratch),
        input_output_aliases=aliases or {},
        compiler_params=pltpu.CompilerParams(vmem_limit_bytes=vmem),
        cost_estimate=pl.CostEstimate(flops=flops, bytes_accessed=moved, transcendentals=0),
    )


def dot(a, b):
    return jnp.dot(a, b, preferred_element_type=f32)


def dot_t(a, b):
    return lax.dot_general(a, b, (((1,), (1,)), ((), ())), preferred_element_type=f32)


def chunk_sizes(channels):
    first, last = max(1, channels * 3 // 10), max(1, channels // 10)
    return [c for c in (first, channels - first - last, last) if c > 0]


def unit_of(count, most=11):
    return max(u for u in range(1, most + 1) if count % u == 0)


def up_first():
    return lax.rem(lax.axis_index("sector"), 2) == 0


def grow_kernel(bounds, left_hbm, right_hbm, edge_l_hbm, edge_r_hbm, *rest):
    n = len(bounds)
    rest = rest[-6 * n - 6 :]
    token, rest = rest[0], rest[1:]
    outs, bufs, results = rest[: 2 * n], rest[2 * n : 4 * n], rest[4 * n : 6 * n]
    edge_l, edge_r, edge_sems, in_sems, out_sems = rest[6 * n :]
    pd, b = edge_l.shape[0], edge_l.shape[1]
    edges = [
        pltpu.make_async_copy(edge_l_hbm.at[0], edge_l, edge_sems.at[0]),
        pltpu.make_async_copy(edge_r_hbm.at[0], edge_r, edge_sems.at[1]),
    ]
    for c in edges:
        c.start()
    loads = {}
    for i, (start, count) in enumerate(bounds):
        for k in range(pd):
            for side, src in enumerate((left_hbm, right_hbm)):
                c = pltpu.make_async_copy(
                    src.at[0, k, pl.ds(start, count)], bufs[2 * i + side].at[k], in_sems.at[i, k, side]
                )
                c.start()
                loads[i, k, side] = c
    for c in edges:
        c.wait()
    sends = []
    for i, (start, count) in enumerate(bounds):
        unit = unit_of(count)
        buf_l, buf_r = bufs[2 * i], bufs[2 * i + 1]
        res_l, res_r = results[2 * i], results[2 * i + 1]
        for k in range(pd):
            e = edge_l[k]
            e_t = e.T
            f = edge_r[k]
            loads[i, k, 0].wait()
            loads[i, k, 1].wait()

            def step(s, carry):
                at = s * unit
                left = [dot(e_t, buf_l[k, at + u]).astype(bf16) for u in range(unit)]
                right = [dot(f, buf_r[k, at + u]).astype(bf16) for u in range(unit)]
                grown = dot(jnp.concatenate(left, axis=0), e).astype(bf16)
                res_l[k, pl.ds(at, unit)] = grown.reshape(unit, b, b)
                for u in range(unit):
                    res_r[k, at + u] = dot_t(f, right[u]).astype(bf16)
                return carry

            if count == unit:
                step(0, 0)
            else:
                lax.fori_loop(0, count // unit, step, 0)
            out_x, out_y = outs[2 * i].at[k], outs[2 * i + 1].at[k]
            sem_x, sem_y = out_sems.at[i, k, 0], out_sems.at[i, k, 1]

            @pl.when(up_first())
            def _():
                pltpu.make_async_copy(res_l.at[k], out_x, sem_x).start()
                pltpu.make_async_copy(res_r.at[k], out_y, sem_y).start()

            @pl.when(jnp.logical_not(up_first()))
            def _():
                pltpu.make_async_copy(res_r.at[k], out_x, sem_x).start()
                pltpu.make_async_copy(res_l.at[k], out_y, sem_y).start()

            sends.append(pltpu.make_async_copy(res_l.at[k], out_x, sem_x))
            sends.append(pltpu.make_async_copy(res_r.at[k], out_y, sem_y))
    token[...] = jnp.zeros_like(token)
    for c in sends:
        c.wait()


def grow(env_left, env_right, edge_left, edge_right, bounds, after, vmem):
    _, pd, _, b, _ = env_left.shape
    n = len(bounds)
    counts = [c for _, c in bounds for _ in range(2)]
    total = sum(c for _, c in bounds)
    blocks = [pltpu.VMEM((pd, c, b, b), bf16) for c in counts]
    edge = pltpu.VMEM((pd, b, b), bf16)
    res = call(
        functools.partial(grow_kernel, bounds),
        [jax.ShapeDtypeStruct((8, 128), f32)] + [jax.ShapeDtypeStruct((pd, c, b, b), bf16) for c in counts],
        [HB] * (4 + len(after)),
        blocks + blocks + [
            edge, edge, pltpu.SemaphoreType.DMA((2,)),
            pltpu.SemaphoreType.DMA((n, pd, 2)), pltpu.SemaphoreType.DMA((n, pd, 2)),
        ],
        flops=8 * pd * total * b**3,
        moved=8 * pd * total * b * b,
        out_specs=[VM] + [HB] * (2 * n),
        vmem=vmem,
    )(env_left, env_right, edge_left, edge_right, *after)
    return res[0], [(res[2 * i + 1], res[2 * i + 2]) for i in range(n)]


def gate_kernel(*refs):
    refs[-1][...] = jnp.zeros_like(refs[-1])


def gate(arrays, after):
    *held, token = call(
        gate_kernel,
        [jax.ShapeDtypeStruct(a.shape, a.dtype) for a in arrays] + [jax.ShapeDtypeStruct((8, 128), f32)],
        [HB] * (len(arrays) + len(after)),
        aliases={i: i for i in range(len(arrays))},
        out_specs=[HB] * len(arrays) + [VM],
    )(*arrays, *after)
    return held, token


def own_kernel(left_hbm, right_hbm, after, out_l, out_r, sem):
    section = lax.axis_index("section")
    at_start = section == 0
    at_end = section == lax.axis_size("section") - 1
    pd, channels = out_l.shape[0], out_l.shape[1]

    @pl.when(at_start)
    def _():
        c = pltpu.make_async_copy(left_hbm.at[0], out_l, sem)
        c.start()
        c.wait()

    @pl.when(jnp.logical_not(at_start))
    def _():
        out_l[...] = jnp.zeros_like(out_l)

    @pl.when(at_end)
    def _():
        c = pltpu.make_async_copy(right_hbm.at[0], out_r, sem)
        c.start()
        c.wait()
        for k in range(pd):

            def step(w, carry):
                out_r[k, w] = out_r[k, w].T
                return carry

            lax.fori_loop(0, channels, step, 0)

    @pl.when(jnp.logical_not(at_end))
    def _():
        out_r[...] = jnp.zeros_like(out_r)


def own_ends(env_left, env_right, after):
    _, pd, channels, b, _ = env_left.shape
    shape = jax.ShapeDtypeStruct((pd, channels, b, b), bf16)
    return call(
        own_kernel, [shape, shape], [HB, HB, HB], [pltpu.SemaphoreType.DMA],
        flops=10**10, moved=10**6,
    )(env_left, env_right, after)


def live_of(size, shape):
    rows = lax.broadcasted_iota(jnp.int32, shape, 0) < size
    cols = lax.broadcasted_iota(jnp.int32, shape, 1) < size
    return rows & cols


def prepare_kernel(scale, wave, coef, onsite, sizes, after, out, live, weights, energy):
    pd, channels = weights.shape[0], weights.shape[1]
    for k in range(pd):
        v = wave[0, k].astype(f32)
        alive = live_of(sizes[k], v.shape)
        out[k] = jnp.where(alive, v, 0.0).astype(bf16)
        live[k] = jnp.where(alive, 1.0, 0.0)
        energy[k] = jnp.full(energy.shape[1:], onsite[0, k], f32)

        def step(w, carry):
            weights[k, w] = jnp.full(weights.shape[2:], coef[0, k, w] * scale, f32)
            return carry

        lax.fori_loop(0, channels, step, 0)


def prepare(wave, coef, onsite, sizes, after):
    _, pd, b, _ = wave.shape
    channels = coef.shape[2]
    return call(
        functools.partial(prepare_kernel, channels ** (-0.5)),
        [
            jax.ShapeDtypeStruct((pd, b, b), bf16),
            jax.ShapeDtypeStruct((pd, b, b), f32),
            jax.ShapeDtypeStruct((pd, channels, 8, b), f32),
            jax.ShapeDtypeStruct((pd, 8, b), f32),
        ],
        [VM, SM, SM, SM, HB],
        moved=4 * pd * b * b,
    )(wave, coef, onsite, sizes, after)


def times(tile, x):
    return (x.reshape(-1, 8, x.shape[-1]) * tile).reshape(x.shape)


def apply_blocks(load, count, vectors, first, acc, weights, routes, unit, ready=None):
    pd, b = len(vectors), vectors[0].shape[0]

    def step(s, carry):
        at = s * unit
        loaded = [load(k, at, unit) for k in range(pd)]
        halves = [dot(loaded[k][0].reshape(unit * b, b), vectors[k]).astype(bf16) for k in range(pd)]
        if ready is not None:
            ready.wait()
        for k in range(pd):
            for u in range(unit):
                contrib = dot(halves[k][u * b : (u + 1) * b], loaded[k][1][u])
                j = routes[0, k, first + at + u]
                acc[j] += times(weights[k, first + at + u], contrib)
        return carry

    if count == unit:
        step(0, 0)
    else:
        lax.fori_loop(0, count // unit, step, 0)


def three_terms(x):
    hi = x.astype(bf16).astype(f32)
    mid = (x - hi).astype(bf16).astype(f32)
    low = x - hi - mid
    return jnp.concatenate([hi, mid, low, jnp.zeros_like(x)], axis=0).astype(bf16)


def from_terms(rows):
    return fold(rows.astype(f32))


def fold(x):
    return jnp.sum(x.reshape(-1, 8, x.shape[-1]), axis=0)


def total_of(x):
    return jnp.sum(jnp.sum(x, axis=0, keepdims=True), axis=1, keepdims=True)


def split_halves(acc, groups, pd, b, bit, send, keep, extra):
    for i in range(groups // 2):
        for q in range(pd):
            kept = acc[(2 * i + bit) * pd + q]
            sent = acc[(2 * i + 1 - bit) * pd + q]
            keep[i * pd + q] = kept
            send[pl.ds((i * pd + q) * b, b)] = sent.astype(bf16)
    send[pl.ds(groups // 2 * pd * b, EXTRA)] = three_terms(extra)


def first_kernel(
    chunk, is_first, is_last, groups,
    own_l, own_r, got_x, got_y, m, weights, routes_in, *rest
):
    start, count = chunk
    up = up_first()
    rest = list(rest)
    acc_in = None if is_first else rest.pop(0)
    if is_last:
        energy = rest.pop(0)
        pieces = []
        at = 1
        while at < groups:
            pieces.append(rest.pop(0))
            at += pieces[-1].shape[0]
        new_l, new_r, send, keep, squares_out, corr_out, routes, routes_sem, acc = rest
    else:
        new_l, new_r, acc, routes, routes_sem = rest
    routes_copy = pltpu.make_async_copy(routes_in, routes, routes_sem)
    routes_copy.start()
    pd, b = m.shape[0], m.shape[1]
    if is_first:
        acc[...] = jnp.zeros_like(acc)
    else:
        acc[...] = acc_in[...]

    def load(k, at, unit):
        here, there = pl.ds(at, unit), pl.ds(start + at, unit)
        got_first, got_second = got_x[k, here], got_y[k, here]
        left = jnp.where(up, got_first, got_second) + own_l[k, there]
        right = jnp.where(up, got_second, got_first) + own_r[k, there]
        new_l[k, here] = left
        new_r[k, here] = right
        return left, right

    unit = unit_of(count)
    ready = routes_copy if unit == count else None
    if ready is None:
        routes_copy.wait()
    apply_blocks(load, count, [m[k] for k in range(pd)], start, acc, weights, routes, unit, ready)
    if not is_last:
        return
    me = lax.axis_index("sector")
    corr = jnp.zeros((b, b), f32)
    squares = jnp.zeros((b, b), f32)
    for k in range(pd):
        g = m[k].astype(f32)
        corr += g * (acc[me * pd + k] + times(energy[k], g))
        squares += g * g
    distance = 1
    for piece in pieces:
        for i in range(piece.shape[0]):
            owner = lax.bitwise_xor(me, distance)
            for k in range(pd):
                g = piece[i, k].astype(f32)
                corr += g * acc[owner * pd + k]
                squares += g * g
            distance += 1
    corr = fold(corr)
    squares_out[...] = fold(squares)
    corr_out[...] = corr
    split_halves(acc, groups, pd, b, lax.rem(me, 2), send, keep, corr)


def first_apply(chunk, is_first, is_last, groups, arrays, acc_in, extra):
    start, count = chunk
    m = arrays[4]
    pd, b, _ = m.shape
    total = jax.ShapeDtypeStruct((groups * pd, b, b), f32)
    block = jax.ShapeDtypeStruct((pd, count, b, b), bf16)
    args = list(arrays)
    specs = [VM, VM, VM, VM, VM, VM, HB]
    if not is_first:
        args.append(acc_in)
        specs.append(VM)
    scratch = [pltpu.SMEM(arrays[6].shape, jnp.int32), pltpu.SemaphoreType.DMA]
    if is_last:
        args += list(extra)
        specs += [VM] * len(extra)
        outs = [block, block] + exchange_shapes(groups, pd, b) + [jax.ShapeDtypeStruct((8, 128), f32)] * 2
        scratch.append(pltpu.VMEM((groups * pd, b, b), f32))
    else:
        outs = [block, block, total]
    return call(
        functools.partial(first_kernel, chunk, is_first, is_last, groups),
        outs,
        specs,
        scratch,
        flops=4 * pd * count * b**3,
        moved=4 * pd * count * b * b,
    )(*args)


def exchange_shapes(groups, pd, b):
    half = groups // 2 * pd
    return [
        jax.ShapeDtypeStruct((half * b + EXTRA, b), bf16),
        jax.ShapeDtypeStruct((half, b, b), f32),
    ]


def combine_kernel(groups, stage, pd, keep_in, got, extra_in, send, keep, extra_out, acc):
    b = keep_in.shape[1]
    me = lax.axis_index("sector")
    for i in range(groups * pd):
        acc[i] = keep_in[i] + got[pl.ds(i * b, b)].astype(f32)
    extra = extra_in[...] + from_terms(got[pl.ds(groups * pd * b, EXTRA)])
    extra_out[...] = extra
    bit = lax.rem(lax.div(me, 2**stage), 2)
    split_halves(acc, groups, pd, b, bit, send, keep, extra)


def combine(groups, stage, pd, keep, got, extra):
    b = keep.shape[1]
    return call(
        functools.partial(combine_kernel, groups, stage, pd),
        exchange_shapes(groups, pd, b) + [jax.ShapeDtypeStruct((8, 128), f32)],
        [VM, VM, VM],
        [pltpu.VMEM((groups * pd, b, b), f32)],
        flops=groups * pd * b * b,
        moved=8 * groups * pd * b * b,
    )(keep, got, extra)


def exchange(sectors, pd, send, keep, extra):
    stage = 0
    groups = sectors
    while True:
        got = lax.ppermute(send, "sector", [(i, i ^ (1 << stage)) for i in range(sectors)])
        groups //= 2
        stage += 1
        if groups == 1:
            return keep, got, extra
        send, keep, extra = combine(groups, stage, pd, keep, got, extra)


def second_kernel(bounds, groups, *rest):
    n = len(bounds)
    lefts, rights = rest[:n], rest[n : 2 * n]
    (m, weights, routes_in, energy, live, keep_in, got, corr_in, squares_in,
     image_hbm, resid_out, send, keep, sq_out, acc, image_out, image_sem, routes, routes_sem) = rest[2 * n :]
    pd, b = m.shape[0], m.shape[1]
    routes_copy = pltpu.make_async_copy(routes_in, routes, routes_sem)
    routes_copy.start()
    acc[...] = jnp.zeros_like(acc)
    squares = total_of(squares_in[...])
    corr = total_of(corr_in[...] + from_terms(got[pl.ds(pd * b, EXTRA)]))
    ritz = corr / (squares + epsilon)
    sums = jnp.zeros((b, b), f32)
    for k in range(pd):
        g = m[k].astype(f32)
        summed = keep_in[k] + got[pl.ds(k * b, b)].astype(f32) + times(energy[k], g)
        image = jnp.where(live[k] > 0.0, summed, 0.0)
        image_out[k] = image.astype(bf16)
        resid = image - ritz * g
        resid_out[k] = resid.astype(bf16)
        sums += resid * resid
    image_copy = pltpu.make_async_copy(image_out, image_hbm.at[0], image_sem)
    image_copy.start()
    total = fold(sums)
    sq_out[...] = total
    vectors = [resid_out[k] for k in range(pd)]
    routes_copy.wait()
    for i, (start, count) in enumerate(bounds):

        def load(k, at, unit):
            return lefts[i][k, pl.ds(at, unit)], rights[i][k, pl.ds(at, unit)]

        apply_blocks(load, count, vectors, start, acc, weights, routes, unit_of(count))
    me = lax.axis_index("sector")
    split_halves(acc, groups, pd, b, lax.rem(me, 2), send, keep, total)
    image_copy.wait()


def second_apply(bounds, groups, channels, lefts, rights, m, weights, routes, energy, live, keep, got, corr, squares):
    pd, b, _ = m.shape
    n = len(bounds)
    block = jax.ShapeDtypeStruct((1, pd, b, b), bf16)
    return call(
        functools.partial(second_kernel, bounds, groups),
        [block, jax.ShapeDtypeStruct((pd, b, b), bf16)]
        + exchange_shapes(groups, pd, b)
        + [jax.ShapeDtypeStruct((8, 128), f32)],
        [VM] * (2 * n) + [VM, VM, HB, VM, VM, VM, VM, VM, VM],
        [
            pltpu.VMEM((groups * pd, b, b), f32), pltpu.VMEM((pd, b, b), bf16), pltpu.SemaphoreType.DMA,
            pltpu.SMEM(routes.shape, jnp.int32), pltpu.SemaphoreType.DMA,
        ],
        flops=4 * pd * channels * b**3,
        moved=4 * pd * channels * b * b,
        out_specs=[HB, VM, VM, VM, VM],
    )(*lefts, *rights, m, weights, routes, energy, live, keep, got, corr, squares)


def final_kernel(resid, energy, live, keep, got, sq_in, squares_in, out, image, sems):
    pd, b = resid.shape[0], resid.shape[1]
    sq = total_of(sq_in[...] + from_terms(got[pl.ds(pd * b, EXTRA)]))
    alpha = jnp.sqrt(total_of(squares_in[...]) / (sq + epsilon))
    copies = []
    for k in range(pd):
        summed = keep[k] + got[pl.ds(k * b, b)].astype(f32) + times(energy[k], resid[k].astype(f32))
        image[k] = jnp.where(live[k] > 0.0, alpha * summed, 0.0).astype(bf16)
        copies.append(pltpu.make_async_copy(image.at[k], out.at[0, k], sems.at[k]))
        copies[-1].start()
    for c in copies:
        c.wait()


def final(resid, energy, live, keep, got, sq, squares):
    pd, b, _ = resid.shape
    return call(
        final_kernel,
        [jax.ShapeDtypeStruct((1, pd, b, b), bf16)],
        [VM] * 7,
        [pltpu.VMEM((pd, b, b), bf16), pltpu.SemaphoreType.DMA((pd,))],
        moved=8 * pd * b * b,
        out_specs=[HB],
    )(resid, energy, live, keep, got, sq, squares)[0]


def gather_waves(sectors, m):
    held, pieces = m[None], []
    step = 1
    while step < sectors:
        other = lax.ppermute(held, "sector", [(i, i ^ step) for i in range(sectors)])
        pieces.append(other)
        step *= 2
        if step < sectors:
            held = jnp.concatenate([held, other], axis=0)
    return pieces


def body(
    env_left, env_right, edge_left, edge_right, wave_blocks, mpo_coef, onsite, routes, sector_sizes
):
    channels = env_left.shape[2]
    sections = lax.axis_size("section")
    sectors = lax.axis_size("sector")
    pd = wave_blocks.shape[1]
    bounds, at = [], 0
    for c in chunk_sizes(channels):
        bounds.append((at, c))
        at += c
    up = [(i * sectors + j, (i + 1) * sectors + j) for i in range(sections - 1) for j in range(sectors)]
    first = [(a, b) if a % sectors % 2 == 0 else (b, a) for a, b in up]
    second = [(b, a) for a, b in first]

    def pass_on(grown):
        axes = ("section", "sector")
        return lax.ppermute(grown[0], axes, first), lax.ppermute(grown[1], axes, second)

    token, (head,) = grow(env_left, env_right, edge_left, edge_right, bounds[:1], (), VMEM_LARGE)
    got = [pass_on(head)]
    _, (middle, last) = grow(env_left, env_right, edge_left, edge_right, bounds[1:], (token,), VMEM_LARGE)
    got.append(pass_on(middle))
    grown, token = gate(last, got[0])
    m, live, weights, energy = prepare(wave_blocks, mpo_coef, onsite, sector_sizes, token)
    got.append(pass_on(grown))
    pieces = gather_waves(sectors, m)
    own_l, own_r = own_ends(env_left, env_right, m)
    acc, lefts, rights = None, [], []
    for i, chunk in enumerate(bounds):
        is_last = i == len(bounds) - 1
        res = first_apply(
            chunk, i == 0, is_last, sectors,
            (own_l, own_r, got[i][0], got[i][1], m, weights, routes), acc, (energy, *pieces),
        )
        lefts.append(res[0])
        rights.append(res[1])
        acc = res[2]
    send, keep, squares, corr = res[2:]
    keep, summed, corr = exchange(sectors, pd, send, keep, corr)
    image1, resid, send, keep, sq = second_apply(
        bounds, sectors, channels, lefts, rights, m, weights, routes, energy,
        live, keep, summed, corr, squares,
    )
    keep, summed, sq = exchange(sectors, pd, send, keep, sq)
    image2 = final(resid, energy, live, keep, summed, sq, squares)
    return (image1, image2)


def solution(mesh):
    in_specs = (
        P(("groups", "section"), "sector", None, None, None),
        P(("groups", "section"), "sector", None, None, None),
        P(("groups", "section"), "sector", None, None),
        P(("groups", "section"), "sector", None, None),
        P(("groups", "section"), "sector", None, None),
        P(("groups", "section"), "sector", None),
        P(("groups", "section"), "sector"),
        P(("groups", "section"), "sector", None),
        P(("groups", "sector")),
    )
    out_specs = (
        P(("groups", "section"), "sector", None, None),
        P(("groups", "section"), "sector", None, None),
    )
    return jax.shard_map(body, mesh=mesh, in_specs=in_specs, out_specs=out_specs, check_vma=False)
```

```python
import functools

import jax
import jax.numpy as jnp
from jax import lax
from jax.experimental import pallas as pl
from jax.experimental.pallas import tpu as pltpu
from jax.sharding import PartitionSpec as P

epsilon = 1e-06
VMEM_BYTES = 16 * 1024 * 1024
VMEM_LARGE = 56 * 1024 * 1024
EXTRA = 32

f32 = jnp.float32
bf16 = jnp.bfloat16

VM = pl.BlockSpec(memory_space=pltpu.VMEM)
SM = pl.BlockSpec(memory_space=pltpu.SMEM)
HB = pl.BlockSpec(memory_space=pltpu.HBM)


def call(kernel, outs, in_specs, scratch=(), aliases=None, flops=0, moved=0, out_specs=None, vmem=VMEM_BYTES):
    return pl.pallas_call(
        kernel,
        out_shape=outs,
        in_specs=in_specs,
        out_specs=[VM] * len(outs) if out_specs is None else out_specs,
        scratch_shapes=list(scratch),
        input_output_aliases=aliases or {},
        compiler_params=pltpu.CompilerParams(vmem_limit_bytes=vmem),
        cost_estimate=pl.CostEstimate(flops=flops, bytes_accessed=moved, transcendentals=0),
    )


def dot(a, b):
    return jnp.dot(a, b, preferred_element_type=f32)


def dot_t(a, b):
    return lax.dot_general(a, b, (((1,), (1,)), ((), ())), preferred_element_type=f32)


def chunk_sizes(channels):
    first, last = max(1, channels * 3 // 10), max(1, channels // 10)
    return [c for c in (first, channels - first - last, last) if c > 0]


def unit_of(count, most=11):
    return max(u for u in range(1, most + 1) if count % u == 0)


def up_first():
    return lax.rem(lax.axis_index("sector"), 2) == 0


def grow_kernel(bounds, left_hbm, right_hbm, edge_l_hbm, edge_r_hbm, *rest):
    n = len(bounds)
    rest = rest[-6 * n - 6 :]
    token, rest = rest[0], rest[1:]
    outs, bufs, results = rest[: 2 * n], rest[2 * n : 4 * n], rest[4 * n : 6 * n]
    edge_l, edge_r, edge_sems, in_sems, out_sems = rest[6 * n :]
    pd, b = edge_l.shape[0], edge_l.shape[1]
    edges = [
        pltpu.make_async_copy(edge_l_hbm.at[0], edge_l, edge_sems.at[0]),
        pltpu.make_async_copy(edge_r_hbm.at[0], edge_r, edge_sems.at[1]),
    ]
    for c in edges:
        c.start()
    loads = {}
    for i, (start, count) in enumerate(bounds):
        for k in range(pd):
            for side, src in enumerate((left_hbm, right_hbm)):
                c = pltpu.make_async_copy(
                    src.at[0, k, pl.ds(start, count)], bufs[2 * i + side].at[k], in_sems.at[i, k, side]
                )
                c.start()
                loads[i, k, side] = c
    for c in edges:
        c.wait()
    sends = []
    for i, (start, count) in enumerate(bounds):
        unit = unit_of(count)
        buf_l, buf_r = bufs[2 * i], bufs[2 * i + 1]
        res_l, res_r = results[2 * i], results[2 * i + 1]
        for k in range(pd):
            e = edge_l[k]
            e_t = e.T
            f = edge_r[k]
            loads[i, k, 0].wait()
            loads[i, k, 1].wait()

            def step(s, carry):
                at = s * unit
                left = [dot(e_t, buf_l[k, at + u]).astype(bf16) for u in range(unit)]
                right = [dot(f, buf_r[k, at + u]).astype(bf16) for u in range(unit)]
                grown = dot(jnp.concatenate(left, axis=0), e).astype(bf16)
                res_l[k, pl.ds(at, unit)] = grown.reshape(unit, b, b)
                for u in range(unit):
                    res_r[k, at + u] = dot_t(f, right[u]).astype(bf16)
                return carry

            if count == unit:
                step(0, 0)
            else:
                lax.fori_loop(0, count // unit, step, 0)
            out_x, out_y = outs[2 * i].at[k], outs[2 * i + 1].at[k]
            sem_x, sem_y = out_sems.at[i, k, 0], out_sems.at[i, k, 1]

            @pl.when(up_first())
            def _():
                pltpu.make_async_copy(res_l.at[k], out_x, sem_x).start()
                pltpu.make_async_copy(res_r.at[k], out_y, sem_y).start()

            @pl.when(jnp.logical_not(up_first()))
            def _():
                pltpu.make_async_copy(res_r.at[k], out_x, sem_x).start()
                pltpu.make_async_copy(res_l.at[k], out_y, sem_y).start()

            sends.append(pltpu.make_async_copy(res_l.at[k], out_x, sem_x))
            sends.append(pltpu.make_async_copy(res_r.at[k], out_y, sem_y))
    token[...] = jnp.zeros_like(token)
    for c in sends:
        c.wait()


def grow(env_left, env_right, edge_left, edge_right, bounds, after, vmem):
    _, pd, _, b, _ = env_left.shape
    n = len(bounds)
    counts = [c for _, c in bounds for _ in range(2)]
    total = sum(c for _, c in bounds)
    blocks = [pltpu.VMEM((pd, c, b, b), bf16) for c in counts]
    edge = pltpu.VMEM((pd, b, b), bf16)
    res = call(
        functools.partial(grow_kernel, bounds),
        [jax.ShapeDtypeStruct((8, 128), f32)] + [jax.ShapeDtypeStruct((pd, c, b, b), bf16) for c in counts],
        [HB] * (4 + len(after)),
        blocks + blocks + [
            edge, edge, pltpu.SemaphoreType.DMA((2,)),
            pltpu.SemaphoreType.DMA((n, pd, 2)), pltpu.SemaphoreType.DMA((n, pd, 2)),
        ],
        flops=8 * pd * total * b**3,
        moved=8 * pd * total * b * b,
        out_specs=[VM] + [HB] * (2 * n),
        vmem=vmem,
    )(env_left, env_right, edge_left, edge_right, *after)
    return res[0], [(res[2 * i + 1], res[2 * i + 2]) for i in range(n)]


def gate_kernel(*refs):
    refs[-1][...] = jnp.zeros_like(refs[-1])


def gate(arrays, after):
    *held, token = call(
        gate_kernel,
        [jax.ShapeDtypeStruct(a.shape, a.dtype) for a in arrays] + [jax.ShapeDtypeStruct((8, 128), f32)],
        [HB] * (len(arrays) + len(after)),
        aliases={i: i for i in range(len(arrays))},
        out_specs=[HB] * len(arrays) + [VM],
    )(*arrays, *after)
    return held, token


def own_kernel(left_hbm, right_hbm, after, out_l, out_r, sem):
    section = lax.axis_index("section")
    at_start = section == 0
    at_end = section == lax.axis_size("section") - 1
    pd, channels = out_l.shape[0], out_l.shape[1]

    @pl.when(at_start)
    def _():
        c = pltpu.make_async_copy(left_hbm.at[0], out_l, sem)
        c.start()
        c.wait()

    @pl.when(jnp.logical_not(at_start))
    def _():
        out_l[...] = jnp.zeros_like(out_l)

    @pl.when(at_end)
    def _():
        c = pltpu.make_async_copy(right_hbm.at[0], out_r, sem)
        c.start()
        c.wait()
        for k in range(pd):

            def step(w, carry):
                out_r[k, w] = out_r[k, w].T
                return carry

            lax.fori_loop(0, channels, step, 0)

    @pl.when(jnp.logical_not(at_end))
    def _():
        out_r[...] = jnp.zeros_like(out_r)


def own_ends(env_left, env_right, after):
    _, pd, channels, b, _ = env_left.shape
    shape = jax.ShapeDtypeStruct((pd, channels, b, b), bf16)
    return call(
        own_kernel, [shape, shape], [HB, HB, HB], [pltpu.SemaphoreType.DMA],
        flops=10**10, moved=10**6,
    )(env_left, env_right, after)


def live_of(size, shape):
    rows = lax.broadcasted_iota(jnp.int32, shape, 0) < size
    cols = lax.broadcasted_iota(jnp.int32, shape, 1) < size
    return rows & cols


def prepare_kernel(scale, wave, coef, onsite, sizes, after, out, live, weights, energy):
    pd, channels = weights.shape[0], weights.shape[1]
    for k in range(pd):
        v = wave[0, k].astype(f32)
        alive = live_of(sizes[k], v.shape)
        out[k] = jnp.where(alive, v, 0.0).astype(bf16)
        live[k] = jnp.where(alive, 1.0, 0.0)
        energy[k] = jnp.full(energy.shape[1:], onsite[0, k], f32)

        def step(w, carry):
            weights[k, w] = jnp.full(weights.shape[2:], coef[0, k, w] * scale, f32)
            return carry

        lax.fori_loop(0, channels, step, 0)


def prepare(wave, coef, onsite, sizes, after):
    _, pd, b, _ = wave.shape
    channels = coef.shape[2]
    return call(
        functools.partial(prepare_kernel, channels ** (-0.5)),
        [
            jax.ShapeDtypeStruct((pd, b, b), bf16),
            jax.ShapeDtypeStruct((pd, b, b), f32),
            jax.ShapeDtypeStruct((pd, channels, 8, b), f32),
            jax.ShapeDtypeStruct((pd, 8, b), f32),
        ],
        [VM, SM, SM, SM, HB],
        moved=4 * pd * b * b,
    )(wave, coef, onsite, sizes, after)


def times(tile, x):
    return (x.reshape(-1, 8, x.shape[-1]) * tile).reshape(x.shape)


def apply_blocks(load, count, vectors, first, acc, weights, routes, unit, ready=None):
    pd, b = len(vectors), vectors[0].shape[0]

    def step(s, carry):
        at = s * unit
        loaded = [load(k, at, unit) for k in range(pd)]
        halves = [dot(loaded[k][0].reshape(unit * b, b), vectors[k]).astype(bf16) for k in range(pd)]
        if ready is not None:
            ready.wait()
        for k in range(pd):
            for u in range(unit):
                contrib = dot(halves[k][u * b : (u + 1) * b], loaded[k][1][u])
                j = routes[0, k, first + at + u]
                acc[j] += times(weights[k, first + at + u], contrib)
        return carry

    if count == unit:
        step(0, 0)
    else:
        lax.fori_loop(0, count // unit, step, 0)


def three_terms(x):
    hi = x.astype(bf16).astype(f32)
    mid = (x - hi).astype(bf16).astype(f32)
    low = x - hi - mid
    return jnp.concatenate([hi, mid, low, jnp.zeros_like(x)], axis=0).astype(bf16)


def from_terms(rows):
    return fold(rows.astype(f32))


def fold(x):
    return jnp.sum(x.reshape(-1, 8, x.shape[-1]), axis=0)


def total_of(x):
    return jnp.sum(jnp.sum(x, axis=0, keepdims=True), axis=1, keepdims=True)


def split_halves(acc, groups, pd, b, bit, send, keep, extra):
    for i in range(groups // 2):
        for q in range(pd):
            kept = acc[(2 * i + bit) * pd + q]
            sent = acc[(2 * i + 1 - bit) * pd + q]
            keep[i * pd + q] = kept
            send[pl.ds((i * pd + q) * b, b)] = sent.astype(bf16)
    send[pl.ds(groups // 2 * pd * b, EXTRA)] = three_terms(extra)


def first_kernel(
    chunk, is_first, is_last, groups,
    own_l, own_r, got_x, got_y, m, weights, routes_in, *rest
):
    start, count = chunk
    up = up_first()
    rest = list(rest)
    acc_in = None if is_first else rest.pop(0)
    if is_last:
        energy = rest.pop(0)
        pieces = []
        at = 1
        while at < groups:
            pieces.append(rest.pop(0))
            at += pieces[-1].shape[0]
        new_l, new_r, send, keep, squares_out, corr_out, routes, routes_sem, acc = rest
    else:
        new_l, new_r, acc, routes, routes_sem = rest
    routes_copy = pltpu.make_async_copy(routes_in, routes, routes_sem)
    routes_copy.start()
    pd, b = m.shape[0], m.shape[1]
    if is_first:
        acc[...] = jnp.zeros_like(acc)
    else:
        acc[...] = acc_in[...]

    def load(k, at, unit):
        here, there = pl.ds(at, unit), pl.ds(start + at, unit)
        got_first, got_second = got_x[k, here], got_y[k, here]
        left = jnp.where(up, got_first, got_second) + own_l[k, there]
        right = jnp.where(up, got_second, got_first) + own_r[k, there]
        new_l[k, here] = left
        new_r[k, here] = right
        return left, right

    unit = unit_of(count)
    ready = routes_copy if unit == count else None
    if ready is None:
        routes_copy.wait()
    apply_blocks(load, count, [m[k] for k in range(pd)], start, acc, weights, routes, unit, ready)
    if not is_last:
        return
    me = lax.axis_index("sector")
    corr = jnp.zeros((b, b), f32)
    squares = jnp.zeros((b, b), f32)
    for k in range(pd):
        g = m[k].astype(f32)
        corr += g * (acc[me * pd + k] + times(energy[k], g))
        squares += g * g
    distance = 1
    for piece in pieces:
        for i in range(piece.shape[0]):
            owner = lax.bitwise_xor(me, distance)
            for k in range(pd):
                g = piece[i, k].astype(f32)
                corr += g * acc[owner * pd + k]
                squares += g * g
            distance += 1
    corr = fold(corr)
    squares_out[...] = fold(squares)
    corr_out[...] = corr
    split_halves(acc, groups, pd, b, lax.rem(me, 2), send, keep, corr)


def first_apply(chunk, is_first, is_last, groups, arrays, acc_in, extra):
    start, count = chunk
    m = arrays[4]
    pd, b, _ = m.shape
    total = jax.ShapeDtypeStruct((groups * pd, b, b), f32)
    block = jax.ShapeDtypeStruct((pd, count, b, b), bf16)
    args = list(arrays)
    specs = [VM, VM, VM, VM, VM, VM, HB]
    if not is_first:
        args.append(acc_in)
        specs.append(VM)
    scratch = [pltpu.SMEM(arrays[6].shape, jnp.int32), pltpu.SemaphoreType.DMA]
    if is_last:
        args += list(extra)
        specs += [VM] * len(extra)
        outs = [block, block] + exchange_shapes(groups, pd, b) + [jax.ShapeDtypeStruct((8, 128), f32)] * 2
        scratch.append(pltpu.VMEM((groups * pd, b, b), f32))
    else:
        outs = [block, block, total]
    return call(
        functools.partial(first_kernel, chunk, is_first, is_last, groups),
        outs,
        specs,
        scratch,
        flops=4 * pd * count * b**3,
        moved=4 * pd * count * b * b,
    )(*args)


def exchange_shapes(groups, pd, b):
    half = groups // 2 * pd
    return [
        jax.ShapeDtypeStruct((half * b + EXTRA, b), bf16),
        jax.ShapeDtypeStruct((half, b, b), f32),
    ]


def combine_kernel(groups, stage, pd, keep_in, got, extra_in, send, keep, extra_out, acc):
    b = keep_in.shape[1]
    me = lax.axis_index("sector")
    for i in range(groups * pd):
        acc[i] = keep_in[i] + got[pl.ds(i * b, b)].astype(f32)
    extra = extra_in[...] + from_terms(got[pl.ds(groups * pd * b, EXTRA)])
    extra_out[...] = extra
    bit = lax.rem(lax.div(me, 2**stage), 2)
    split_halves(acc, groups, pd, b, bit, send, keep, extra)


def combine(groups, stage, pd, keep, got, extra):
    b = keep.shape[1]
    return call(
        functools.partial(combine_kernel, groups, stage, pd),
        exchange_shapes(groups, pd, b) + [jax.ShapeDtypeStruct((8, 128), f32)],
        [VM, VM, VM],
        [pltpu.VMEM((groups * pd, b, b), f32)],
        flops=groups * pd * b * b,
        moved=8 * groups * pd * b * b,
    )(keep, got, extra)


def exchange(sectors, pd, send, keep, extra):
    stage = 0
    groups = sectors
    while True:
        got = lax.ppermute(send, "sector", [(i, i ^ (1 << stage)) for i in range(sectors)])
        groups //= 2
        stage += 1
        if groups == 1:
            return keep, got, extra
        send, keep, extra = combine(groups, stage, pd, keep, got, extra)


def second_kernel(bounds, groups, *rest):
    n = len(bounds)
    lefts, rights = rest[:n], rest[n : 2 * n]
    (m, weights, routes_in, energy, live, keep_in, got, corr_in, squares_in,
     image_hbm, resid_out, send, keep, sq_out, acc, image_out, image_sem, routes, routes_sem) = rest[2 * n :]
    pd, b = m.shape[0], m.shape[1]
    routes_copy = pltpu.make_async_copy(routes_in, routes, routes_sem)
    routes_copy.start()
    acc[...] = jnp.zeros_like(acc)
    squares = total_of(squares_in[...])
    corr = total_of(corr_in[...] + from_terms(got[pl.ds(pd * b, EXTRA)]))
    ritz = corr / (squares + epsilon)
    sums = jnp.zeros((b, b), f32)
    for k in range(pd):
        g = m[k].astype(f32)
        summed = keep_in[k] + got[pl.ds(k * b, b)].astype(f32) + times(energy[k], g)
        image = jnp.where(live[k] > 0.0, summed, 0.0)
        image_out[k] = image.astype(bf16)
        resid = image - ritz * g
        resid_out[k] = resid.astype(bf16)
        sums += resid * resid
    image_copy = pltpu.make_async_copy(image_out, image_hbm.at[0], image_sem)
    image_copy.start()
    total = fold(sums)
    sq_out[...] = total
    vectors = [resid_out[k] for k in range(pd)]
    routes_copy.wait()
    for i, (start, count) in enumerate(bounds):

        def load(k, at, unit):
            return lefts[i][k, pl.ds(at, unit)], rights[i][k, pl.ds(at, unit)]

        apply_blocks(load, count, vectors, start, acc, weights, routes, unit_of(count, 18))
    me = lax.axis_index("sector")
    split_halves(acc, groups, pd, b, lax.rem(me, 2), send, keep, total)
    image_copy.wait()


def second_apply(bounds, groups, channels, lefts, rights, m, weights, routes, energy, live, keep, got, corr, squares):
    pd, b, _ = m.shape
    n = len(bounds)
    block = jax.ShapeDtypeStruct((1, pd, b, b), bf16)
    return call(
        functools.partial(second_kernel, bounds, groups),
        [block, jax.ShapeDtypeStruct((pd, b, b), bf16)]
        + exchange_shapes(groups, pd, b)
        + [jax.ShapeDtypeStruct((8, 128), f32)],
        [VM] * (2 * n) + [VM, VM, HB, VM, VM, VM, VM, VM, VM],
        [
            pltpu.VMEM((groups * pd, b, b), f32), pltpu.VMEM((pd, b, b), bf16), pltpu.SemaphoreType.DMA,
            pltpu.SMEM(routes.shape, jnp.int32), pltpu.SemaphoreType.DMA,
        ],
        flops=4 * pd * channels * b**3,
        moved=4 * pd * channels * b * b,
        out_specs=[HB, VM, VM, VM, VM],
    )(*lefts, *rights, m, weights, routes, energy, live, keep, got, corr, squares)


def final_kernel(resid, energy, live, keep, got, sq_in, squares_in, out, image, sems):
    pd, b = resid.shape[0], resid.shape[1]
    sq = total_of(sq_in[...] + from_terms(got[pl.ds(pd * b, EXTRA)]))
    alpha = jnp.sqrt(total_of(squares_in[...]) / (sq + epsilon))
    copies = []
    for k in range(pd):
        summed = keep[k] + got[pl.ds(k * b, b)].astype(f32) + times(energy[k], resid[k].astype(f32))
        image[k] = jnp.where(live[k] > 0.0, alpha * summed, 0.0).astype(bf16)
        copies.append(pltpu.make_async_copy(image.at[k], out.at[0, k], sems.at[k]))
        copies[-1].start()
    for c in copies:
        c.wait()


def final(resid, energy, live, keep, got, sq, squares):
    pd, b, _ = resid.shape
    return call(
        final_kernel,
        [jax.ShapeDtypeStruct((1, pd, b, b), bf16)],
        [VM] * 7,
        [pltpu.VMEM((pd, b, b), bf16), pltpu.SemaphoreType.DMA((pd,))],
        moved=8 * pd * b * b,
        out_specs=[HB],
    )(resid, energy, live, keep, got, sq, squares)[0]


def gather_waves(sectors, m):
    held, pieces = m[None], []
    step = 1
    while step < sectors:
        other = lax.ppermute(held, "sector", [(i, i ^ step) for i in range(sectors)])
        pieces.append(other)
        step *= 2
        if step < sectors:
            held = jnp.concatenate([held, other], axis=0)
    return pieces


def body(
    env_left, env_right, edge_left, edge_right, wave_blocks, mpo_coef, onsite, routes, sector_sizes
):
    channels = env_left.shape[2]
    sections = lax.axis_size("section")
    sectors = lax.axis_size("sector")
    pd = wave_blocks.shape[1]
    bounds, at = [], 0
    for c in chunk_sizes(channels):
        bounds.append((at, c))
        at += c
    up = [(i * sectors + j, (i + 1) * sectors + j) for i in range(sections - 1) for j in range(sectors)]
    first = [(a, b) if a % sectors % 2 == 0 else (b, a) for a, b in up]
    second = [(b, a) for a, b in first]

    def pass_on(grown):
        axes = ("section", "sector")
        return lax.ppermute(grown[0], axes, first), lax.ppermute(grown[1], axes, second)

    token, (head,) = grow(env_left, env_right, edge_left, edge_right, bounds[:1], (), VMEM_LARGE)
    got = [pass_on(head)]
    _, (middle, last) = grow(env_left, env_right, edge_left, edge_right, bounds[1:], (token,), VMEM_LARGE)
    got.append(pass_on(middle))
    grown, token = gate(last, got[0])
    m, live, weights, energy = prepare(wave_blocks, mpo_coef, onsite, sector_sizes, token)
    got.append(pass_on(grown))
    pieces = gather_waves(sectors, m)
    own_l, own_r = own_ends(env_left, env_right, m)
    acc, lefts, rights = None, [], []
    for i, chunk in enumerate(bounds):
        is_last = i == len(bounds) - 1
        res = first_apply(
            chunk, i == 0, is_last, sectors,
            (own_l, own_r, got[i][0], got[i][1], m, weights, routes), acc, (energy, *pieces),
        )
        lefts.append(res[0])
        rights.append(res[1])
        acc = res[2]
    send, keep, squares, corr = res[2:]
    keep, summed, corr = exchange(sectors, pd, send, keep, corr)
    image1, resid, send, keep, sq = second_apply(
        bounds, sectors, channels, lefts, rights, m, weights, routes, energy,
        live, keep, summed, corr, squares,
    )
    keep, summed, sq = exchange(sectors, pd, send, keep, sq)
    image2 = final(resid, energy, live, keep, summed, sq, squares)
    return (image1, image2)


def solution(mesh):
    in_specs = (
        P(("groups", "section"), "sector", None, None, None),
        P(("groups", "section"), "sector", None, None, None),
        P(("groups", "section"), "sector", None, None),
        P(("groups", "section"), "sector", None, None),
        P(("groups", "section"), "sector", None, None),
        P(("groups", "section"), "sector", None),
        P(("groups", "section"), "sector"),
        P(("groups", "section"), "sector", None),
        P(("groups", "sector")),
    )
    out_specs = (
        P(("groups", "section"), "sector", None, None),
        P(("groups", "section"), "sector", None, None),
    )
    return jax.shard_map(body, mesh=mesh, in_specs=in_specs, out_specs=out_specs, check_vma=False)
```

```python
import functools

import jax
import jax.numpy as jnp
from jax import lax
from jax.experimental import pallas as pl
from jax.experimental.pallas import tpu as pltpu
from jax.sharding import PartitionSpec as P

epsilon = 1e-06
VMEM_BYTES = 16 * 1024 * 1024
VMEM_LARGE = 56 * 1024 * 1024
EXTRA = 32

f32 = jnp.float32
bf16 = jnp.bfloat16

VM = pl.BlockSpec(memory_space=pltpu.VMEM)
SM = pl.BlockSpec(memory_space=pltpu.SMEM)
HB = pl.BlockSpec(memory_space=pltpu.HBM)


def call(kernel, outs, in_specs, scratch=(), aliases=None, flops=0, moved=0, out_specs=None, vmem=VMEM_BYTES):
    return pl.pallas_call(
        kernel,
        out_shape=outs,
        in_specs=in_specs,
        out_specs=[VM] * len(outs) if out_specs is None else out_specs,
        scratch_shapes=list(scratch),
        input_output_aliases=aliases or {},
        compiler_params=pltpu.CompilerParams(vmem_limit_bytes=vmem),
        cost_estimate=pl.CostEstimate(flops=flops, bytes_accessed=moved, transcendentals=0),
    )


def dot(a, b):
    return jnp.dot(a, b, preferred_element_type=f32)


def dot_t(a, b):
    return lax.dot_general(a, b, (((1,), (1,)), ((), ())), preferred_element_type=f32)


def chunk_sizes(channels):
    first, last = max(1, channels * 3 // 10), max(1, channels // 10)
    return [c for c in (first, channels - first - last, last) if c > 0]


def unit_of(count, most=11):
    return max(u for u in range(1, most + 1) if count % u == 0)


def up_first():
    return lax.rem(lax.axis_index("sector"), 2) == 0


def grow_kernel(bounds, left_hbm, right_hbm, edge_l_hbm, edge_r_hbm, *rest):
    n = len(bounds)
    rest = rest[-6 * n - 6 :]
    token, rest = rest[0], rest[1:]
    outs, bufs, results = rest[: 2 * n], rest[2 * n : 4 * n], rest[4 * n : 6 * n]
    edge_l, edge_r, edge_sems, in_sems, out_sems = rest[6 * n :]
    pd, b = edge_l.shape[0], edge_l.shape[1]
    edges = [
        pltpu.make_async_copy(edge_l_hbm.at[0], edge_l, edge_sems.at[0]),
        pltpu.make_async_copy(edge_r_hbm.at[0], edge_r, edge_sems.at[1]),
    ]
    for c in edges:
        c.start()
    loads = {}
    for i, (start, count) in enumerate(bounds):
        for k in range(pd):
            for side, src in enumerate((left_hbm, right_hbm)):
                c = pltpu.make_async_copy(
                    src.at[0, k, pl.ds(start, count)], bufs[2 * i + side].at[k], in_sems.at[i, k, side]
                )
                c.start()
                loads[i, k, side] = c
    for c in edges:
        c.wait()
    sends = []
    for i, (start, count) in enumerate(bounds):
        unit = unit_of(count)
        buf_l, buf_r = bufs[2 * i], bufs[2 * i + 1]
        res_l, res_r = results[2 * i], results[2 * i + 1]
        for k in range(pd):
            e = edge_l[k]
            e_t = e.T
            f = edge_r[k]
            loads[i, k, 0].wait()
            loads[i, k, 1].wait()

            def step(s, carry):
                at = s * unit
                left = [dot(e_t, buf_l[k, at + u]).astype(bf16) for u in range(unit)]
                right = [dot(f, buf_r[k, at + u]).astype(bf16) for u in range(unit)]
                grown = dot(jnp.concatenate(left, axis=0), e).astype(bf16)
                res_l[k, pl.ds(at, unit)] = grown.reshape(unit, b, b)
                for u in range(unit):
                    res_r[k, at + u] = dot_t(f, right[u]).astype(bf16)
                return carry

            if count == unit:
                step(0, 0)
            else:
                lax.fori_loop(0, count // unit, step, 0)
            out_x, out_y = outs[2 * i].at[k], outs[2 * i + 1].at[k]
            sem_x, sem_y = out_sems.at[i, k, 0], out_sems.at[i, k, 1]

            @pl.when(up_first())
            def _():
                pltpu.make_async_copy(res_l.at[k], out_x, sem_x).start()
                pltpu.make_async_copy(res_r.at[k], out_y, sem_y).start()

            @pl.when(jnp.logical_not(up_first()))
            def _():
                pltpu.make_async_copy(res_r.at[k], out_x, sem_x).start()
                pltpu.make_async_copy(res_l.at[k], out_y, sem_y).start()

            sends.append(pltpu.make_async_copy(res_l.at[k], out_x, sem_x))
            sends.append(pltpu.make_async_copy(res_r.at[k], out_y, sem_y))
    token[...] = jnp.zeros_like(token)
    for c in sends:
        c.wait()


def grow(env_left, env_right, edge_left, edge_right, bounds, after, vmem):
    _, pd, _, b, _ = env_left.shape
    n = len(bounds)
    counts = [c for _, c in bounds for _ in range(2)]
    total = sum(c for _, c in bounds)
    blocks = [pltpu.VMEM((pd, c, b, b), bf16) for c in counts]
    edge = pltpu.VMEM((pd, b, b), bf16)
    res = call(
        functools.partial(grow_kernel, bounds),
        [jax.ShapeDtypeStruct((8, 128), f32)] + [jax.ShapeDtypeStruct((pd, c, b, b), bf16) for c in counts],
        [HB] * (4 + len(after)),
        blocks + blocks + [
            edge, edge, pltpu.SemaphoreType.DMA((2,)),
            pltpu.SemaphoreType.DMA((n, pd, 2)), pltpu.SemaphoreType.DMA((n, pd, 2)),
        ],
        flops=8 * pd * total * b**3,
        moved=8 * pd * total * b * b,
        out_specs=[VM] + [HB] * (2 * n),
        vmem=vmem,
    )(env_left, env_right, edge_left, edge_right, *after)
    return res[0], [(res[2 * i + 1], res[2 * i + 2]) for i in range(n)]


def raw(env_left, env_right, edge_left, edge_right, count):
    left = jnp.concatenate([env_left[0, :, :count], edge_left[0][:, None]], axis=1)
    right = jnp.concatenate([env_right[0, :, :count], edge_right[0][:, None]], axis=1)
    up = up_first()
    return jnp.where(up, left, right), jnp.where(up, right, left)


def gate_kernel(*refs):
    refs[-1][...] = jnp.zeros_like(refs[-1])


def gate(arrays, after):
    *held, token = call(
        gate_kernel,
        [jax.ShapeDtypeStruct(a.shape, a.dtype) for a in arrays] + [jax.ShapeDtypeStruct((8, 128), f32)],
        [HB] * (len(arrays) + len(after)),
        aliases={i: i for i in range(len(arrays))},
        out_specs=[HB] * len(arrays) + [VM],
    )(*arrays, *after)
    return held, token


def own_kernel(left_hbm, right_hbm, after, out_l, out_r, sem):
    section = lax.axis_index("section")
    at_start = section == 0
    at_end = section == lax.axis_size("section") - 1
    pd, channels = out_l.shape[0], out_l.shape[1]

    @pl.when(at_start)
    def _():
        c = pltpu.make_async_copy(left_hbm.at[0], out_l, sem)
        c.start()
        c.wait()

    @pl.when(jnp.logical_not(at_start))
    def _():
        out_l[...] = jnp.zeros_like(out_l)

    @pl.when(at_end)
    def _():
        c = pltpu.make_async_copy(right_hbm.at[0], out_r, sem)
        c.start()
        c.wait()
        for k in range(pd):

            def step(w, carry):
                out_r[k, w] = out_r[k, w].T
                return carry

            lax.fori_loop(0, channels, step, 0)

    @pl.when(jnp.logical_not(at_end))
    def _():
        out_r[...] = jnp.zeros_like(out_r)


def own_ends(env_left, env_right, after):
    _, pd, channels, b, _ = env_left.shape
    shape = jax.ShapeDtypeStruct((pd, channels, b, b), bf16)
    return call(
        own_kernel, [shape, shape], [HB, HB, HB], [pltpu.SemaphoreType.DMA],
        flops=10**10, moved=10**6,
    )(env_left, env_right, after)


def live_of(size, shape):
    rows = lax.broadcasted_iota(jnp.int32, shape, 0) < size
    cols = lax.broadcasted_iota(jnp.int32, shape, 1) < size
    return rows & cols


def prepare_kernel(scale, wave, coef, onsite, sizes, after, out, live, weights, energy):
    pd, channels = weights.shape[0], weights.shape[1]
    for k in range(pd):
        v = wave[0, k].astype(f32)
        alive = live_of(sizes[k], v.shape)
        out[k] = jnp.where(alive, v, 0.0).astype(bf16)
        live[k] = jnp.where(alive, 1.0, 0.0)
        energy[k] = jnp.full(energy.shape[1:], onsite[0, k], f32)

        def step(w, carry):
            weights[k, w] = jnp.full(weights.shape[2:], coef[0, k, w] * scale, f32)
            return carry

        lax.fori_loop(0, channels, step, 0)


def prepare(wave, coef, onsite, sizes, after):
    _, pd, b, _ = wave.shape
    channels = coef.shape[2]
    return call(
        functools.partial(prepare_kernel, channels ** (-0.5)),
        [
            jax.ShapeDtypeStruct((pd, b, b), bf16),
            jax.ShapeDtypeStruct((pd, b, b), f32),
            jax.ShapeDtypeStruct((pd, channels, 8, b), f32),
            jax.ShapeDtypeStruct((pd, 8, b), f32),
        ],
        [VM, SM, SM, SM, HB],
        moved=4 * pd * b * b,
    )(wave, coef, onsite, sizes, after)


def times(tile, x):
    return (x.reshape(-1, 8, x.shape[-1]) * tile).reshape(x.shape)


def apply_blocks(load, count, vectors, first, acc, weights, routes, unit, ready=None):
    pd, b = len(vectors), vectors[0].shape[0]

    def step(s, carry):
        at = s * unit
        loaded = [load(k, at, unit) for k in range(pd)]
        halves = [dot(loaded[k][0].reshape(unit * b, b), vectors[k]).astype(bf16) for k in range(pd)]
        if ready is not None:
            ready.wait()
        for k in range(pd):
            for u in range(unit):
                contrib = dot(halves[k][u * b : (u + 1) * b], loaded[k][1][u])
                j = routes[0, k, first + at + u]
                acc[j] += times(weights[k, first + at + u], contrib)
        return carry

    if count == unit:
        step(0, 0)
    else:
        lax.fori_loop(0, count // unit, step, 0)


def three_terms(x):
    hi = x.astype(bf16).astype(f32)
    mid = (x - hi).astype(bf16).astype(f32)
    low = x - hi - mid
    return jnp.concatenate([hi, mid, low, jnp.zeros_like(x)], axis=0).astype(bf16)


def from_terms(rows):
    return fold(rows.astype(f32))


def fold(x):
    return jnp.sum(x.reshape(-1, 8, x.shape[-1]), axis=0)


def total_of(x):
    return jnp.sum(jnp.sum(x, axis=0, keepdims=True), axis=1, keepdims=True)


def split_halves(acc, groups, pd, b, bit, send, keep, extra):
    for i in range(groups // 2):
        for q in range(pd):
            kept = acc[(2 * i + bit) * pd + q]
            sent = acc[(2 * i + 1 - bit) * pd + q]
            keep[i * pd + q] = kept
            send[pl.ds((i * pd + q) * b, b)] = sent.astype(bf16)
    send[pl.ds(groups // 2 * pd * b, EXTRA)] = three_terms(extra)


def first_kernel(
    chunk, is_first, is_last, groups,
    own_l, own_r, got_x, got_y, m, weights, routes_in, *rest
):
    start, count = chunk
    up = up_first()
    rest = list(rest)
    acc_in = None if is_first else rest.pop(0)
    if is_last:
        energy = rest.pop(0)
        pieces = []
        at = 1
        while at < groups:
            pieces.append(rest.pop(0))
            at += pieces[-1].shape[0]
        new_l, new_r, send, keep, squares_out, corr_out, routes, routes_sem, acc = rest
    else:
        new_l, new_r, acc, routes, routes_sem = rest
    routes_copy = pltpu.make_async_copy(routes_in, routes, routes_sem)
    routes_copy.start()
    pd, b = m.shape[0], m.shape[1]
    if is_first:
        acc[...] = jnp.zeros_like(acc)
    else:
        acc[...] = acc_in[...]

    def load(k, at, unit):
        here, there = pl.ds(at, unit), pl.ds(start + at, unit)
        got_first, got_second = got_x[k, here], got_y[k, here]
        left, right = jnp.where(up, got_first, got_second), jnp.where(up, got_second, got_first)
        if is_first:
            edge_first, edge_second = got_x[k, count], got_y[k, count]
            e, f = jnp.where(up, edge_first, edge_second), jnp.where(up, edge_second, edge_first)
            e_t = e.T
            inner = jnp.concatenate([dot(e_t, left[u]).astype(bf16) for u in range(unit)], axis=0)
            left = dot(inner, e).astype(bf16).reshape(left.shape)
            inner = [dot(f, right[u]).astype(bf16) for u in range(unit)]
            right = jnp.stack([dot_t(f, x).astype(bf16) for x in inner])
        left, right = left + own_l[k, there], right + own_r[k, there]
        new_l[k, here] = left
        new_r[k, here] = right
        return left, right

    unit = unit_of(count)
    ready = routes_copy if unit == count else None
    if ready is None:
        routes_copy.wait()
    apply_blocks(load, count, [m[k] for k in range(pd)], start, acc, weights, routes, unit, ready)
    if not is_last:
        return
    me = lax.axis_index("sector")
    corr = jnp.zeros((b, b), f32)
    squares = jnp.zeros((b, b), f32)
    for k in range(pd):
        g = m[k].astype(f32)
        corr += g * (acc[me * pd + k] + times(energy[k], g))
        squares += g * g
    distance = 1
    for piece in pieces:
        for i in range(piece.shape[0]):
            owner = lax.bitwise_xor(me, distance)
            for k in range(pd):
                g = piece[i, k].astype(f32)
                corr += g * acc[owner * pd + k]
                squares += g * g
            distance += 1
    corr = fold(corr)
    squares_out[...] = fold(squares)
    corr_out[...] = corr
    split_halves(acc, groups, pd, b, lax.rem(me, 2), send, keep, corr)


def first_apply(chunk, is_first, is_last, groups, arrays, acc_in, extra):
    start, count = chunk
    m = arrays[4]
    pd, b, _ = m.shape
    total = jax.ShapeDtypeStruct((groups * pd, b, b), f32)
    block = jax.ShapeDtypeStruct((pd, count, b, b), bf16)
    args = list(arrays)
    specs = [VM, VM, VM, VM, VM, VM, HB]
    if not is_first:
        args.append(acc_in)
        specs.append(VM)
    scratch = [pltpu.SMEM(arrays[6].shape, jnp.int32), pltpu.SemaphoreType.DMA]
    if is_last:
        args += list(extra)
        specs += [VM] * len(extra)
        outs = [block, block] + exchange_shapes(groups, pd, b) + [jax.ShapeDtypeStruct((8, 128), f32)] * 2
        scratch.append(pltpu.VMEM((groups * pd, b, b), f32))
    else:
        outs = [block, block, total]
    return call(
        functools.partial(first_kernel, chunk, is_first, is_last, groups),
        outs,
        specs,
        scratch,
        flops=4 * pd * count * b**3,
        moved=4 * pd * count * b * b,
    )(*args)


def exchange_shapes(groups, pd, b):
    half = groups // 2 * pd
    return [
        jax.ShapeDtypeStruct((half * b + EXTRA, b), bf16),
        jax.ShapeDtypeStruct((half, b, b), f32),
    ]


def combine_kernel(groups, stage, pd, keep_in, got, extra_in, send, keep, extra_out, acc):
    b = keep_in.shape[1]
    me = lax.axis_index("sector")
    for i in range(groups * pd):
        acc[i] = keep_in[i] + got[pl.ds(i * b, b)].astype(f32)
    extra = extra_in[...] + from_terms(got[pl.ds(groups * pd * b, EXTRA)])
    extra_out[...] = extra
    bit = lax.rem(lax.div(me, 2**stage), 2)
    split_halves(acc, groups, pd, b, bit, send, keep, extra)


def combine(groups, stage, pd, keep, got, extra):
    b = keep.shape[1]
    return call(
        functools.partial(combine_kernel, groups, stage, pd),
        exchange_shapes(groups, pd, b) + [jax.ShapeDtypeStruct((8, 128), f32)],
        [VM, VM, VM],
        [pltpu.VMEM((groups * pd, b, b), f32)],
        flops=groups * pd * b * b,
        moved=8 * groups * pd * b * b,
    )(keep, got, extra)


def exchange(sectors, pd, send, keep, extra):
    stage = 0
    groups = sectors
    while True:
        got = lax.ppermute(send, "sector", [(i, i ^ (1 << stage)) for i in range(sectors)])
        groups //= 2
        stage += 1
        if groups == 1:
            return keep, got, extra
        send, keep, extra = combine(groups, stage, pd, keep, got, extra)


def second_kernel(bounds, groups, *rest):
    n = len(bounds)
    lefts, rights = rest[:n], rest[n : 2 * n]
    (m, weights, routes_in, energy, live, keep_in, got, corr_in, squares_in,
     image_hbm, resid_out, send, keep, sq_out, acc, image_out, image_sem, routes, routes_sem) = rest[2 * n :]
    pd, b = m.shape[0], m.shape[1]
    routes_copy = pltpu.make_async_copy(routes_in, routes, routes_sem)
    routes_copy.start()
    acc[...] = jnp.zeros_like(acc)
    squares = total_of(squares_in[...])
    corr = total_of(corr_in[...] + from_terms(got[pl.ds(pd * b, EXTRA)]))
    ritz = corr / (squares + epsilon)
    sums = jnp.zeros((b, b), f32)
    for k in range(pd):
        g = m[k].astype(f32)
        summed = keep_in[k] + got[pl.ds(k * b, b)].astype(f32) + times(energy[k], g)
        image = jnp.where(live[k] > 0.0, summed, 0.0)
        image_out[k] = image.astype(bf16)
        resid = image - ritz * g
        resid_out[k] = resid.astype(bf16)
        sums += resid * resid
    image_copy = pltpu.make_async_copy(image_out, image_hbm.at[0], image_sem)
    image_copy.start()
    total = fold(sums)
    sq_out[...] = total
    vectors = [resid_out[k] for k in range(pd)]
    routes_copy.wait()
    for i, (start, count) in enumerate(bounds):

        def load(k, at, unit):
            return lefts[i][k, pl.ds(at, unit)], rights[i][k, pl.ds(at, unit)]

        apply_blocks(load, count, vectors, start, acc, weights, routes, unit_of(count, 18))
    me = lax.axis_index("sector")
    split_halves(acc, groups, pd, b, lax.rem(me, 2), send, keep, total)
    image_copy.wait()


def second_apply(bounds, groups, channels, lefts, rights, m, weights, routes, energy, live, keep, got, corr, squares):
    pd, b, _ = m.shape
    n = len(bounds)
    block = jax.ShapeDtypeStruct((1, pd, b, b), bf16)
    return call(
        functools.partial(second_kernel, bounds, groups),
        [block, jax.ShapeDtypeStruct((pd, b, b), bf16)]
        + exchange_shapes(groups, pd, b)
        + [jax.ShapeDtypeStruct((8, 128), f32)],
        [VM] * (2 * n) + [VM, VM, HB, VM, VM, VM, VM, VM, VM],
        [
            pltpu.VMEM((groups * pd, b, b), f32), pltpu.VMEM((pd, b, b), bf16), pltpu.SemaphoreType.DMA,
            pltpu.SMEM(routes.shape, jnp.int32), pltpu.SemaphoreType.DMA,
        ],
        flops=4 * pd * channels * b**3,
        moved=4 * pd * channels * b * b,
        out_specs=[HB, VM, VM, VM, VM],
    )(*lefts, *rights, m, weights, routes, energy, live, keep, got, corr, squares)


def final_kernel(resid, energy, live, keep, got, sq_in, squares_in, out, image, sems):
    pd, b = resid.shape[0], resid.shape[1]
    sq = total_of(sq_in[...] + from_terms(got[pl.ds(pd * b, EXTRA)]))
    alpha = jnp.sqrt(total_of(squares_in[...]) / (sq + epsilon))
    copies = []
    for k in range(pd):
        summed = keep[k] + got[pl.ds(k * b, b)].astype(f32) + times(energy[k], resid[k].astype(f32))
        image[k] = jnp.where(live[k] > 0.0, alpha * summed, 0.0).astype(bf16)
        copies.append(pltpu.make_async_copy(image.at[k], out.at[0, k], sems.at[k]))
        copies[-1].start()
    for c in copies:
        c.wait()


def final(resid, energy, live, keep, got, sq, squares):
    pd, b, _ = resid.shape
    return call(
        final_kernel,
        [jax.ShapeDtypeStruct((1, pd, b, b), bf16)],
        [VM] * 7,
        [pltpu.VMEM((pd, b, b), bf16), pltpu.SemaphoreType.DMA((pd,))],
        moved=8 * pd * b * b,
        out_specs=[HB],
    )(resid, energy, live, keep, got, sq, squares)[0]


def gather_waves(sectors, m):
    held, pieces = m[None], []
    step = 1
    while step < sectors:
        other = lax.ppermute(held, "sector", [(i, i ^ step) for i in range(sectors)])
        pieces.append(other)
        step *= 2
        if step < sectors:
            held = jnp.concatenate([held, other], axis=0)
    return pieces


def body(
    env_left, env_right, edge_left, edge_right, wave_blocks, mpo_coef, onsite, routes, sector_sizes
):
    channels = env_left.shape[2]
    sections = lax.axis_size("section")
    sectors = lax.axis_size("sector")
    pd = wave_blocks.shape[1]
    bounds, at = [], 0
    for c in chunk_sizes(channels):
        bounds.append((at, c))
        at += c
    up = [(i * sectors + j, (i + 1) * sectors + j) for i in range(sections - 1) for j in range(sectors)]
    first = [(a, b) if a % sectors % 2 == 0 else (b, a) for a, b in up]
    second = [(b, a) for a, b in first]

    def pass_on(grown):
        axes = ("section", "sector")
        return lax.ppermute(grown[0], axes, first), lax.ppermute(grown[1], axes, second)

    head = raw(env_left, env_right, edge_left, edge_right, bounds[0][1])
    got = [pass_on(head)]
    _, (middle, last) = grow(env_left, env_right, edge_left, edge_right, bounds[1:], head[:1], VMEM_LARGE)
    got.append(pass_on(middle))
    grown, token = gate(last, got[0])
    m, live, weights, energy = prepare(wave_blocks, mpo_coef, onsite, sector_sizes, token)
    got.append(pass_on(grown))
    pieces = gather_waves(sectors, m)
    own_l, own_r = own_ends(env_left, env_right, m)
    acc, lefts, rights = None, [], []
    for i, chunk in enumerate(bounds):
        is_last = i == len(bounds) - 1
        res = first_apply(
            chunk, i == 0, is_last, sectors,
            (own_l, own_r, got[i][0], got[i][1], m, weights, routes), acc, (energy, *pieces),
        )
        lefts.append(res[0])
        rights.append(res[1])
        acc = res[2]
    send, keep, squares, corr = res[2:]
    keep, summed, corr = exchange(sectors, pd, send, keep, corr)
    image1, resid, send, keep, sq = second_apply(
        bounds, sectors, channels, lefts, rights, m, weights, routes, energy,
        live, keep, summed, corr, squares,
    )
    keep, summed, sq = exchange(sectors, pd, send, keep, sq)
    image2 = final(resid, energy, live, keep, summed, sq, squares)
    return (image1, image2)


def solution(mesh):
    in_specs = (
        P(("groups", "section"), "sector", None, None, None),
        P(("groups", "section"), "sector", None, None, None),
        P(("groups", "section"), "sector", None, None),
        P(("groups", "section"), "sector", None, None),
        P(("groups", "section"), "sector", None, None),
        P(("groups", "section"), "sector", None),
        P(("groups", "section"), "sector"),
        P(("groups", "section"), "sector", None),
        P(("groups", "sector")),
    )
    out_specs = (
        P(("groups", "section"), "sector", None, None),
        P(("groups", "section"), "sector", None, None),
    )
    return jax.shard_map(body, mesh=mesh, in_specs=in_specs, out_specs=out_specs, check_vma=False)
```

```python
import functools

import jax
import jax.numpy as jnp
from jax import lax
from jax.experimental import pallas as pl
from jax.experimental.pallas import tpu as pltpu
from jax.sharding import PartitionSpec as P

epsilon = 1e-06
VMEM_BYTES = 16 * 1024 * 1024
VMEM_LARGE = 56 * 1024 * 1024
EXTRA = 32

f32 = jnp.float32
bf16 = jnp.bfloat16

VM = pl.BlockSpec(memory_space=pltpu.VMEM)
SM = pl.BlockSpec(memory_space=pltpu.SMEM)
HB = pl.BlockSpec(memory_space=pltpu.HBM)


def call(kernel, outs, in_specs, scratch=(), aliases=None, flops=0, moved=0, out_specs=None, vmem=VMEM_BYTES):
    return pl.pallas_call(
        kernel,
        out_shape=outs,
        in_specs=in_specs,
        out_specs=[VM] * len(outs) if out_specs is None else out_specs,
        scratch_shapes=list(scratch),
        input_output_aliases=aliases or {},
        compiler_params=pltpu.CompilerParams(vmem_limit_bytes=vmem),
        cost_estimate=pl.CostEstimate(flops=flops, bytes_accessed=moved, transcendentals=0),
    )


def dot(a, b):
    return jnp.dot(a, b, preferred_element_type=f32)


def dot_t(a, b):
    return lax.dot_general(a, b, (((1,), (1,)), ((), ())), preferred_element_type=f32)


def chunk_sizes(channels):
    first, last = max(1, channels * 11 // 30), max(1, channels * 3 // 30)
    return [c for c in (first, channels - first - last, last) if c > 0]


def unit_of(count, most=11):
    return max(u for u in range(1, most + 1) if count % u == 0)


def up_first():
    return lax.rem(lax.axis_index("sector"), 2) == 0


def grow_kernel(bounds, left_hbm, right_hbm, edge_l_hbm, edge_r_hbm, *rest):
    n = len(bounds)
    rest = rest[-6 * n - 6 :]
    token, rest = rest[0], rest[1:]
    outs, bufs, results = rest[: 2 * n], rest[2 * n : 4 * n], rest[4 * n : 6 * n]
    edge_l, edge_r, edge_sems, in_sems, out_sems = rest[6 * n :]
    pd, b = edge_l.shape[0], edge_l.shape[1]
    edges = [
        pltpu.make_async_copy(edge_l_hbm.at[0], edge_l, edge_sems.at[0]),
        pltpu.make_async_copy(edge_r_hbm.at[0], edge_r, edge_sems.at[1]),
    ]
    for c in edges:
        c.start()
    loads = {}
    for i, (start, count) in enumerate(bounds):
        for k in range(pd):
            for side, src in enumerate((left_hbm, right_hbm)):
                c = pltpu.make_async_copy(
                    src.at[0, k, pl.ds(start, count)], bufs[2 * i + side].at[k], in_sems.at[i, k, side]
                )
                c.start()
                loads[i, k, side] = c
    for c in edges:
        c.wait()
    sends = []
    for i, (start, count) in enumerate(bounds):
        unit = unit_of(count)
        buf_l, buf_r = bufs[2 * i], bufs[2 * i + 1]
        res_l, res_r = results[2 * i], results[2 * i + 1]
        for k in range(pd):
            e = edge_l[k]
            e_t = e.T
            f = edge_r[k]
            loads[i, k, 0].wait()
            loads[i, k, 1].wait()

            def step(s, carry):
                at = s * unit
                left = [dot(e_t, buf_l[k, at + u]).astype(bf16) for u in range(unit)]
                right = [dot(f, buf_r[k, at + u]).astype(bf16) for u in range(unit)]
                grown = dot(jnp.concatenate(left, axis=0), e).astype(bf16)
                res_l[k, pl.ds(at, unit)] = grown.reshape(unit, b, b)
                for u in range(unit):
                    res_r[k, at + u] = dot_t(f, right[u]).astype(bf16)
                return carry

            if count == unit:
                step(0, 0)
            else:
                lax.fori_loop(0, count // unit, step, 0)
            out_x, out_y = outs[2 * i].at[k], outs[2 * i + 1].at[k]
            sem_x, sem_y = out_sems.at[i, k, 0], out_sems.at[i, k, 1]

            @pl.when(up_first())
            def _():
                pltpu.make_async_copy(res_l.at[k], out_x, sem_x).start()
                pltpu.make_async_copy(res_r.at[k], out_y, sem_y).start()

            @pl.when(jnp.logical_not(up_first()))
            def _():
                pltpu.make_async_copy(res_r.at[k], out_x, sem_x).start()
                pltpu.make_async_copy(res_l.at[k], out_y, sem_y).start()

            sends.append(pltpu.make_async_copy(res_l.at[k], out_x, sem_x))
            sends.append(pltpu.make_async_copy(res_r.at[k], out_y, sem_y))
    token[...] = jnp.zeros_like(token)
    for c in sends:
        c.wait()


def grow(env_left, env_right, edge_left, edge_right, bounds, after, vmem):
    _, pd, _, b, _ = env_left.shape
    n = len(bounds)
    counts = [c for _, c in bounds for _ in range(2)]
    total = sum(c for _, c in bounds)
    blocks = [pltpu.VMEM((pd, c, b, b), bf16) for c in counts]
    edge = pltpu.VMEM((pd, b, b), bf16)
    res = call(
        functools.partial(grow_kernel, bounds),
        [jax.ShapeDtypeStruct((8, 128), f32)] + [jax.ShapeDtypeStruct((pd, c, b, b), bf16) for c in counts],
        [HB] * (4 + len(after)),
        blocks + blocks + [
            edge, edge, pltpu.SemaphoreType.DMA((2,)),
            pltpu.SemaphoreType.DMA((n, pd, 2)), pltpu.SemaphoreType.DMA((n, pd, 2)),
        ],
        flops=8 * pd * total * b**3,
        moved=8 * pd * total * b * b,
        out_specs=[VM] + [HB] * (2 * n),
        vmem=vmem,
    )(env_left, env_right, edge_left, edge_right, *after)
    return res[0], [(res[2 * i + 1], res[2 * i + 2]) for i in range(n)]


def raw(env_left, env_right, edge_left, edge_right, count):
    left = jnp.concatenate([env_left[0, :, :count], edge_left[0][:, None]], axis=1)
    right = jnp.concatenate([env_right[0, :, :count], edge_right[0][:, None]], axis=1)
    return jnp.where(up_first(), left, right)


def other_kernel(count, left_hbm, right_hbm, edge_l_hbm, edge_r_hbm, after, token, out, buf, edge, res, sems, out_sems):
    pd = buf.shape[0]

    def copies(env, src):
        made = [pltpu.make_async_copy(src.at[0], edge, sems.at[0])]
        for k in range(pd):
            made.append(pltpu.make_async_copy(env.at[0, k, pl.ds(0, count)], buf.at[k], sems.at[k + 1]))
        return made

    @pl.when(up_first())
    def _():
        for c in copies(right_hbm, edge_r_hbm):
            c.start()

    @pl.when(jnp.logical_not(up_first()))
    def _():
        for c in copies(left_hbm, edge_l_hbm):
            c.start()

    token[...] = jnp.zeros_like(token)
    for c in copies(left_hbm, edge_l_hbm):
        c.wait()
    sends = [pltpu.make_async_copy(res.at[k], out.at[k], out_sems.at[k]) for k in range(pd)]

    @pl.when(up_first())
    def _():
        for k in range(pd):
            res[k] = grown_right(edge[k], buf[k])
            sends[k].start()

    @pl.when(jnp.logical_not(up_first()))
    def _():
        for k in range(pd):
            res[k] = grown_left(edge[k], buf[k])
            sends[k].start()

    for c in sends:
        c.wait()


def grown_left(e, x):
    e_t = e.T
    inner = jnp.concatenate([dot(e_t, x[u]).astype(bf16) for u in range(x.shape[0])], axis=0)
    return dot(inner, e).astype(bf16).reshape(x.shape)


def grown_right(f, x):
    inner = [dot(f, x[u]).astype(bf16) for u in range(x.shape[0])]
    return jnp.stack([dot_t(f, i).astype(bf16) for i in inner])


def other(env_left, env_right, edge_left, edge_right, count, after):
    _, pd, _, b, _ = env_left.shape
    buf = pltpu.VMEM((pd, count, b, b), bf16)
    return call(
        functools.partial(other_kernel, count),
        [jax.ShapeDtypeStruct((8, 128), f32), jax.ShapeDtypeStruct((pd, count, b, b), bf16)],
        [HB] * 5,
        [buf, pltpu.VMEM((pd, b, b), bf16), buf, pltpu.SemaphoreType.DMA((pd + 1,)), pltpu.SemaphoreType.DMA((pd,))],
        flops=4 * pd * count * b**3,
        moved=4 * pd * count * b * b,
        out_specs=[VM, HB],
        vmem=VMEM_LARGE,
    )(env_left, env_right, edge_left, edge_right, after)


def gate_kernel(*refs):
    refs[-1][...] = jnp.zeros_like(refs[-1])


def gate(arrays, after):
    *held, token = call(
        gate_kernel,
        [jax.ShapeDtypeStruct(a.shape, a.dtype) for a in arrays] + [jax.ShapeDtypeStruct((8, 128), f32)],
        [HB] * (len(arrays) + len(after)),
        aliases={i: i for i in range(len(arrays))},
        out_specs=[HB] * len(arrays) + [VM],
    )(*arrays, *after)
    return held, token


def own_kernel(left_hbm, right_hbm, after, out_l, out_r, sem):
    section = lax.axis_index("section")
    at_start = section == 0
    at_end = section == lax.axis_size("section") - 1
    pd, channels = out_l.shape[0], out_l.shape[1]

    @pl.when(at_start)
    def _():
        c = pltpu.make_async_copy(left_hbm.at[0], out_l, sem)
        c.start()
        c.wait()

    @pl.when(jnp.logical_not(at_start))
    def _():
        out_l[...] = jnp.zeros_like(out_l)

    @pl.when(at_end)
    def _():
        c = pltpu.make_async_copy(right_hbm.at[0], out_r, sem)
        c.start()
        c.wait()
        for k in range(pd):

            def step(w, carry):
                out_r[k, w] = out_r[k, w].T
                return carry

            lax.fori_loop(0, channels, step, 0)

    @pl.when(jnp.logical_not(at_end))
    def _():
        out_r[...] = jnp.zeros_like(out_r)


def own_ends(env_left, env_right, after):
    _, pd, channels, b, _ = env_left.shape
    shape = jax.ShapeDtypeStruct((pd, channels, b, b), bf16)
    return call(
        own_kernel, [shape, shape], [HB, HB, HB], [pltpu.SemaphoreType.DMA],
        flops=7 * 10**9, moved=10**6,
    )(env_left, env_right, after)


def live_of(size, shape):
    rows = lax.broadcasted_iota(jnp.int32, shape, 0) < size
    cols = lax.broadcasted_iota(jnp.int32, shape, 1) < size
    return rows & cols


def prepare_kernel(scale, wave, coef, onsite, sizes, after, out, live, weights, energy):
    pd, channels = weights.shape[0], weights.shape[1]
    for k in range(pd):
        v = wave[0, k].astype(f32)
        alive = live_of(sizes[k], v.shape)
        out[k] = jnp.where(alive, v, 0.0).astype(bf16)
        live[k] = jnp.where(alive, 1.0, 0.0)
        energy[k] = jnp.full(energy.shape[1:], onsite[0, k], f32)

        def step(w, carry):
            weights[k, w] = jnp.full(weights.shape[2:], coef[0, k, w] * scale, f32)
            return carry

        lax.fori_loop(0, channels, step, 0)


def prepare(wave, coef, onsite, sizes, after):
    _, pd, b, _ = wave.shape
    channels = coef.shape[2]
    return call(
        functools.partial(prepare_kernel, channels ** (-0.5)),
        [
            jax.ShapeDtypeStruct((pd, b, b), bf16),
            jax.ShapeDtypeStruct((pd, b, b), f32),
            jax.ShapeDtypeStruct((pd, channels, 8, b), f32),
            jax.ShapeDtypeStruct((pd, 8, b), f32),
        ],
        [VM, SM, SM, SM, HB],
        moved=4 * pd * b * b,
    )(wave, coef, onsite, sizes, after)


def times(tile, x):
    return (x.reshape(-1, 8, x.shape[-1]) * tile).reshape(x.shape)


def apply_blocks(load, count, vectors, first, acc, weights, routes, unit, ready=None):
    pd, b = len(vectors), vectors[0].shape[0]

    def step(s, carry):
        at = s * unit
        loaded = [load(k, at, unit) for k in range(pd)]
        halves = [dot(loaded[k][0].reshape(unit * b, b), vectors[k]).astype(bf16) for k in range(pd)]
        if ready is not None:
            ready.wait()
        for k in range(pd):
            for u in range(unit):
                contrib = dot(halves[k][u * b : (u + 1) * b], loaded[k][1][u])
                j = routes[0, k, first + at + u]
                acc[j] += times(weights[k, first + at + u], contrib)
        return carry

    if count == unit:
        step(0, 0)
    else:
        lax.fori_loop(0, count // unit, step, 0)


def three_terms(x):
    hi = x.astype(bf16).astype(f32)
    mid = (x - hi).astype(bf16).astype(f32)
    low = x - hi - mid
    return jnp.concatenate([hi, mid, low, jnp.zeros_like(x)], axis=0).astype(bf16)


def from_terms(rows):
    return fold(rows.astype(f32))


def fold(x):
    return jnp.sum(x.reshape(-1, 8, x.shape[-1]), axis=0)


def total_of(x):
    return jnp.sum(jnp.sum(x, axis=0, keepdims=True), axis=1, keepdims=True)


def split_halves(acc, groups, pd, b, bit, send, keep, extra):
    for i in range(groups // 2):
        for q in range(pd):
            kept = acc[(2 * i + bit) * pd + q]
            sent = acc[(2 * i + 1 - bit) * pd + q]
            keep[i * pd + q] = kept
            send[pl.ds((i * pd + q) * b, b)] = sent.astype(bf16)
    send[pl.ds(groups // 2 * pd * b, EXTRA)] = three_terms(extra)


def first_kernel(
    chunk, is_first, is_last, groups,
    own_l, own_r, got_x, got_y, m, weights, routes_in, *rest
):
    start, count = chunk
    up = up_first()
    rest = list(rest)
    acc_in = None if is_first else rest.pop(0)
    if is_last:
        energy = rest.pop(0)
        pieces = []
        at = 1
        while at < groups:
            pieces.append(rest.pop(0))
            at += pieces[-1].shape[0]
        new_l, new_r, send, keep, squares_out, corr_out, routes, routes_sem, acc = rest
    else:
        new_l, new_r, acc, routes, routes_sem = rest
    routes_copy = pltpu.make_async_copy(routes_in, routes, routes_sem)
    routes_copy.start()
    pd, b = m.shape[0], m.shape[1]
    if is_first:
        acc[...] = jnp.zeros_like(acc)
    else:
        acc[...] = acc_in[...]

    def load(k, at, unit):
        here, there = pl.ds(at, unit), pl.ds(start + at, unit)
        got_first, got_second = got_x[k, here], got_y[k, here]
        as_left, as_right = got_first, got_first
        if is_first:
            edge = got_x[k, count]
            as_left, as_right = grown_left(edge, got_first), grown_right(edge, got_first)
        left, right = jnp.where(up, as_left, got_second), jnp.where(up, got_second, as_right)
        left, right = left + own_l[k, there], right + own_r[k, there]
        new_l[k, here] = left
        new_r[k, here] = right
        return left, right

    unit = unit_of(count)
    ready = routes_copy if unit == count else None
    if ready is None:
        routes_copy.wait()
    apply_blocks(load, count, [m[k] for k in range(pd)], start, acc, weights, routes, unit, ready)
    if not is_last:
        return
    me = lax.axis_index("sector")
    corr = jnp.zeros((b, b), f32)
    squares = jnp.zeros((b, b), f32)
    for k in range(pd):
        g = m[k].astype(f32)
        corr += g * (acc[me * pd + k] + times(energy[k], g))
        squares += g * g
    distance = 1
    for piece in pieces:
        for i in range(piece.shape[0]):
            owner = lax.bitwise_xor(me, distance)
            for k in range(pd):
                g = piece[i, k].astype(f32)
                corr += g * acc[owner * pd + k]
                squares += g * g
            distance += 1
    corr = fold(corr)
    squares_out[...] = fold(squares)
    corr_out[...] = corr
    split_halves(acc, groups, pd, b, lax.rem(me, 2), send, keep, corr)


def first_apply(chunk, is_first, is_last, groups, arrays, acc_in, extra):
    start, count = chunk
    m = arrays[4]
    pd, b, _ = m.shape
    total = jax.ShapeDtypeStruct((groups * pd, b, b), f32)
    block = jax.ShapeDtypeStruct((pd, count, b, b), bf16)
    args = list(arrays)
    specs = [VM, VM, VM, VM, VM, VM, HB]
    if not is_first:
        args.append(acc_in)
        specs.append(VM)
    scratch = [pltpu.SMEM(arrays[6].shape, jnp.int32), pltpu.SemaphoreType.DMA]
    if is_last:
        args += list(extra)
        specs += [VM] * len(extra)
        outs = [block, block] + exchange_shapes(groups, pd, b) + [jax.ShapeDtypeStruct((8, 128), f32)] * 2
        scratch.append(pltpu.VMEM((groups * pd, b, b), f32))
    else:
        outs = [block, block, total]
    return call(
        functools.partial(first_kernel, chunk, is_first, is_last, groups),
        outs,
        specs,
        scratch,
        flops=4 * pd * count * b**3,
        moved=4 * pd * count * b * b,
    )(*args)


def exchange_shapes(groups, pd, b):
    half = groups // 2 * pd
    return [
        jax.ShapeDtypeStruct((half * b + EXTRA, b), bf16),
        jax.ShapeDtypeStruct((half, b, b), f32),
    ]


def combine_kernel(groups, stage, pd, keep_in, got, extra_in, send, keep, extra_out, acc):
    b = keep_in.shape[1]
    me = lax.axis_index("sector")
    for i in range(groups * pd):
        acc[i] = keep_in[i] + got[pl.ds(i * b, b)].astype(f32)
    extra = extra_in[...] + from_terms(got[pl.ds(groups * pd * b, EXTRA)])
    extra_out[...] = extra
    bit = lax.rem(lax.div(me, 2**stage), 2)
    split_halves(acc, groups, pd, b, bit, send, keep, extra)


def combine(groups, stage, pd, keep, got, extra):
    b = keep.shape[1]
    return call(
        functools.partial(combine_kernel, groups, stage, pd),
        exchange_shapes(groups, pd, b) + [jax.ShapeDtypeStruct((8, 128), f32)],
        [VM, VM, VM],
        [pltpu.VMEM((groups * pd, b, b), f32)],
        flops=groups * pd * b * b,
        moved=8 * groups * pd * b * b,
    )(keep, got, extra)


def exchange(sectors, pd, send, keep, extra):
    stage = 0
    groups = sectors
    while True:
        got = lax.ppermute(send, "sector", [(i, i ^ (1 << stage)) for i in range(sectors)])
        groups //= 2
        stage += 1
        if groups == 1:
            return keep, got, extra
        send, keep, extra = combine(groups, stage, pd, keep, got, extra)


def second_kernel(bounds, groups, *rest):
    n = len(bounds)
    lefts, rights = rest[:n], rest[n : 2 * n]
    (m, weights, routes_in, energy, live, keep_in, got, corr_in, squares_in,
     image_hbm, resid_out, send, keep, sq_out, acc, image_out, image_sem, routes, routes_sem) = rest[2 * n :]
    pd, b = m.shape[0], m.shape[1]
    routes_copy = pltpu.make_async_copy(routes_in, routes, routes_sem)
    routes_copy.start()
    acc[...] = jnp.zeros_like(acc)
    squares = total_of(squares_in[...])
    corr = total_of(corr_in[...] + from_terms(got[pl.ds(pd * b, EXTRA)]))
    ritz = corr / (squares + epsilon)
    sums = jnp.zeros((b, b), f32)
    for k in range(pd):
        g = m[k].astype(f32)
        summed = keep_in[k] + got[pl.ds(k * b, b)].astype(f32) + times(energy[k], g)
        image = jnp.where(live[k] > 0.0, summed, 0.0)
        image_out[k] = image.astype(bf16)
        resid = image - ritz * g
        resid_out[k] = resid.astype(bf16)
        sums += resid * resid
    image_copy = pltpu.make_async_copy(image_out, image_hbm.at[0], image_sem)
    image_copy.start()
    total = fold(sums)
    sq_out[...] = total
    vectors = [resid_out[k] for k in range(pd)]
    routes_copy.wait()
    for i, (start, count) in enumerate(bounds):

        def load(k, at, unit):
            return lefts[i][k, pl.ds(at, unit)], rights[i][k, pl.ds(at, unit)]

        apply_blocks(load, count, vectors, start, acc, weights, routes, unit_of(count, 18))
    me = lax.axis_index("sector")
    split_halves(acc, groups, pd, b, lax.rem(me, 2), send, keep, total)
    image_copy.wait()


def second_apply(bounds, groups, channels, lefts, rights, m, weights, routes, energy, live, keep, got, corr, squares):
    pd, b, _ = m.shape
    n = len(bounds)
    block = jax.ShapeDtypeStruct((1, pd, b, b), bf16)
    return call(
        functools.partial(second_kernel, bounds, groups),
        [block, jax.ShapeDtypeStruct((pd, b, b), bf16)]
        + exchange_shapes(groups, pd, b)
        + [jax.ShapeDtypeStruct((8, 128), f32)],
        [VM] * (2 * n) + [VM, VM, HB, VM, VM, VM, VM, VM, VM],
        [
            pltpu.VMEM((groups * pd, b, b), f32), pltpu.VMEM((pd, b, b), bf16), pltpu.SemaphoreType.DMA,
            pltpu.SMEM(routes.shape, jnp.int32), pltpu.SemaphoreType.DMA,
        ],
        flops=4 * pd * channels * b**3,
        moved=4 * pd * channels * b * b,
        out_specs=[HB, VM, VM, VM, VM],
    )(*lefts, *rights, m, weights, routes, energy, live, keep, got, corr, squares)


def final_kernel(resid, energy, live, keep, got, sq_in, squares_in, out, image, sems):
    pd, b = resid.shape[0], resid.shape[1]
    sq = total_of(sq_in[...] + from_terms(got[pl.ds(pd * b, EXTRA)]))
    alpha = jnp.sqrt(total_of(squares_in[...]) / (sq + epsilon))
    copies = []
    for k in range(pd):
        summed = keep[k] + got[pl.ds(k * b, b)].astype(f32) + times(energy[k], resid[k].astype(f32))
        image[k] = jnp.where(live[k] > 0.0, alpha * summed, 0.0).astype(bf16)
        copies.append(pltpu.make_async_copy(image.at[k], out.at[0, k], sems.at[k]))
        copies[-1].start()
    for c in copies:
        c.wait()


def final(resid, energy, live, keep, got, sq, squares):
    pd, b, _ = resid.shape
    return call(
        final_kernel,
        [jax.ShapeDtypeStruct((1, pd, b, b), bf16)],
        [VM] * 7,
        [pltpu.VMEM((pd, b, b), bf16), pltpu.SemaphoreType.DMA((pd,))],
        moved=8 * pd * b * b,
        out_specs=[HB],
    )(resid, energy, live, keep, got, sq, squares)[0]


def gather_waves(sectors, m):
    held, pieces = m[None], []
    step = 1
    while step < sectors:
        other = lax.ppermute(held, "sector", [(i, i ^ step) for i in range(sectors)])
        pieces.append(other)
        step *= 2
        if step < sectors:
            held = jnp.concatenate([held, other], axis=0)
    return pieces


def body(
    env_left, env_right, edge_left, edge_right, wave_blocks, mpo_coef, onsite, routes, sector_sizes
):
    channels = env_left.shape[2]
    sections = lax.axis_size("section")
    sectors = lax.axis_size("sector")
    pd = wave_blocks.shape[1]
    bounds, at = [], 0
    for c in chunk_sizes(channels):
        bounds.append((at, c))
        at += c
    up = [(i * sectors + j, (i + 1) * sectors + j) for i in range(sections - 1) for j in range(sectors)]
    first = [(a, b) if a % sectors % 2 == 0 else (b, a) for a, b in up]
    second = [(b, a) for a, b in first]

    def pass_on(grown):
        axes = ("section", "sector")
        return lax.ppermute(grown[0], axes, first), lax.ppermute(grown[1], axes, second)

    whole = raw(env_left, env_right, edge_left, edge_right, bounds[0][1])
    token, half = other(env_left, env_right, edge_left, edge_right, bounds[0][1], whole)
    head = (whole, half)
    got = [pass_on(head)]
    _, (middle, last) = grow(env_left, env_right, edge_left, edge_right, bounds[1:], (token,), VMEM_LARGE)
    got.append(pass_on(middle))
    grown, token = gate(last, got[0])
    m, live, weights, energy = prepare(wave_blocks, mpo_coef, onsite, sector_sizes, token)
    got.append(pass_on(grown))
    pieces = gather_waves(sectors, m)
    own_l, own_r = own_ends(env_left, env_right, m)
    acc, lefts, rights = None, [], []
    for i, chunk in enumerate(bounds):
        is_last = i == len(bounds) - 1
        res = first_apply(
            chunk, i == 0, is_last, sectors,
            (own_l, own_r, got[i][0], got[i][1], m, weights, routes), acc, (energy, *pieces),
        )
        lefts.append(res[0])
        rights.append(res[1])
        acc = res[2]
    send, keep, squares, corr = res[2:]
    keep, summed, corr = exchange(sectors, pd, send, keep, corr)
    image1, resid, send, keep, sq = second_apply(
        bounds, sectors, channels, lefts, rights, m, weights, routes, energy,
        live, keep, summed, corr, squares,
    )
    keep, summed, sq = exchange(sectors, pd, send, keep, sq)
    image2 = final(resid, energy, live, keep, summed, sq, squares)
    return (image1, image2)


def solution(mesh):
    in_specs = (
        P(("groups", "section"), "sector", None, None, None),
        P(("groups", "section"), "sector", None, None, None),
        P(("groups", "section"), "sector", None, None),
        P(("groups", "section"), "sector", None, None),
        P(("groups", "section"), "sector", None, None),
        P(("groups", "section"), "sector", None),
        P(("groups", "section"), "sector"),
        P(("groups", "section"), "sector", None),
        P(("groups", "sector")),
    )
    out_specs = (
        P(("groups", "section"), "sector", None, None),
        P(("groups", "section"), "sector", None, None),
    )
    return jax.shard_map(body, mesh=mesh, in_specs=in_specs, out_specs=out_specs, check_vma=False)
```
